32 devices in a mesh: gx: 2 (over x), gy: 4 (over z), gz: 4 (over y, core).
Axes of the slice: x: 2, y: 2, z: 4, core: 2. Of those that a mesh axis runs over, the one named last changes fastest.
Arguments:
- velocity: float32 [3, 64, 256, 512], P(None, 'gx', 'gy', 'gz'), may hold values from -12 to 12
- inv_density: float32 [64, 256, 512], P('gx', 'gy', 'gz'), may hold values from 0.2 to 5
- factor_x: float32 [64, 64], P('gx'), may hold values from -1 to 1
- factor_y: float32 [256, 64], P('gy'), may hold values from -0.5 to 0.5
- factor_z: float32 [512, 64], P('gz'), may hold values from -0.375 to 0.375
Outputs:
- pressure: float32 [64, 256, 512], P('gx', 'gy', 'gz')
- corrected: float32 [3, 64, 256, 512], P(None, 'gx', 'gy', 'gz')
- core: float32 [64, 4, 64, 64], P('gx', None, 'gy', 'gz')
The draws below stay inside these ranges and needn't reach their ends.
All inputs are finite; a program needn't handle non-finite values.
Results may differ from the reference program's by a relative error of at most 0.00013.
Values sent between devices are 32-bit elements; how exact they have to be, the bound alone decides.
No kernel may reach another device: no remote copies, remote signals or barrier semaphores. Data moves between devices by JAX's collectives and lax.ppermute only.
A program may use at most 128 MiB of HBM per device.

```python
import math
import jax
import jax.numpy as jnp
from jax import lax

RANK = 64
ITERS = 4
NX = 64
NY = 256
NZ = 512


def draw_velocity(key, part):
    position = jnp.arange(NX, dtype=jnp.float32) / NX
    ramp = (1.0 + 2.0 * position)[None, :, None, None]
    rough = jnp.clip(jax.random.normal(key, (3, NX, NY, NZ), jnp.float32), -4.0, 4.0)
    return ramp * rough


def strengthened(values, stream_key, source, target, shards_of, factor):
    def block_of(dim):
        return (jnp.arange(values.shape[dim]) // (values.shape[dim] // shards_of)).reshape((-1,) + (1,) * (values.ndim - 1 - dim))

    near = jax.random.permutation(stream_key, shards_of)[block_of(target)]
    second = (block_of(target) + shards_of // 2) % shards_of
    return jnp.where((block_of(source) == near) | (block_of(source) == second), factor * values, values)


def block_levels(stream_key, dims, cuts, low, largest):
    gain, own = 1.0, jax.random.fold_in(stream_key, 6)
    for dim, blocks in cuts:
        heights = jnp.exp(jax.random.uniform(jax.random.fold_in(own, dim), (blocks,), jnp.float32, low / len(cuts), largest / len(cuts)))
        gain = gain * jnp.repeat(heights, dims[dim] // blocks).reshape([-1 if axis == dim else 1 for axis in range(len(dims))])
    return gain


def bell_draw_with(own_key, extent, scale, bound, pieces, heavy, kind=jnp.bfloat16):
    values = scale * jax.random.normal(own_key, extent, jnp.float32)
    if pieces:
        values = values * block_levels(own_key, extent, pieces, -0.22, 0.18)
    return jnp.clip(strengthened(values, jax.random.fold_in(own_key, 3), *heavy), -bound, bound).astype(kind)


def setup_inputs(seed: int = 0) -> dict:
    keys = jax.random.split(jax.random.key(seed), 6)
    return {
        "velocity": draw_velocity(jax.random.fold_in(keys[5], 71), 0),
        "inv_density": jnp.clip(jnp.exp(math.log(5.0) - 3.218876 * jax.random.uniform(keys[1], (NX, NY, NZ), jnp.float32) ** block_levels(keys[1], (NX, NY, NZ), ((0, 2), (1, 4), (2, 4)), -0.2, 0.2)), 0.2, 5.0),
        "factor_x": bell_draw_with(keys[2], (NX, RANK), NX ** -0.5, 1.0, ((0, 2),), (0, 1, 2, 2.0), jnp.float32),
        "factor_y": bell_draw_with(keys[3], (NY, RANK), NY ** -0.5, 0.5, ((0, 4),), (0, 1, 4, 2.0), jnp.float32),
        "factor_z": bell_draw_with(keys[4], (NZ, RANK), NZ ** -0.5, 0.375, ((0, 4),), (0, 1, 4, 2.0), jnp.float32),
    }


SHIFT = 0.1
HIGHEST = lax.Precision.HIGHEST


def neighbours(padded):
    centre_cut = (slice(None),) + (slice(1, -1),) * 3
    result = []
    for dimension in range(1, 4):
        forward = list(centre_cut)
        forward[dimension] = slice(2, None)
        backward = list(centre_cut)
        backward[dimension] = slice(None, -2)
        result.append((padded[tuple(forward)], padded[tuple(backward)]))
    return result


def pad_cells(stack):
    return jnp.pad(stack, ((0, 0), (1, 1), (1, 1), (1, 1)))


def assemble(sides, inv_density):
    couplings = []
    diagonal = SHIFT + jnp.zeros_like(inv_density)
    divergence = jnp.zeros_like(inv_density)
    for dimension in range(3):
        forward, backward = sides[dimension]
        c_forward = 0.5 * (inv_density + forward[3])
        c_backward = 0.5 * (inv_density + backward[3])
        couplings.append((c_forward, c_backward))
        diagonal = diagonal + c_forward + c_backward
        divergence = divergence + 0.5 * (forward[dimension] - backward[dimension])
    return couplings, diagonal, -divergence


def apply_operator(sides, field, couplings, diagonal):
    result = diagonal * field
    for dimension in range(3):
        forward, backward = sides[dimension]
        result = result - couplings[dimension][0] * forward[0] - couplings[dimension][1] * backward[0]
    return result


def correct(sides, velocity, inv_density):
    parts = []
    for dimension in range(3):
        gradient = 0.5 * (sides[dimension][0][0] - sides[dimension][1][0])
        parts.append(velocity[dimension] - inv_density * gradient)
    return jnp.stack(parts, 0)


def reference(velocity, inv_density, factor_x, factor_y, factor_z):
    sides = neighbours(pad_cells(jnp.concatenate([velocity, inv_density[None]], 0)))
    couplings, diagonal, rhs = assemble(sides, inv_density)

    def operate(field):
        return apply_operator(neighbours(pad_cells(field[None])), field, couplings, diagonal)

    pressure = jnp.zeros_like(rhs)
    residual = rhs
    precond = residual / diagonal
    direction = precond
    product = jnp.sum(residual * precond)
    for iteration in range(ITERS):
        image = operate(direction)
        alpha = product / jnp.sum(direction * image)
        pressure = pressure + alpha * direction
        residual = residual - alpha * image
        precond = residual / diagonal
        fresh = jnp.sum(residual * precond)
        direction = precond + (fresh / product) * direction
        product = fresh
    corrected = correct(neighbours(pad_cells(pressure[None])), velocity, inv_density)
    fields = jnp.concatenate([corrected, pressure[None]], 0)
    first = jnp.einsum("fijk,ia->afjk", fields, factor_x, precision=HIGHEST)
    second = jnp.einsum("afjk,jb->afbk", first, factor_y, precision=HIGHEST)
    core = jnp.einsum("afbk,kc->afbc", second, factor_z, precision=HIGHEST)
    return pressure, corrected, core
```

```python
import functools

import jax
import jax.numpy as jnp
from jax import lax
from jax.experimental import pallas as pl
from jax.experimental.pallas import tpu as pltpu
from jax.sharding import PartitionSpec as P

ITERS = 4
SHIFT = 0.1
AXES = ("gx", "gy", "gz")

REACH = ITERS
LAYERS = ITERS + 1
WIDE = 8
SLOT = 16
ROWS = 24
NEWTON = (0.5, 0.5, 0.5)
PAIRS = [(a, b) for a in range(ITERS) for b in range(a, ITERS)]
VMEM = pl.BlockSpec(memory_space=pltpu.VMEM)
SMEM = pl.BlockSpec(memory_space=pltpu.SMEM)
F32 = jnp.float32
BF16 = jnp.bfloat16


def call(body, outs, operands, scratch=(), smem=0, limit=56):
    return pl.pallas_call(
        body,
        out_shape=[jax.ShapeDtypeStruct(shape, F32) for shape in outs],
        in_specs=[SMEM] * smem + [VMEM] * (len(operands) - smem),
        out_specs=[VMEM] * len(outs),
        scratch_shapes=[pltpu.VMEM(shape, F32) for shape in scratch],
        compiler_params=pltpu.CompilerParams(vmem_limit_bytes=limit * 2**20),
    )(*operands)


def lanes(shape):
    return lax.broadcasted_iota(jnp.int32, shape, len(shape) - 1)


def sublanes(shape):
    return lax.broadcasted_iota(jnp.int32, shape, len(shape) - 2)


def exchange(up, down, axis):
    count = lax.axis_size(axis)
    ends = count - 1
    below = lax.ppermute(up, axis, [(i, i + 1) for i in range(ends)])
    above = lax.ppermute(down, axis, [(i + 1, i) for i in range(ends)])
    return below, above


def pack_x(velocity, inv, rhs, up, down):
    nx, ny, nz = inv.shape
    shape = (ny, nz)
    first_lane, last_lane = lanes(shape) == 0, lanes(shape) == nz - 1
    first_row, last_row = sublanes(shape) == 0, sublanes(shape) == ny - 1

    def plane(x, carry):
        before = jnp.where(x == 0, 0.0, velocity[0, jnp.maximum(x - 1, 0)])
        after = jnp.where(x == nx - 1, 0.0, velocity[0, jnp.minimum(x + 1, nx - 1)])
        along_y = velocity[1, x]
        along_z = velocity[2, x]
        total = after - before
        total = total + jnp.where(last_row, 0.0, pltpu.roll(along_y, ny - 1, 0))
        total = total - jnp.where(first_row, 0.0, pltpu.roll(along_y, 1, 0))
        total = total + jnp.where(last_lane, 0.0, pltpu.roll(along_z, nz - 1, 1))
        total = total - jnp.where(first_lane, 0.0, pltpu.roll(along_z, 1, 1))
        rhs[x] = -0.5 * total
        return carry

    lax.fori_loop(0, nx, plane, 0)
    for message, start, own, sign, layer in (
        (up, nx - REACH, nx - 1, 0.5, nx - LAYERS),
        (down, 0, 0, -0.5, 0),
    ):
        for k in range(REACH):
            message[k * ny : (k + 1) * ny, :] = rhs[start + k]
        base = REACH * ny
        message[base : base + ny, :] = sign * velocity[0, own]
        base += ny
        for k in range(LAYERS):
            message[base : base + ny, :] = inv[layer + k]
            base += ny
        ends = jnp.zeros(shape, F32)
        for k in range(REACH):
            plane_z = velocity[2, start + k]
            ends = jnp.where(lanes(shape) == 2 * k, plane_z[:, 0:1], ends)
            ends = jnp.where(lanes(shape) == 2 * k + 1, plane_z[:, nz - 1 : nz], ends)
        message[base : base + ny, :] = ends
        base += ny
        for k in range(REACH):
            message[base + 2 * k : base + 2 * k + 1, :] = velocity[1, start + k, 0:1, :]
            message[base + 2 * k + 1 : base + 2 * k + 2, :] = velocity[1, start + k, ny - 1 : ny, :]


def pack_y(velocity, inv, rhs, below, above, up, down):
    nx, ny, nz = inv.shape
    each = REACH + 1 + LAYERS + 1

    def put(pair, parity, rows_rhs, ghost, rows_inv, first, last):
        offset = parity * each
        for message, part in ((up, 1), (down, 0)):
            message[pair, pl.ds(offset, REACH), :] = rows_rhs[part]
            message[pair, pl.ds(offset + REACH, 1), :] = (0.5 if part else -0.5) * ghost[part]
            message[pair, pl.ds(offset + REACH + 1, LAYERS), :] = rows_inv[part]
            ends = jnp.zeros((1, nz), F32)
            for k in range(REACH):
                ends = jnp.where(lanes((1, nz)) == 2 * k, first[part][k : k + 1], ends)
                ends = jnp.where(lanes((1, nz)) == 2 * k + 1, last[part][k : k + 1], ends)
            message[pair, pl.ds(offset + each - 1, 1), :] = ends

    def halo(x, message, k_rhs, k_inv, extra):
        base = (REACH + 1 + k_inv) * ny
        rows_inv = (message[pl.ds(base, LAYERS), :], message[pl.ds(base + ny - LAYERS, LAYERS), :])
        zero_row = jnp.zeros((1, nz), F32)
        zero = jnp.zeros((REACH, nz), F32)
        if k_rhs is None:
            column = jnp.zeros((REACH, 1), F32)
            put(x // 2, x % 2, (zero, zero), (zero_row, zero_row), rows_inv, (column, column), (column, column))
            return
        low, high = message[pl.ds(k_rhs * ny, REACH), :], message[pl.ds((k_rhs + 1) * ny - REACH, REACH), :]
        if extra is not None:
            sign, source = extra
            low = low + sign * velocity[0, source, 0:REACH, :]
            high = high + sign * velocity[0, source, ny - REACH : ny, :]
        ends = (REACH + 1 + LAYERS) * ny
        lines = ends + ny + 2 * k_rhs
        ghost = (message[pl.ds(lines, 1), :], message[pl.ds(lines + 1, 1), :])
        head, tail = message[pl.ds(ends, REACH), :], message[pl.ds(ends + ny - REACH, REACH), :]
        first = (head[:, 2 * k_rhs : 2 * k_rhs + 1], tail[:, 2 * k_rhs : 2 * k_rhs + 1])
        last = (head[:, 2 * k_rhs + 1 : 2 * k_rhs + 2], tail[:, 2 * k_rhs + 1 : 2 * k_rhs + 2])
        put(x // 2, x % 2, (low, high), ghost, rows_inv, first, last)

    for k in range(LAYERS):
        halo(k, below, k - 1 if k else None, k, (-0.5, 0) if k == LAYERS - 1 else None)
        halo(
            nx + LAYERS + k,
            above,
            k if k < REACH else None,
            k,
            (0.5, nx - 1) if k == 0 else None,
        )

    def own(x, pair, parity, extra):
        low, high = rhs[x, 0:REACH, :], rhs[x, ny - REACH : ny, :]
        if extra is not None:
            low = low + extra[pl.ds(REACH * ny, REACH), :]
            high = high + extra[pl.ds((REACH + 1) * ny - REACH, REACH), :]
        ghost = (velocity[1, x, 0:1, :], velocity[1, x, ny - 1 : ny, :])
        rows_inv = (inv[x, 0:LAYERS, :], inv[x, ny - LAYERS : ny, :])
        head, tail = velocity[2, x, 0:REACH, :], velocity[2, x, ny - REACH : ny, :]
        first = (head[:, 0:1], tail[:, 0:1])
        last = (head[:, nz - 1 : nz], tail[:, nz - 1 : nz])
        put(pair, parity, (low, high), ghost, rows_inv, first, last)

    def at(x, extra):
        own(x, (x + LAYERS) // 2, (x + LAYERS) % 2, extra)

    at(0, below)
    at(nx - 1, above)
    begin = 1 + (1 + LAYERS) % 2
    finish = begin + (nx - 1 - begin) // 2 * 2
    for x in (*range(1, begin), *range(finish, nx - 1)):
        at(x, None)

    def planes(n, carry):
        for parity in range(2):
            own(begin + 2 * n + parity, (begin + LAYERS) // 2 + n, parity, None)
        return carry

    lax.fori_loop(0, (finish - begin) // 2, planes, 0)


def pack_z(velocity, inv, rhs, below, above, before, after, rhs_wide, inv_wide, up, down, ends):
    nx, ny, nz = inv.shape
    wide = nx + 2 * LAYERS
    rows = ny + 2 * WIDE
    each = REACH + 1 + LAYERS + 1
    group = nz // SLOT
    mine = pl.ds(WIDE, ny)

    edge = (WIDE, nz)
    zero_edge = jnp.zeros(edge, F32)
    for k in range(LAYERS):
        for message, x, layer in ((below, k, k - 1), (above, nx + LAYERS + k, k if k < REACH else -1)):
            base = (REACH + 1 + k) * ny
            inv_wide[x, mine, :] = message[pl.ds(base, ny), :]
            if layer < 0:
                rhs_wide[x, mine, :] = jnp.zeros((ny, nz), F32)
                ends[x, mine, :] = jnp.zeros((ny, nz), F32)
                continue
            part = message[pl.ds(layer * ny, ny), :]
            if x == LAYERS - 1:
                part = part - 0.5 * velocity[0, 0]
            if x == nx + LAYERS:
                part = part + 0.5 * velocity[0, nx - 1]
            rhs_wide[x, mine, :] = part
            line = message[pl.ds((REACH + 1 + LAYERS) * ny, ny), :]
            ends[x, mine, :] = jnp.where(
                lanes((ny, nz)) == 0, line[:, 2 * layer : 2 * layer + 1], line[:, 2 * layer + 1 : 2 * layer + 2]
            )

    def plane(x, carry):
        inv_wide[x + LAYERS, mine, :] = inv[x]
        rhs_wide[x + LAYERS, mine, :] = rhs[x]
        ends[x + LAYERS, mine, :] = velocity[2, x]
        return carry

    lax.fori_loop(0, nx, plane, 0)
    rhs_wide[LAYERS, mine, :] += below[pl.ds(REACH * ny, ny), :]
    rhs_wide[LAYERS + nx - 1, mine, :] += above[pl.ds(REACH * ny, ny), :]

    def finish(x, ghost_low, ghost_high):
        low, high = before[x // 2], after[x // 2]
        low = jnp.where(x % 2 == 0, low, pltpu.roll(low, ROWS - each, 0))[0:SLOT]
        high = jnp.where(x % 2 == 0, high, pltpu.roll(high, ROWS - each, 0))[0:SLOT]
        row = sublanes((SLOT, nz))
        part = pltpu.roll(low, WIDE - REACH, 0)[0:WIDE]
        part = jnp.where(sublanes(edge) >= WIDE - REACH, part, 0.0)
        part = part - jnp.where(sublanes(edge) == WIDE - 1, 0.5 * ghost_low, 0.0)
        rhs_wide[x, 0:WIDE, :] = part
        part = pltpu.roll(low, SLOT - (REACH + 1) + WIDE - LAYERS, 0)[0:WIDE]
        inv_wide[x, 0:WIDE, :] = jnp.where(sublanes(edge) >= WIDE - LAYERS, part, 0.0)
        part = jnp.where(sublanes(edge) < REACH, high[0:WIDE], 0.0)
        part = part + jnp.where(sublanes(edge) == 0, 0.5 * ghost_high, 0.0)
        rhs_wide[x, WIDE + ny : rows, :] = part
        part = pltpu.roll(high, SLOT - (REACH + 1), 0)[0:WIDE]
        inv_wide[x, WIDE + ny : rows, :] = jnp.where(sublanes(edge) < LAYERS, part, 0.0)
        head = rhs_wide[x, WIDE : 2 * WIDE, :]
        rhs_wide[x, WIDE : 2 * WIDE, :] = head + jnp.where(sublanes(edge) == 0, low[REACH : REACH + 1], 0.0)
        tail = rhs_wide[x, ny : WIDE + ny, :]
        rhs_wide[x, ny : WIDE + ny, :] = tail + jnp.where(
            sublanes(edge) == WIDE - 1, high[REACH : REACH + 1], 0.0
        )
        for message, start, place in ((low, WIDE - REACH, 0), (high, 0, WIDE + ny)):
            line = message[each - 1 : each]
            one = jnp.zeros(edge, F32)
            two = jnp.zeros(edge, F32)
            for k in range(REACH):
                here = sublanes(edge) == start + k
                one = jnp.where(here, line[:, 2 * k : 2 * k + 1], one)
                two = jnp.where(here, line[:, 2 * k + 1 : 2 * k + 2], two)
            ends[x, place : place + WIDE, :] = jnp.where(lanes(edge) == 0, one, two)
        slot = x // group, (x % group) * SLOT
        whole = (rows, nz)
        lane = lanes(whole)
        r, i, e = rhs_wide[x], inv_wide[x], ends[x]
        base = slot[1]
        inside = (lane >= base) & (lane < base + SLOT)
        place = lane - base
        value = jnp.where(place < REACH, pltpu.roll(r, base + REACH, 1), pltpu.roll(i, base + REACH + 1 + LAYERS, 1))
        value = jnp.where(place == REACH, 0.5 * e[:, nz - 1 : nz], value)
        up[slot[0]] = jnp.where(inside, value, up[slot[0]])
        value = jnp.where(place < REACH, pltpu.roll(r, base, 1), pltpu.roll(i, base + REACH + 1, 1))
        value = jnp.where(place == REACH, -0.5 * e[:, 0:1], value)
        down[slot[0]] = jnp.where(inside, value, down[slot[0]])

    up[...] = jnp.zeros(up.shape, F32)
    down[...] = jnp.zeros(down.shape, F32)
    for k in range(LAYERS):
        for message, x, layer in ((below, k, k - 1), (above, nx + LAYERS + k, k if k < REACH else -1)):
            lines = (REACH + 1 + LAYERS + 1) * ny + 2 * layer
            if layer < 0:
                zero = jnp.zeros((1, nz), F32)
                finish(x, zero, zero)
            else:
                finish(x, message[lines : lines + 1, :], message[lines + 1 : lines + 2, :])

    def middle(x, carry):
        finish(x + LAYERS, velocity[1, x, 0:1, :], velocity[1, x, ny - 1 : ny, :])
        return carry

    lax.fori_loop(0, nx, middle, 0)


def basis(rhs_wide, inv_wide, ends, before, after, *refs):
    outs, dots, (im, ih, axm, axh, aym, ayh, azm, azh, hdm, hdh, vm, vh) = refs[: ITERS + 1], refs[ITERS + 1], refs[ITERS + 2 :]
    wide, rows, nz = inv_wide.shape
    nx, ny = wide - 2 * LAYERS, rows - 2 * WIDE
    group = nz // SLOT
    tile = (WIDE, nz)
    tiles = rows // WIDE
    lane = lanes(tile)
    first, last = lane == 0, lane == nz - 1

    def left(main, side):
        a, b = pltpu.roll(main, 1, 1), pltpu.roll(side, 1, 1)
        return jnp.where(first, b, a), jnp.where(first, a, b)

    def right(main, side):
        a, b = pltpu.roll(main, nz - 1, 1), pltpu.roll(side, nz - 1, 1)
        return jnp.where(last, b, a), jnp.where(last, a, b)

    def shifted(ref, x, t, step):
        start = t * WIDE + step
        if start < 0:
            return pltpu.roll(ref[x, 0:WIDE, :], 1, 0)
        if start + WIDE > rows:
            return pltpu.roll(ref[x, rows - WIDE : rows, :], WIDE - 1, 0)
        return ref[x, start : start + WIDE, :]

    def load(x, carry):
        g, s = x // group, (x % group) * SLOT
        for t in range(tiles):
            here = slice(t * WIDE, (t + 1) * WIDE)
            low, high = before[g, here, :], after[g, here, :]
            i = inv_wide[x, here, :]
            im[x, here, :] = i
            side = pltpu.roll(high, lax.rem(2 * nz - s - REACH - 1, nz), 1)
            other = pltpu.roll(low, lax.rem(2 * nz - s - REACH - 1 - LAYERS, nz), 1)
            ih[x, here, :] = jnp.where(lane < LAYERS, side, jnp.where(lane >= nz - LAYERS, other, 0.0))
            p = pltpu.roll(low, lax.rem(2 * nz - s - REACH, nz), 1)
            r = rhs_wide[x, here, :]
            r = r + jnp.where(first, p, 0.0) + jnp.where(last, side, 0.0)
            e = ends[x, here, :]
            q = pltpu.roll(high, lax.rem(nz - s, nz), 1)
            q = jnp.where(lane < REACH, q, 0.0) + jnp.where(first, 0.5 * e[:, nz - 1 : nz], 0.0)
            p = jnp.where(lane >= nz - REACH, p, 0.0) - jnp.where(last, 0.5 * e[:, 0:1], 0.0)
            vm[0, x, here, :] = r
            vh[0, x, here, :] = jnp.where(lane < REACH, q, p)
        return carry

    lax.fori_loop(0, wide, load, 0)

    def setup(x, carry):
        for t in range(tiles):
            here = slice(t * WIDE, (t + 1) * WIDE)
            m, h = im[x, here, :], ih[x, here, :]
            m_r, h_r = right(m, h)
            m_l, h_l = left(m, h)
            for ref, ax, ay, az, hd, v, c, c_r, c_l in (
                (im, axm, aym, azm, hdm, vm, m, m_r, m_l),
                (ih, axh, ayh, azh, hdh, vh, h, h_r, h_l),
            ):
                x_f, x_b = ref[x + 1, here, :], ref[x - 1, here, :]
                y_f, y_b = shifted(ref, x, t, 1), shifted(ref, x, t, -1)
                ax[x, here, :] = 0.5 * (c + x_f)
                ay[x, here, :] = 0.5 * (c + y_f)
                az[x, here, :] = 0.5 * (c + c_r)
                total = (x_f + x_b) + (y_f + y_b) + (c_r + c_l)
                diagonal = SHIFT + 0.5 * (6.0 * c + total)
                inverse = jnp.where(c > 0.0, 1.0 / diagonal, 0.0)
                hd[x, here, :] = inverse
                v[0, x, here, :] = v[0, x, here, :] * inverse
        return carry

    lax.fori_loop(1, wide - 1, setup, 0)
    for ref in (vm, vh):
        ref[0, 0] = jnp.zeros((rows, nz), F32)
        ref[0, wide - 1] = jnp.zeros((rows, nz), F32)
    for ref in (axm, axh):
        ref[0] = jnp.zeros((rows, nz), F32)

    def couple(k, x, t, sides):
        here = slice(t * WIDE, (t + 1) * WIDE)
        m, h = vm[k, x, here, :], vh[k, x, here, :]
        fm, fh = azm[x, here, :] * m, azh[x, here, :] * h
        m_r, h_r = right(m, h)
        m_l, h_l = left(fm, fh)
        result = []
        for v, ax, ay, az, c, c_r, c_l in (
            (vm, axm, aym, azm, m, m_r, m_l),
            (vh, axh, ayh, azh, h, h_r, h_l),
        )[:sides]:
            total = ax[x, here, :] * v[k, x + 1, here, :] + ax[x - 1, here, :] * v[k, x - 1, here, :]
            total = total + (az[x, here, :] * c_r + c_l)
            y_f = shifted(v.at[k], x, t, 1)
            y_b = shifted(v.at[k], x, t, -1)
            total = total + (ay[x, here, :] * y_f + shifted(ay, x, t, -1) * y_b)
            result.append((c, total))
        return result

    for k in range(ITERS - 1):
        scale = 1.0 - NEWTON[k]

        def step(x, carry, k=k, scale=scale):
            for t in range(tiles):
                here = slice(t * WIDE, (t + 1) * WIDE)
                for (c, total), hd, v in zip(couple(k, x, t, 2), (hdm, hdh), (vm, vh)):
                    value = -hd[x, here, :] * total
                    if scale:
                        value = value + scale * c
                    v[k + 1, x, here, :] = value
            return carry

        lax.fori_loop(2 + k, wide - 2 - k, step, 0)

    def measure(x, sums):
        sums = list(sums)
        for t in range(1, tiles - 1):
            here = slice(t * WIDE, (t + 1) * WIDE)
            (own, total), = couple(ITERS - 1, x, t, 1)
            d = 1.0 / hdm[x, here, :]
            v = [vm[k, x, here, :] for k in range(ITERS)]
            w = [d * one for one in v]
            for n, (a, b) in enumerate(PAIRS):
                sums[n] = sums[n] + v[a] * w[b]
            sums[-1] = sums[-1] + own * (w[-1] - total)
        return tuple(sums)

    sums = lax.fori_loop(
        LAYERS, LAYERS + nx, measure, (jnp.zeros(tile, F32),) * (len(PAIRS) + 1)
    )
    row = sublanes((2 * WIDE, nz))
    message = jnp.zeros((2 * WIDE, nz), F32)
    for n, one in enumerate(sums):
        message = jnp.where(row == n, jnp.sum(one, axis=0, keepdims=True), message)

    def send(n, carry):
        dots[n] = message
        return carry

    lax.fori_loop(0, dots.shape[0], send, 0)

    def result(x, carry):
        for k in range(ITERS):
            outs[k][x] = vm[k, x + LAYERS - 1]
        pieces = jnp.zeros((ny, nz), F32)
        for k in range(ITERS):
            side = vh[k, x + LAYERS - 1, WIDE : WIDE + ny, :]
            pieces = jnp.where(lanes((ny, nz)) == 2 * k, side[:, nz - 1 : nz], pieces)
            pieces = jnp.where(lanes((ny, nz)) == 2 * k + 1, side[:, 0:1], pieces)
        outs[ITERS][x] = pieces
        return carry

    lax.fori_loop(0, nx + 2, result, 0)


def coefficients(dots):
    total = jnp.sum(dots, axis=1, keepdims=True)

    def entry(n):
        return total[n : n + 1]

    gram = {}
    for n, (a, b) in enumerate(PAIRS):
        gram[a, b] = gram[b, a] = entry(n)
    last = ITERS - 1
    image = {}
    for b in range(last):
        for a in range(ITERS):
            image[a, b] = gram[a, b + 1]
            if NEWTON[b]:
                image[a, b] = image[a, b] + NEWTON[b] * gram[a, b]
    for a in range(last):
        image[a, last] = image[last, a]
    image[last, last] = entry(len(PAIRS))

    def product(table, one, two):
        total = None
        for a, left in enumerate(one):
            for b, right in enumerate(two):
                term = left * right * table[a, b]
                total = term if total is None else total + term
        return total

    unit = jnp.ones((1, 1), F32)
    pressure = []
    precond = [unit]
    direction = [unit]
    rz = gram[0, 0]
    for iteration in range(ITERS):
        alpha = rz / product(image, direction, direction)
        pressure = [
            (pressure[n] if n < len(pressure) else 0.0) + alpha * one for n, one in enumerate(direction)
        ]
        if iteration == last:
            break
        moved = []
        for n in range(len(direction) + 1):
            value = None
            if n < len(direction) and NEWTON[n]:
                value = NEWTON[n] * direction[n]
            if n > 0:
                value = direction[n - 1] if value is None else value + direction[n - 1]
            moved.append(value)
        fresh_precond = []
        for n, one in enumerate(moved):
            old = precond[n] if n < len(precond) else None
            if one is None:
                fresh_precond.append(old)
            else:
                fresh_precond.append(-alpha * one if old is None else old - alpha * one)
        precond = fresh_precond
        fresh = product(gram, precond, precond)
        beta = fresh / rz
        direction = [
            one + beta * direction[n] if n < len(direction) else one for n, one in enumerate(precond)
        ]
        rz = fresh
    return pressure


def finish(dots, velocity, inv, columns, *refs):
    spans = refs[:ITERS]
    sides = refs[ITERS]
    pressure, corrected, keep, keep_more, send, p, cut = refs[ITERS + 1 :]
    nx, ny, nz = inv.shape
    shape = (ny, nz)
    lane = lanes(shape)
    total = dots[0]
    for n in range(1, dots.shape[0]):
        total = total + dots[n]
    weights = coefficients(total)
    mixed = jnp.zeros((1, nz), F32)
    for k, one in enumerate(weights):
        mixed = jnp.where(lanes((1, nz)) // 2 == k, one, mixed)

    def combine(x, carry):
        value = weights[0] * spans[0][x]
        for k in range(1, ITERS):
            value = value + weights[k] * spans[k][x]
        p[x] = value
        return carry

    lax.fori_loop(0, nx + 2, combine, 0)
    mine = slice(WIDE, WIDE + ny)
    half = columns.shape[0] // 2
    ranks = half // 2

    def pair(n, carry):
        for which in range(2):
            x = 2 * n + which
            centre = p[x + 1, mine, :]
            gap = sides[x + 1] * mixed
            step = 2
            while step < 2 * ITERS:
                gap = gap + pltpu.roll(gap, nz - step, 1)
                step *= 2
            before = jnp.where(lane == 0, gap, pltpu.roll(centre, 1, 1))
            after = jnp.where(lane == nz - 1, pltpu.roll(gap, nz - 2, 1), pltpu.roll(centre, nz - 1, 1))
            pressure[x] = centre
            half_inv = 0.5 * inv[x]
            slopes = (
                p[x + 2, mine, :] - p[x, mine, :],
                p[x + 1, WIDE + 1 : WIDE + 1 + ny, :] - p[x + 1, WIDE - 1 : WIDE - 1 + ny, :],
                after - before,
            )
            fields = [velocity[d, x] - half_inv * slopes[d] for d in range(3)] + [centre]
            for d in range(3):
                corrected[d, x] = fields[d]
            for f, field in enumerate(fields):
                high = field.astype(BF16)
                low = (field - high.astype(F32)).astype(BF16)
                cut[f, which * ny : (which + 1) * ny, 0:nz] = high
                cut[f, which * ny : (which + 1) * ny, nz : 2 * nz] = low
        for f in range(4):
            out = lax.dot_general(
                columns[...], cut[f], (((1,), (1,)), ((), ())), preferred_element_type=F32
            )
            out = out[:half] + out[half:]
            block = f * (nx // 2) + n
            quarter = half // 4
            keep[block] = out[0:quarter]
            keep_more[block] = out[quarter : 2 * quarter]
            send[0, block] = out[2 * quarter : 3 * quarter]
            send[1, block] = out[3 * quarter :]
        return carry

    lax.fori_loop(0, nx // 2, pair, 0)


def split(value):
    high = value.astype(BF16)
    return high, (value - high.astype(F32)).astype(BF16)


def split_table(value):
    high = lax.reduce_precision(value, exponent_bits=8, mantissa_bits=7)
    return high.astype(BF16), (value - high).astype(BF16)


def three(a, b, dims=(((1,), (0,)), ((), ()))):
    dot = functools.partial(lax.dot_general, dimension_numbers=dims, preferred_element_type=F32)
    (ah, al), (bh, bl) = a, b
    return dot(ah, bh) + (dot(al, bh) + dot(ah, bl))


def rank_y(kept, came, wide_high, wide_low, keep, keep_more, send):
    blocks, ranks, nz = kept.shape
    group = wide_high.shape[0] // nz
    parts = []
    for n in range(blocks // group):
        parts.append(
            jnp.concatenate(
                [kept[n * group + q] + came[n * group + q] for q in range(group)], axis=1
            )
        )
    x = jnp.concatenate(parts, axis=0)
    out = three(split(x), (wide_high[...], wide_low[...]))
    quarter = out.shape[1] // 4
    keep[...] = out[:, 0:quarter]
    keep_more[...] = out[:, quarter : 2 * quarter]
    send[0] = out[:, 2 * quarter : 3 * quarter]
    send[1] = out[:, 3 * quarter :]


def rank_x(ranks, kept, came, wide_high, wide_low, *outs):
    u = kept[...] + came[...]
    rows, nz = u.shape
    group = wide_high.shape[0] // nz
    parts = []
    for f in range(rows // ranks // group):
        parts.append(
            jnp.concatenate(
                [u[(f * group + q) * ranks : (f * group + q + 1) * ranks] for q in range(group)], axis=1
            )
        )
    x = jnp.concatenate(parts, axis=0)
    out = three(split(x), (wide_high[...], wide_low[...]))
    width = out.shape[1] // len(outs)
    for n, ref in enumerate(outs):
        ref[...] = out[:, n * width : (n + 1) * width]


def last_core(kept, came, core):
    ranks_x, fields, ranks_y, ranks_z = core.shape
    z = jnp.transpose(kept[...] + came[...])
    for f in range(fields):
        core[:, f] = z[:, f * ranks_z : (f + 1) * ranks_z].reshape(ranks_x, ranks_y, ranks_z)


def relative(factor, axis):
    count = lax.axis_size(axis)
    order = [0]
    step = 1
    while step < count:
        order = order + [n + step for n in order]
        step *= 2
    bits = count.bit_length() - 1
    order = [sum(((n >> b) & 1) << (bits - 1 - b) for b in range(bits)) for n in range(count)]
    blocks = factor.reshape(factor.shape[0], count, factor.shape[1] // count)
    here = lax.axis_index(axis)
    picked = [
        lax.dynamic_index_in_dim(blocks, jnp.bitwise_xor(here, n), axis=1, keepdims=False) for n in order
    ]
    return jnp.stack(picked, axis=1)


def swap(value, axis, mask):
    count = lax.axis_size(axis)
    return lax.ppermute(value, axis, [(i, i ^ mask) for i in range(count)])


def per_device(velocity, inv_density, factor_x, factor_y, factor_z):
    nx, ny, nz = inv_density.shape
    wide, rows = nx + 2 * LAYERS, ny + 2 * WIDE
    devices = lax.axis_size("gx") * lax.axis_size("gy") * lax.axis_size("gz")
    group = nz // SLOT
    cells = (nx, ny, nz)

    message = (((REACH + 1 + LAYERS + 1) * ny + 2 * REACH), nz)
    rhs, up, down = call(pack_x, [cells, message, message], [velocity, inv_density])
    below, above = exchange(up, down, "gx")
    message = (wide // 2, ROWS, nz)
    up, down = call(pack_y, [message, message], [velocity, inv_density, rhs, below, above])
    before, after = exchange(up, down, "gy")
    message = (-(-wide // group), rows, nz)
    whole = (wide, rows, nz)
    rhs_wide, inv_wide, up, down, ends = call(
        pack_z,
        [whole, whole, message, message, whole],
        [velocity, inv_density, rhs, below, above, before, after],
    )
    before, after = exchange(up, down, "gz")
    span = (nx + 2, rows, nz)
    slots = (devices, 2 * WIDE, nz)
    *spans, dots = call(
        basis,
        [span] * ITERS + [(nx + 2, ny, nz), slots],
        [rhs_wide, inv_wide, ends, before, after],
        scratch=[whole] * 10 + [(ITERS,) + whole] * 2,
        limit=60,
    )
    dots = lax.all_to_all(dots, AXES, 0, 0, tiled=True)

    columns = relative(factor_z, "gz")
    count_z = lax.axis_size("gz")
    columns = jnp.transpose(columns.reshape(nz, -1))
    high, low = split_table(columns)
    columns = jnp.concatenate(
        [jnp.concatenate([high, high], axis=1), jnp.concatenate([low, low], axis=1)], axis=0
    )
    rank = factor_z.shape[1]
    ranks_z = rank // count_z
    blocks = 4 * nx // 2
    piece = (blocks, ranks_z, nz)
    pressure, corrected, keep, keep_more, send = pl.pallas_call(
        finish,
        out_shape=[
            jax.ShapeDtypeStruct(shape, F32)
            for shape in (cells, (3,) + cells, piece, piece, (2,) + piece)
        ],
        in_specs=[VMEM] * (4 + ITERS + 1),
        out_specs=[VMEM] * 5,
        scratch_shapes=[pltpu.VMEM(span, F32), pltpu.VMEM((4, 2 * ny, 2 * nz), BF16)],
        compiler_params=pltpu.CompilerParams(vmem_limit_bytes=56 * 2**20),
    )(dots, velocity, inv_density, columns, *spans)

    came = swap(send, "gz", 1)
    send = keep_more + came[1]
    keep = keep + came[0]
    came = swap(send, "gz", 2)

    group_y = nz // 16
    count_y = lax.axis_size("gy")
    ranks_y = rank // count_y
    planes = nz // ranks_y
    table = relative(factor_y, "gy")
    eye = jnp.eye(planes, dtype=F32)
    table = (eye[:, None, None, :, None] * table[None, :, :, None, :]).reshape(planes * ny, count_y * nz)
    keep, keep_more, send = call(
        rank_y,
        [(4 * nx // planes * ranks_z, nz)] * 2 + [(2, 4 * nx // planes * ranks_z, nz)],
        [keep, came, *split_table(table)],
    )
    came = swap(send, "gy", 1)
    send = keep_more + came[1]
    keep = keep + came[0]
    came = swap(send, "gy", 2)

    count_x = lax.axis_size("gx")
    table = relative(factor_x, "gx")
    eye = jnp.eye(ranks_y, dtype=F32)
    table = (table.reshape(nx, 1, rank, 1) * eye[None, :, None, :]).reshape(nx * ranks_y, rank * ranks_y)
    pieces = 2 if count_x > 1 else 1
    half = (4 * ranks_z, rank * ranks_y // 2)
    keep, send = call(
        functools.partial(rank_x, ranks_z), [half] * 2, [keep, came, *split_table(table)]
    )
    mask = 1
    while True:
        came = swap(send, "gx", mask)
        mask *= 2
        if mask >= count_x:
            break
        total = keep + came
        width = total.shape[1] // 2
        keep, send = total[:, :width], total[:, width:]
    core, = call(last_core, [(rank // count_x, 4, ranks_y, ranks_z)], [keep, came])
    return pressure, corrected, core


def solution(mesh):
    placed = (
        P(None, "gx", "gy", "gz"),
        P("gx", "gy", "gz"),
        P("gx", None),
        P("gy", None),
        P("gz", None),
    )
    return jax.shard_map(
        per_device,
        mesh=mesh,
        in_specs=placed,
        out_specs=(P("gx", "gy", "gz"), P(None, "gx", "gy", "gz"), P("gx", None, "gy", "gz")),
        check_vma=False,
    )
```

```python
import functools
import math

import jax
import jax.numpy as jnp
from jax import lax
from jax.experimental import pallas as pl
from jax.experimental.pallas import tpu as pltpu
from jax.sharding import PartitionSpec as P

ITERS = 4
SHIFT = 0.1
AXES = ("gx", "gy", "gz")

REACH = ITERS
LAYERS = ITERS + 1
WIDE = 8
SLOT = 16
STRIP = 2 * LAYERS
SPAN = 32
ROWS = 24
NEWTON = (0.5, 0.5, 0.5)
PAIRS = [(a, b) for a in range(ITERS) for b in range(a, ITERS)]
VMEM = pl.BlockSpec(memory_space=pltpu.VMEM)
SMEM = pl.BlockSpec(memory_space=pltpu.SMEM)
HBM = pl.BlockSpec(memory_space=pltpu.HBM)
F32 = jnp.float32
BF16 = jnp.bfloat16


def call(body, outs, operands, scratch=(), smem=0, limit=12, cost=None, far_in=(), far_out=(), sems=0):
    scratch = [pltpu.VMEM(shape, F32) if isinstance(shape, tuple) else shape for shape in scratch]
    return pl.pallas_call(
        body,
        out_shape=[
            pltpu.HBM(shape, F32) if n in far_out else jax.ShapeDtypeStruct(shape, F32)
            for n, shape in enumerate(outs)
        ],
        in_specs=[SMEM if n < smem else HBM if n in far_in else VMEM for n in range(len(operands))],
        out_specs=[HBM if n in far_out else VMEM for n in range(len(outs))],
        scratch_shapes=scratch + ([pltpu.SemaphoreType.DMA((sems,))] if sems else []),
        compiler_params=pltpu.CompilerParams(vmem_limit_bytes=limit * 2**20),
        cost_estimate=cost
        and pl.CostEstimate(flops=cost[0], bytes_accessed=cost[1], transcendentals=0),
    )(
        *(
            pltpu.with_memory_space_constraint(one, pltpu.HBM) if n in far_in else one
            for n, one in enumerate(operands)
        )
    )


def cost_of(shape):
    return 4 * math.prod(shape)


def lanes(shape):
    return lax.broadcasted_iota(jnp.int32, shape, len(shape) - 1)


def sublanes(shape):
    return lax.broadcasted_iota(jnp.int32, shape, len(shape) - 2)


def exchange(up, down, axis):
    count = lax.axis_size(axis)
    ends = count - 1
    below = lax.ppermute(up, axis, [(i, i + 1) for i in range(ends)])
    above = lax.ppermute(down, axis, [(i + 1, i) for i in range(ends)])
    return below, above


def source(velocity, x, nx):
    ny, nz = velocity.shape[2:]
    shape = (ny, nz)
    before = jnp.where(x == 0, 0.0, velocity[0, jnp.maximum(x - 1, 0)])
    after = jnp.where(x == nx - 1, 0.0, velocity[0, jnp.minimum(x + 1, nx - 1)])
    along_y = velocity[1, x]
    along_z = velocity[2, x]
    total = after - before
    total = total + jnp.where(sublanes(shape) == ny - 1, 0.0, pltpu.roll(along_y, ny - 1, 0))
    total = total - jnp.where(sublanes(shape) == 0, 0.0, pltpu.roll(along_y, 1, 0))
    total = total + jnp.where(lanes(shape) == nz - 1, 0.0, pltpu.roll(along_z, nz - 1, 1))
    total = total - jnp.where(lanes(shape) == 0, 0.0, pltpu.roll(along_z, 1, 1))
    return -0.5 * total


def sources(velocity, rhs):
    nx = rhs.shape[0]

    def plane(x, carry):
        rhs[x] = source(velocity, x, nx)
        return carry

    lax.fori_loop(0, nx, plane, 0)


def pack_x(index, velocity_far, inv_far, *refs):
    velocity, inv, sems = refs[-3:]
    messages = refs[:-3]
    layers, ny, nz = inv.shape[1:]
    far = inv_far.shape[0] - layers
    shape = (ny, nz)
    only = len(messages) == 1
    first = index[0] == 0

    def copies(n):
        start = jnp.where(first, far, 0) if only else (far, 0)[n]
        part = pl.ds(start, layers)
        yield pltpu.make_async_copy(inv_far.at[part], inv.at[n], sems.at[4 * n])
        for d in range(3):
            yield pltpu.make_async_copy(velocity_far.at[d, part], velocity.at[n, d], sems.at[4 * n + d + 1])

    for n in range(len(messages)):
        for copy in copies(n):
            copy.start()

    def fill(n, start, own, sign):
        message, near = messages[n], velocity.at[n]
        for k in range(REACH):
            message[k * ny : (k + 1) * ny, :] = source(near, start + k, layers)
        base = REACH * ny
        message[base : base + ny, :] = sign * near[0, own]
        base += ny
        for k in range(LAYERS):
            message[base : base + ny, :] = inv[n, k]
            base += ny
        ends = jnp.zeros(shape, F32)
        for k in range(REACH):
            plane_z = near[2, start + k]
            ends = jnp.where(lanes(shape) == 2 * k, plane_z[:, 0:1], ends)
            ends = jnp.where(lanes(shape) == 2 * k + 1, plane_z[:, nz - 1 : nz], ends)
        message[base : base + ny, :] = ends
        base += ny
        for k in range(REACH):
            message[base + 2 * k : base + 2 * k + 1, :] = near[1, start + k, 0:1, :]
            message[base + 2 * k + 1 : base + 2 * k + 2, :] = near[1, start + k, ny - 1 : ny, :]

    for n in range(len(messages)):
        for copy in copies(n):
            copy.wait()
    upper = (1, layers - 1, 0.5)
    lower = (0, 0, -0.5)
    if only:
        fill(0, *(jnp.where(first, one, two) for one, two in zip(upper, lower)))
    else:
        fill(0, *upper)
        fill(1, *lower)


class Scaled:
    def __init__(self, ref, factor):
        self.ref, self.factor = ref, factor

    def __getitem__(self, where):
        return self.ref[where] * self.factor


def sides_x(index, messages):
    if len(messages) == 2:
        return messages
    first = jnp.where(index[0] == 0, 1.0, 0.0)
    return Scaled(messages[0], 1.0 - first), Scaled(messages[0], first)


def pack_y(index, velocity, inv, rhs, *refs):
    (below, above), (up, down) = sides_x(index, refs[:-2]), refs[-2:]
    nx, ny, nz = inv.shape
    each = REACH + 1 + LAYERS + 1

    def put(pair, parity, rows_rhs, ghost, rows_inv, first, last):
        offset = parity * each
        for message, part in ((up, 1), (down, 0)):
            message[pair, pl.ds(offset, REACH), :] = rows_rhs[part]
            message[pair, pl.ds(offset + REACH, 1), :] = (0.5 if part else -0.5) * ghost[part]
            message[pair, pl.ds(offset + REACH + 1, LAYERS), :] = rows_inv[part]
            ends = jnp.zeros((1, nz), F32)
            for k in range(REACH):
                ends = jnp.where(lanes((1, nz)) == 2 * k, first[part][k : k + 1], ends)
                ends = jnp.where(lanes((1, nz)) == 2 * k + 1, last[part][k : k + 1], ends)
            message[pair, pl.ds(offset + each - 1, 1), :] = ends

    def halo(x, message, k_rhs, k_inv, extra):
        base = (REACH + 1 + k_inv) * ny
        rows_inv = (message[pl.ds(base, LAYERS), :], message[pl.ds(base + ny - LAYERS, LAYERS), :])
        zero_row = jnp.zeros((1, nz), F32)
        zero = jnp.zeros((REACH, nz), F32)
        if k_rhs is None:
            column = jnp.zeros((REACH, 1), F32)
            put(x // 2, x % 2, (zero, zero), (zero_row, zero_row), rows_inv, (column, column), (column, column))
            return
        low, high = message[pl.ds(k_rhs * ny, REACH), :], message[pl.ds((k_rhs + 1) * ny - REACH, REACH), :]
        if extra is not None:
            sign, source = extra
            low = low + sign * velocity[0, source, 0:REACH, :]
            high = high + sign * velocity[0, source, ny - REACH : ny, :]
        ends = (REACH + 1 + LAYERS) * ny
        lines = ends + ny + 2 * k_rhs
        ghost = (message[pl.ds(lines, 1), :], message[pl.ds(lines + 1, 1), :])
        head, tail = message[pl.ds(ends, REACH), :], message[pl.ds(ends + ny - REACH, REACH), :]
        first = (head[:, 2 * k_rhs : 2 * k_rhs + 1], tail[:, 2 * k_rhs : 2 * k_rhs + 1])
        last = (head[:, 2 * k_rhs + 1 : 2 * k_rhs + 2], tail[:, 2 * k_rhs + 1 : 2 * k_rhs + 2])
        put(x // 2, x % 2, (low, high), ghost, rows_inv, first, last)

    for k in range(LAYERS):
        halo(k, below, k - 1 if k else None, k, (-0.5, 0) if k == LAYERS - 1 else None)
        halo(
            nx + LAYERS + k,
            above,
            k if k < REACH else None,
            k,
            (0.5, nx - 1) if k == 0 else None,
        )

    def own(x, pair, parity, extra):
        low, high = rhs[x, 0:REACH, :], rhs[x, ny - REACH : ny, :]
        if extra is not None:
            low = low + extra[pl.ds(REACH * ny, REACH), :]
            high = high + extra[pl.ds((REACH + 1) * ny - REACH, REACH), :]
        ghost = (velocity[1, x, 0:1, :], velocity[1, x, ny - 1 : ny, :])
        rows_inv = (inv[x, 0:LAYERS, :], inv[x, ny - LAYERS : ny, :])
        head, tail = velocity[2, x, 0:REACH, :], velocity[2, x, ny - REACH : ny, :]
        first = (head[:, 0:1], tail[:, 0:1])
        last = (head[:, nz - 1 : nz], tail[:, nz - 1 : nz])
        put(pair, parity, (low, high), ghost, rows_inv, first, last)

    def at(x, extra):
        own(x, (x + LAYERS) // 2, (x + LAYERS) % 2, extra)

    at(0, below)
    at(nx - 1, above)
    begin = 1 + (1 + LAYERS) % 2
    finish = begin + (nx - 1 - begin) // 2 * 2
    for x in (*range(1, begin), *range(finish, nx - 1)):
        at(x, None)

    def planes(n, carry):
        for parity in range(2):
            own(begin + 2 * n + parity, (begin + LAYERS) // 2 + n, parity, None)
        return carry

    lax.fori_loop(0, (finish - begin) // 2, planes, 0)


def pack_z(index, velocity, inv, rhs, *refs):
    (below, above), before, after = sides_x(index, refs[:-14]), refs[-14], refs[-13]
    rhs_far, inv_far, up, down, strip_rhs_far, strip_inv_far = refs[-12:-6]
    rhs_wide, inv_wide, ends, strip_rhs, strip_inv, sems = refs[-6:]
    nx, ny, nz = inv.shape
    wide = nx + 2 * LAYERS
    rows = ny + 2 * WIDE
    each = REACH + 1 + LAYERS + 1
    mine = pl.ds(WIDE, ny)
    edge = (WIDE, nz)
    groups = strip_rhs.shape[0]

    for k in range(LAYERS):
        for message, x, layer in ((below, k, k - 1), (above, nx + LAYERS + k, k if k < REACH else -1)):
            base = (REACH + 1 + k) * ny
            inv_wide[x, mine, :] = message[pl.ds(base, ny), :]
            if layer < 0:
                rhs_wide[x, mine, :] = jnp.zeros((ny, nz), F32)
                ends[x, mine, :] = jnp.zeros((ny, nz), F32)
                continue
            part = message[pl.ds(layer * ny, ny), :]
            if x == LAYERS - 1:
                part = part - 0.5 * velocity[0, 0]
            if x == nx + LAYERS:
                part = part + 0.5 * velocity[0, nx - 1]
            rhs_wide[x, mine, :] = part
            line = message[pl.ds((REACH + 1 + LAYERS) * ny, ny), :]
            ends[x, mine, :] = jnp.where(
                lanes((ny, nz)) == 0, line[:, 2 * layer : 2 * layer + 1], line[:, 2 * layer + 1 : 2 * layer + 2]
            )

    def plane(x, carry):
        inv_wide[x + LAYERS, mine, :] = inv[x]
        rhs_wide[x + LAYERS, mine, :] = rhs[x]
        ends[x + LAYERS, mine, :] = velocity[2, x]
        return carry

    lax.fori_loop(0, nx, plane, 0)
    rhs_wide[LAYERS, mine, :] += below[pl.ds(REACH * ny, ny), :]
    rhs_wide[LAYERS + nx - 1, mine, :] += above[pl.ds(REACH * ny, ny), :]
    for ref in (rhs_wide, inv_wide, ends):
        for x in range(wide, ref.shape[0]):
            ref[x] = jnp.zeros((rows, nz), F32)

    def finish(x, ghost_low, ghost_high):
        low, high = before[x // 2], after[x // 2]
        low = jnp.where(x % 2 == 0, low, pltpu.roll(low, ROWS - each, 0))[0:SLOT]
        high = jnp.where(x % 2 == 0, high, pltpu.roll(high, ROWS - each, 0))[0:SLOT]
        part = pltpu.roll(low, WIDE - REACH, 0)[0:WIDE]
        part = jnp.where(sublanes(edge) >= WIDE - REACH, part, 0.0)
        part = part - jnp.where(sublanes(edge) == WIDE - 1, 0.5 * ghost_low, 0.0)
        rhs_wide[x, 0:WIDE, :] = part
        part = pltpu.roll(low, SLOT - (REACH + 1) + WIDE - LAYERS, 0)[0:WIDE]
        inv_wide[x, 0:WIDE, :] = jnp.where(sublanes(edge) >= WIDE - LAYERS, part, 0.0)
        part = jnp.where(sublanes(edge) < REACH, high[0:WIDE], 0.0)
        part = part + jnp.where(sublanes(edge) == 0, 0.5 * ghost_high, 0.0)
        rhs_wide[x, WIDE + ny : rows, :] = part
        part = pltpu.roll(high, SLOT - (REACH + 1), 0)[0:WIDE]
        inv_wide[x, WIDE + ny : rows, :] = jnp.where(sublanes(edge) < LAYERS, part, 0.0)
        head = rhs_wide[x, WIDE : 2 * WIDE, :]
        rhs_wide[x, WIDE : 2 * WIDE, :] = head + jnp.where(sublanes(edge) == 0, low[REACH : REACH + 1], 0.0)
        tail = rhs_wide[x, ny : WIDE + ny, :]
        rhs_wide[x, ny : WIDE + ny, :] = tail + jnp.where(
            sublanes(edge) == WIDE - 1, high[REACH : REACH + 1], 0.0
        )
        for message, start, place in ((low, WIDE - REACH, 0), (high, 0, WIDE + ny)):
            line = message[each - 1 : each]
            one = jnp.zeros(edge, F32)
            two = jnp.zeros(edge, F32)
            for k in range(REACH):
                here = sublanes(edge) == start + k
                one = jnp.where(here, line[:, 2 * k : 2 * k + 1], one)
                two = jnp.where(here, line[:, 2 * k + 1 : 2 * k + 2], two)
            ends[x, place : place + WIDE, :] = jnp.where(lanes(edge) == 0, one, two)

    for k in range(LAYERS):
        for message, x, layer in ((below, k, k - 1), (above, nx + LAYERS + k, k if k < REACH else -1)):
            lines = (REACH + 1 + LAYERS + 1) * ny + 2 * layer
            if layer < 0:
                zero = jnp.zeros((1, nz), F32)
                finish(x, zero, zero)
            else:
                finish(x, message[pl.ds(lines, 1), :], message[pl.ds(lines + 1, 1), :])

    def middle(x, carry):
        finish(x + LAYERS, velocity[1, x, 0:1, :], velocity[1, x, ny - 1 : ny, :])
        return carry

    lax.fori_loop(0, nx, middle, 0)
    copies = [
        pltpu.make_async_copy(ref.at[pl.ds(0, wide)], far, sems.at[n])
        for n, (ref, far) in enumerate(((rhs_wide, rhs_far), (inv_wide, inv_far)))
    ]
    for copy in copies:
        copy.start()

    whole = (rows, nz)
    lane = lanes(whole)
    place = lane % SPAN

    def back(value, step):
        return pltpu.roll(value, nz - step, 1)

    def gather(ref, g):
        value = None
        for n in range(nz // SPAN):
            moved = pltpu.roll(ref[g + n * groups], n * SPAN + STRIP, 1)
            value = moved if value is None else jnp.where(lane >= n * SPAN, moved, value)
        return value

    def pack(g):
        r, i, e = gather(rhs_wide, g), gather(inv_wide, g), gather(ends, g)
        apart = SPAN - 2 * STRIP
        for ref, value in ((strip_rhs, r), (strip_inv, i)):
            out = jnp.where(place < STRIP, value, 0.0)
            ref[g] = jnp.where(place >= SPAN - STRIP, pltpu.roll(value, apart, 1), out)
        ghost = jnp.where(place == STRIP, 0.5 * pltpu.roll(e, 1, 1), 0.0)
        ghost = jnp.where(place == SPAN - STRIP - 1, -0.5 * pltpu.roll(e, apart - 1, 1), ghost)
        strip_rhs[g] += ghost
        out = jnp.where(place < REACH, back(r, STRIP - REACH), 0.0)
        out = jnp.where(place == REACH, 0.5 * back(e, STRIP - 1 - REACH), out)
        here = (place > REACH) & (place <= REACH + LAYERS)
        higher = jnp.where(here, pltpu.roll(i, (nz + REACH + 1 + LAYERS - STRIP) % nz, 1), out)
        out = jnp.where(place < REACH, back(r, STRIP), 0.0)
        out = jnp.where(place == REACH, -0.5 * back(e, STRIP - REACH), out)
        return higher, jnp.where(here, back(i, STRIP - REACH - 1), out)

    halves = up.shape[0]

    def both(n, carry):
        one, two = pack(n)
        up[n] = one
        down[n] = two
        return carry

    lax.fori_loop(0, halves, both, 0)

    def more(n, carry):
        one, two = pack(n + halves)
        up[n] += pltpu.roll(one, SPAN // 2, 1)
        down[n] += pltpu.roll(two, SPAN // 2, 1)
        return carry

    lax.fori_loop(0, groups - halves, more, 0)
    for ref, far in ((strip_rhs, strip_rhs_far), (strip_inv, strip_inv_far)):
        copies.append(pltpu.make_async_copy(ref, far, sems.at[len(copies)]))
        copies[-1].start()
    for copy in copies:
        copy.wait()


def shifted(ref, x, t, step):
    rows = ref.shape[1]
    start = t * WIDE + step
    if start < 0:
        return pltpu.roll(ref[x, 0:WIDE, :], 1, 0)
    if start + WIDE > rows:
        return pltpu.roll(ref[x, rows - WIDE : rows, :], WIDE - 1, 0)
    return ref[x, start : start + WIDE, :]


class Stencil:
    def __init__(self, inv, root, ax, ay, az, vs, planes, edges=None):
        self.inv, self.root, self.ax, self.ay, self.az, self.vs = inv, root, ax, ay, az, vs
        self.planes, self.edges = planes, edges or (lambda ref: None)
        self.count, self.rows, self.nz = inv.shape
        self.tiles = self.rows // WIDE

    def here(self, t):
        return slice(t * WIDE, (t + 1) * WIDE)

    def right(self, value):
        return pltpu.roll(value, self.nz - 1, 1)

    def left(self, value):
        return pltpu.roll(value, 1, 1)

    def prepare(self, rhs):
        inv, root = self.inv, self.root
        self.edges(inv)

        def scales(x, carry):
            writes = []
            for t in range(self.tiles):
                here = self.here(t)
                c = inv[x, here, :]
                total = (inv[x + 1, here, :] + inv[x - 1, here, :]) + (self.right(c) + self.left(c))
                total = total + (shifted(inv, x, t, 1) + shifted(inv, x, t, -1))
                value = jnp.where(c > 0.0, lax.rsqrt(SHIFT + 0.5 * (6.0 * c + total)), 0.0)
                writes.append((here, value, rhs[x, here, :] * value))
            for here, one, two in writes:
                root[x, here, :] = one
                self.vs[0][x, here, :] = two
            return carry

        lax.fori_loop(1, self.count - 1, scales, 0)
        zero = jnp.zeros((self.rows, self.nz), F32)
        for ref in (root, self.vs[0]):
            ref[0] = zero
            ref[self.count - 1] = zero
            self.edges(ref)

        def couplings(x, carry):
            writes = []
            for t in range(self.tiles):
                here = self.here(t)
                c, d = inv[x, here, :], root[x, here, :]
                half = 0.5 * d
                writes.append(
                    (
                        here,
                        (c + inv[x + 1, here, :]) * (half * root[x + 1, here, :]),
                        (c + shifted(inv, x, t, 1)) * (half * shifted(root, x, t, 1)),
                        (c + self.right(c)) * (half * self.right(d)),
                    )
                )
            for here, x_face, y_face, z_face in writes:
                self.ax[x, here, :] = x_face
                self.ay[x, here, :] = y_face
                self.az[x, here, :] = z_face
            return carry

        lax.fori_loop(1, self.count - 1, couplings, 0)
        self.ax[0] = zero
        self.edges(self.ax)

    def couple(self, k, x, t):
        here = self.here(t)
        v, ax, ay = self.vs[k], self.ax, self.ay
        c, f = v[x, here, :], self.az[x, here, :]
        total = ax[x, here, :] * v[x + 1, here, :] + ax[x - 1, here, :] * v[x - 1, here, :]
        total = total + (f * self.right(c) + self.left(f * c))
        total = total + ay[x, here, :] * shifted(v, x, t, 1)
        return c, total + shifted(ay, x, t, -1) * shifted(v, x, t, -1)

    def extend(self, k):
        scale = 1.0 - NEWTON[k]

        def step(x, carry):
            writes = []
            for t in range(self.tiles):
                c, total = self.couple(k, x, t)
                writes.append((t, scale * c - total if scale else -total))
            for t, value in writes:
                self.vs[k + 1][x, self.here(t), :] = value
            return carry

        start, stop = self.planes(k)
        lax.fori_loop(start, stop, step, 0)
        self.edges(self.vs[k + 1])

    def products(self, start, stop, mask):
        def measure(x, sums):
            sums = list(sums)
            for t in range(1, self.tiles - 1):
                keep = mask(x)
                v = [self.vs[k][x, self.here(t), :] for k in range(ITERS)]
                own, total = self.couple(ITERS - 1, x, t)
                kept = [jnp.where(keep, one, 0.0) for one in v]
                for n, (a, b) in enumerate(PAIRS):
                    sums[n] = sums[n] + v[a] * kept[b]
                sums[-1] = sums[-1] + kept[-1] * (own - total)
            return tuple(sums)

        zero = jnp.zeros((WIDE, self.nz), F32)
        return lax.fori_loop(start, stop, measure, (zero,) * (len(PAIRS) + 1))


def basis_main(far_rhs, far_inv, *refs):
    outs, sums = refs[: ITERS + 1], refs[ITERS + 1]
    rhs, inv, root, ax, ay, az = refs[ITERS + 2 : ITERS + 8]
    vs, sems = refs[ITERS + 8 : -1], refs[-1]
    wide, rows, nz = ax.shape
    nx = wide - 2 * LAYERS
    loads = [
        pltpu.make_async_copy(far, ref, sems.at[n]) for n, (far, ref) in enumerate(((far_rhs, rhs), (far_inv, inv)))
    ]
    for load in loads:
        load.start()
    for load in loads:
        load.wait()
    stencil = Stencil(inv, root, ax, ay, az, vs, lambda k: (2 + k, wide - 2 - k))
    copies = []

    def send(n, ref):
        copy = pltpu.make_async_copy(ref.at[pl.ds(LAYERS - 1, nx + 2)], outs[n], sems.at[2 + n])
        copy.start()
        copies.append(copy)

    stencil.prepare(rhs)
    send(ITERS, root)
    send(0, vs[0])
    for k in range(ITERS - 1):
        stencil.extend(k)
        send(k + 1, vs[k + 1])
    lane = lanes((WIDE, nz))
    inner = (lane > REACH) & (lane < nz - 1 - REACH)
    for n, one in enumerate(stencil.products(LAYERS, LAYERS + nx, lambda x: inner)):
        sums[n] = one
    for copy in copies:
        copy.wait()


def basis_strips(nx, rhs_far, inv_far, before, after, sums, *refs):
    outs, dots = refs[:ITERS], refs[ITERS]
    rhs, inv, root, ax, ay, az = refs[ITERS + 1 : ITERS + 7]
    vs, strip_rhs, strip_inv, sems = refs[ITERS + 7 : -3], *refs[-3:]
    groups, rows, nz = strip_inv.shape
    loads = [
        pltpu.make_async_copy(far, ref, sems.at[ITERS + n])
        for n, (far, ref) in enumerate(((rhs_far, strip_rhs), (inv_far, strip_inv)))
    ]
    for load in loads:
        load.start()
    for load in loads:
        load.wait()
    halves = before.shape[0]
    whole = (rows, nz)
    place = lanes(whole) % SPAN

    def edges(ref):
        ref[0] = pltpu.roll(ref[groups], SPAN, 1)
        ref[groups + 1] = pltpu.roll(ref[1], nz - SPAN, 1)

    def receive(g, low, high):
        start = SPAN - STRIP - LAYERS
        moved = pltpu.roll(low, start + 1, 1)
        r = strip_rhs[g] + jnp.where((place > start) & (place <= SPAN - STRIP), moved, 0.0)
        moved = pltpu.roll(low, start - REACH - 1, 1)
        i = strip_inv[g] + jnp.where((place >= start) & (place < SPAN - STRIP), moved, 0.0)
        moved = pltpu.roll(high, STRIP, 1)
        r = r + jnp.where((place >= STRIP) & (place < STRIP + REACH), moved, 0.0)
        moved = pltpu.roll(high, STRIP - REACH - 1, 1)
        r = r + jnp.where(place == STRIP - 1, moved, 0.0)
        i = i + jnp.where((place >= STRIP) & (place < STRIP + LAYERS), moved, 0.0)
        rhs[g + 1] = r
        inv[g + 1] = i

    def first(n, carry):
        receive(n, before[n], after[n])
        return carry

    def second(n, carry):
        half = nz - SPAN // 2
        receive(n + halves, pltpu.roll(before[n], half, 1), pltpu.roll(after[n], half, 1))
        return carry

    lax.fori_loop(0, halves, first, 0)
    lax.fori_loop(0, groups - halves, second, 0)
    stencil = Stencil(inv, root, ax, ay, az, vs, lambda k: (1, groups + 1), edges)
    stencil.prepare(rhs)
    for k in range(ITERS - 1):
        stencil.extend(k)
    lane = lanes((WIDE, nz))
    part = lane // SPAN
    spot = lane % SPAN
    ends = ((spot >= STRIP - LAYERS) & (spot < STRIP)) | (
        (spot >= SPAN - STRIP) & (spot < SPAN - STRIP + LAYERS)
    )

    def mask(x):
        plane = x - 1 + part * groups
        return ends & (plane >= LAYERS) & (plane < LAYERS + nx)

    totals = []
    for n, one in enumerate(stencil.products(1, groups + 1, mask)):
        line = jnp.sum(one + sums[n], axis=0, keepdims=True)
        totals.append(line + pltpu.roll(line, nz // 2, 1))
    row = sublanes((WIDE, nz))
    message = jnp.zeros((WIDE, nz), F32)
    for n, line in enumerate(totals):
        half = lane < nz // 2 if n < WIDE else lane >= nz // 2
        message = jnp.where((row == n % WIDE) & half, line, message)

    def send(n, carry):
        dots[n] = message
        return carry

    lax.fori_loop(0, dots.shape[0], send, 0)

    def result(g, carry):
        for k in range(ITERS):
            vs[k][g] = vs[k][g] * root[g]
        return carry

    lax.fori_loop(1, groups + 1, result, 0)
    copies = [pltpu.make_async_copy(vs[k].at[pl.ds(1, groups)], outs[k], sems.at[k]) for k in range(ITERS)]
    for copy in copies:
        copy.start()
    for copy in copies:
        copy.wait()


def coefficients(dots):
    half = lanes(dots.shape) < dots.shape[1] // 2
    one = jnp.sum(jnp.where(half, dots, 0.0), axis=1, keepdims=True)
    two = jnp.sum(jnp.where(half, 0.0, dots), axis=1, keepdims=True)

    def entry(n):
        return one[n : n + 1] if n < WIDE else two[n - WIDE : n - WIDE + 1]

    gram = {}
    for n, (a, b) in enumerate(PAIRS):
        gram[a, b] = gram[b, a] = entry(n)
    last = ITERS - 1
    image = {}
    for b in range(last):
        for a in range(ITERS):
            image[a, b] = gram[a, b + 1]
            if NEWTON[b]:
                image[a, b] = image[a, b] + NEWTON[b] * gram[a, b]
    for a in range(last):
        image[a, last] = image[last, a]
    image[last, last] = entry(len(PAIRS))

    def product(table, one, two):
        total = None
        for a, left in enumerate(one):
            for b, right in enumerate(two):
                term = left * right * table[a, b]
                total = term if total is None else total + term
        return total

    unit = jnp.ones((1, 1), F32)
    pressure = []
    precond = [unit]
    direction = [unit]
    rz = gram[0, 0]
    for iteration in range(ITERS):
        alpha = rz / product(image, direction, direction)
        pressure = [
            (pressure[n] if n < len(pressure) else 0.0) + alpha * one for n, one in enumerate(direction)
        ]
        if iteration == last:
            break
        moved = []
        for n in range(len(direction) + 1):
            value = None
            if n < len(direction) and NEWTON[n]:
                value = NEWTON[n] * direction[n]
            if n > 0:
                value = direction[n - 1] if value is None else value + direction[n - 1]
            moved.append(value)
        fresh_precond = []
        for n, one in enumerate(moved):
            old = precond[n] if n < len(precond) else None
            if one is None:
                fresh_precond.append(old)
            else:
                fresh_precond.append(-alpha * one if old is None else old - alpha * one)
        precond = fresh_precond
        fresh = product(gram, precond, precond)
        beta = fresh / rz
        direction = [
            one + beta * direction[n] if n < len(direction) else one for n, one in enumerate(precond)
        ]
        rz = fresh
    return pressure


def finish(dots, columns, *refs):
    inputs = 2 * ITERS + 3
    pressure_far, corrected_far, keep, keep_more, send, p, gaps, mixed, cut, pressure, corrected = refs[inputs : inputs + 11]
    held, sems = refs[inputs + 11 : -1], refs[-1]
    loads = [pltpu.make_async_copy(far, ref, sems.at[n]) for n, (far, ref) in enumerate(zip(refs, held))]
    for load in loads:
        load.start()
    strips, spans, roots = held[:ITERS], held[ITERS : 2 * ITERS], held[2 * ITERS]
    velocity, inv = held[2 * ITERS + 1 :]
    nx, ny, nz = inv.shape
    shape = (ny, nz)
    groups = mixed.shape[0]
    total = dots[0]
    for n in range(1, dots.shape[0]):
        total = total + dots[n]
    weights = coefficients(total)

    def strip(g, carry):
        value = weights[0] * strips[0][g]
        for k in range(1, ITERS):
            value = value + weights[k] * strips[k][g]
        mixed[g] = value
        return carry

    for load in loads[:ITERS]:
        load.wait()
    lax.fori_loop(0, groups, strip, 0)
    for load in loads[ITERS : 2 * ITERS + 1]:
        load.wait()
    mine = slice(WIDE, WIDE + ny)
    lane = lanes(spans[0].shape[1:])

    def combine(x, carry):
        value = weights[0] * spans[0][x]
        for k in range(1, ITERS):
            value = value + weights[k] * spans[k][x]
        value = value * roots[x]
        plane = x + LAYERS - 1
        ends = mixed[plane % groups]
        start = plane // groups * SPAN
        last = pltpu.roll(ends, lax.rem(2 * nz - STRIP - start, nz), 1)
        first = pltpu.roll(ends, lax.rem(nz + STRIP - SPAN - start + nz, nz), 1)
        value = jnp.where(lane < LAYERS, first, jnp.where(lane >= nz - LAYERS, last, value))
        p[x] = value
        after = pltpu.roll(jnp.where(lane == 0, last, value), nz - 1, 1)
        before = pltpu.roll(jnp.where(lane == nz - 1, first, value), 1, 1)
        gaps[x] = (after - before)[mine]
        return carry

    lax.fori_loop(0, nx + 2, combine, 0)
    half = columns.shape[0] // 2
    for load in loads[2 * ITERS + 1 :]:
        load.wait()
    batch = 4
    each = nx // batch
    stores = []

    def pair(n, carry):
        for which in range(2):
            x = 2 * n + which
            centre = p[x + 1, mine, :]
            pressure[x] = centre
            half_inv = 0.5 * inv[x]
            slopes = (
                p[x + 2, mine, :] - p[x, mine, :],
                p[x + 1, WIDE + 1 : WIDE + 1 + ny, :] - p[x + 1, WIDE - 1 : WIDE - 1 + ny, :],
                gaps[x + 1],
            )
            fields = [velocity[d, x] - half_inv * slopes[d] for d in range(3)] + [centre]
            for d in range(3):
                corrected[d, x] = fields[d]
            for f, field in enumerate(fields):
                high = field.astype(BF16)
                low = (field - high.astype(F32)).astype(BF16)
                cut[f, which * ny : (which + 1) * ny, 0:nz] = high
                cut[f, which * ny : (which + 1) * ny, nz : 2 * nz] = low
        for f in range(4):
            out = lax.dot_general(
                columns[...], cut[f], (((1,), (1,)), ((), ())), preferred_element_type=F32
            )
            out = out[:half] + out[half:]
            block = f * (nx // 2) + n
            quarter = half // 4
            keep[block] = out[0:quarter]
            keep_more[block] = out[quarter : 2 * quarter]
            send[0, block] = out[2 * quarter : 3 * quarter]
            send[1, block] = out[3 * quarter :]
        return carry

    for n in range(batch):
        lax.fori_loop(n * each // 2, (n + 1) * each // 2, pair, 0)
        part = pl.ds(n * each, each)
        for ref, far in [(pressure.at[part], pressure_far.at[part])] + [
            (corrected.at[d, part], corrected_far.at[d, part]) for d in range(3)
        ]:
            store = pltpu.make_async_copy(ref, far, sems.at[len(loads) + len(stores)])
            store.start()
            stores.append(store)
    for store in stores:
        store.wait()


def tables(factor_y, factor_x, y_high, y_low, x_high, x_low, spread_high, spread_low):
    ny, rank = factor_y.shape
    nx = factor_x.shape[0]
    planes = y_high.shape[0] // ny
    nz = x_high.shape[1] // rank * planes
    count = y_high.shape[1] // nz
    ranks = rank // count
    wide = jnp.concatenate([factor_y[...], jnp.zeros((ny, nz - rank), F32)], axis=1)
    lane = lanes((ny, nz))
    for h in range(count):
        value = pltpu.roll(wide, (nz - h * ranks) % nz, 1)
        value = jnp.where(lane < ranks, value, 0.0)
        step = ranks
        while step < nz:
            value = value + pltpu.roll(value, step, 1)
            step *= 2
        for n in range(planes):
            high, low = split(jnp.where(lane // ranks == n, value, 0.0))
            y_high[n * ny : (n + 1) * ny, h * nz : (h + 1) * nz] = high
            y_low[n * ny : (n + 1) * ny, h * nz : (h + 1) * nz] = low
    width = x_high.shape[1]
    shape = (rank, width)
    copy = jnp.where(lanes(shape) // ranks == sublanes(shape), 1.0, 0.0).astype(BF16)
    for ref, value in zip((spread_high, spread_low), split(factor_x[...])):
        ref[...] = jnp.dot(value, copy, preferred_element_type=F32)
    shape = (ranks, width)
    here = lanes(shape) % ranks == sublanes(shape)

    def row(i, carry):
        at = pl.ds(pl.multiple_of(i * ranks, ranks), ranks)
        x_high[at, :] = jnp.where(here, spread_high[pl.ds(i, 1), :], 0.0).astype(BF16)
        x_low[at, :] = jnp.where(here, spread_low[pl.ds(i, 1), :], 0.0).astype(BF16)
        return carry

    lax.fori_loop(0, nx, row, 0)


def split(value):
    high = value.astype(BF16)
    return high, (value - high.astype(F32)).astype(BF16)


def split_table(value):
    high = lax.reduce_precision(value, exponent_bits=8, mantissa_bits=7)
    return high.astype(BF16), (value - high).astype(BF16)


def three(a, b, dims=(((1,), (0,)), ((), ()))):
    dot = functools.partial(lax.dot_general, dimension_numbers=dims, preferred_element_type=F32)
    (ah, al), (bh, bl) = a, b
    return dot(ah, bh) + (dot(al, bh) + dot(ah, bl))


def rank_y(kept, came, wide_high, wide_low, keep, keep_more, send):
    blocks, ranks, nz = kept.shape
    group = wide_high.shape[0] // nz
    parts = []
    for n in range(blocks // group):
        parts.append(
            jnp.concatenate(
                [kept[n * group + q] + came[n * group + q] for q in range(group)], axis=1
            )
        )
    x = jnp.concatenate(parts, axis=0)
    out = three(split(x), (wide_high[...], wide_low[...]))
    quarter = out.shape[1] // 4
    keep[...] = out[:, 0:quarter]
    keep_more[...] = out[:, quarter : 2 * quarter]
    send[0] = out[:, 2 * quarter : 3 * quarter]
    send[1] = out[:, 3 * quarter :]


def rank_x(ranks, kept, came, wide_high, wide_low, *outs):
    u = kept[...] + came[...]
    rows, nz = u.shape
    group = wide_high.shape[0] // nz
    parts = []
    for f in range(rows // ranks // group):
        parts.append(
            jnp.concatenate(
                [u[(f * group + q) * ranks : (f * group + q + 1) * ranks] for q in range(group)], axis=1
            )
        )
    x = jnp.concatenate(parts, axis=0)
    out = three(split(x), (wide_high[...], wide_low[...]))
    width = out.shape[1] // len(outs)
    for n, ref in enumerate(outs):
        ref[...] = out[:, n * width : (n + 1) * width]


def last_core(kept, came, core):
    ranks_x, fields, ranks_y, ranks_z = core.shape
    z = jnp.transpose(kept[...] + came[...])
    for f in range(fields):
        core[:, f] = z[:, f * ranks_z : (f + 1) * ranks_z].reshape(ranks_x, ranks_y, ranks_z)


def relative(factor, axis):
    count = lax.axis_size(axis)
    order = [0]
    step = 1
    while step < count:
        order = order + [n + step for n in order]
        step *= 2
    bits = count.bit_length() - 1
    order = [sum(((n >> b) & 1) << (bits - 1 - b) for b in range(bits)) for n in range(count)]
    blocks = factor.reshape(factor.shape[0], count, factor.shape[1] // count)
    here = lax.axis_index(axis)
    picked = [
        lax.dynamic_index_in_dim(blocks, jnp.bitwise_xor(here, n), axis=1, keepdims=False) for n in order
    ]
    return jnp.stack(picked, axis=1)


def swap(value, axis, mask):
    count = lax.axis_size(axis)
    return lax.ppermute(value, axis, [(i, i ^ mask) for i in range(count)])


def per_device(velocity, inv_density, factor_x, factor_y, factor_z):
    nx, ny, nz = inv_density.shape
    wide, rows = nx + 2 * LAYERS, ny + 2 * WIDE
    count_x, count_y, count_z = (lax.axis_size(axis) for axis in AXES)
    devices = count_x * count_y * count_z
    cells = (nx, ny, nz)
    rank = factor_x.shape[1]
    index = lax.axis_index("gx").reshape(1)

    shape = (((REACH + 1 + LAYERS + 1) * ny + 2 * REACH), nz)
    number = 1 if count_x == 2 else 2
    sent = call(
        pack_x,
        [shape] * number,
        [index, velocity, inv_density],
        scratch=[(number, 3, LAYERS, ny, nz), (number, LAYERS, ny, nz)],
        smem=1,
        far_in=(1, 2),
        sems=4 * number,
    )
    near = [swap(sent[0], "gx", 1)] if count_x == 2 else list(exchange(*sent, "gx"))
    rhs, = call(sources, [cells], [velocity], cost=(nx * ny * nz * 10, 4 * cost_of(cells)))
    shape = (wide // 2, ROWS, nz)
    up, down = call(pack_y, [shape, shape], [index, velocity, inv_density, rhs, *near], smem=1)
    before, after = exchange(up, down, "gy")
    parts = nz // SPAN
    groups = -(-wide // parts)
    message = (-(-groups // 2), rows, nz)
    whole = (groups * parts, rows, nz)
    strip = (groups, rows, nz)
    rhs_wide, inv_wide, up, down, strip_rhs, strip_inv = call(
        pack_z,
        [(wide, rows, nz)] * 2 + [message, message, strip, strip],
        [index, velocity, inv_density, rhs, *near, before, after],
        scratch=[whole] * 3 + [strip] * 2,
        smem=1,
        limit=18,
        far_out=(0, 1, 4, 5),
        sems=4,
    )
    before, after = exchange(up, down, "gz")
    span = (nx + 2, rows, nz)
    whole = (wide, rows, nz)
    *spans, sums = call(
        basis_main,
        [span] * (ITERS + 1) + [(len(PAIRS) + 1, WIDE, nz)],
        [rhs_wide, inv_wide],
        scratch=[whole] * (6 + ITERS),
        limit=22,
        cost=(wide * rows * nz * 100, 7 * cost_of(whole)),
        far_in=(0, 1),
        far_out=range(ITERS + 1),
        sems=ITERS + 3,
    )
    padded = (groups + 2, rows, nz)
    *strips, dots = call(
        functools.partial(basis_strips, nx),
        [strip] * ITERS + [(devices, WIDE, nz)],
        [strip_rhs, strip_inv, before, after, sums],
        scratch=[padded] * (6 + ITERS) + [strip] * 2,
        far_in=(0, 1),
        far_out=range(ITERS),
        sems=ITERS + 2,
    )
    dots = lax.all_to_all(dots, AXES, 0, 0, tiled=True)

    ranks_y, ranks_z = rank // count_y, rank // count_z
    planes = nz // ranks_y
    table_y, table_x = (planes * ny, count_y * nz), (nx * ranks_y, rank * ranks_y)
    y_high, y_low, x_high, x_low = pl.pallas_call(
        tables,
        out_shape=[jax.ShapeDtypeStruct(one, BF16) for one in (table_y, table_y, table_x, table_x)],
        in_specs=[VMEM] * 2,
        out_specs=[VMEM] * 4,
        scratch_shapes=[pltpu.VMEM((nx, rank * ranks_y), F32)] * 2,
        compiler_params=pltpu.CompilerParams(vmem_limit_bytes=16 * 2**20),
        cost_estimate=pl.CostEstimate(
            flops=4 * nx * ranks_y * rank * ranks_y, bytes_accessed=6 * 2**20, transcendentals=0
        ),
    )(relative(factor_y, "gy").reshape(ny, rank), relative(factor_x, "gx").reshape(nx, rank))
    columns = relative(factor_z, "gz")
    columns = jnp.transpose(columns.reshape(nz, -1))
    high, low = split_table(columns)
    columns = jnp.concatenate(
        [jnp.concatenate([high, high], axis=1), jnp.concatenate([low, low], axis=1)], axis=0
    )
    piece = (4 * nx // 2, ranks_z, nz)
    far = [*strips, *spans, velocity, inv_density]
    pressure, corrected, keep, keep_more, send = call(
        finish,
        [cells, (3,) + cells, piece, piece, (2,) + piece],
        [dots, columns, *far],
        scratch=[span, (nx + 2, ny, nz), strip, pltpu.VMEM((4, 2 * ny, 2 * nz), BF16), cells, (3,) + cells]
        + [one.shape for one in far],
        limit=32,
        far_in=range(2, 2 + len(far)),
        far_out=(0, 1),
        sems=len(far) + 16,
    )

    came = swap(send, "gz", 1)
    send = keep_more + came[1]
    keep = keep + came[0]
    came = swap(send, "gz", 2)

    shape = (4 * nx // planes * ranks_z, nz)
    keep, keep_more, send = call(
        rank_y, [shape] * 2 + [(2,) + shape], [keep, came, y_high, y_low], limit=16
    )
    came = swap(send, "gy", 1)
    send = keep_more + came[1]
    keep = keep + came[0]
    came = swap(send, "gy", 2)

    half = (4 * ranks_z, rank * ranks_y // 2)
    keep, send = call(
        functools.partial(rank_x, ranks_z), [half] * 2, [keep, came, x_high, x_low], limit=16
    )
    mask = 1
    while True:
        came = swap(send, "gx", mask)
        mask *= 2
        if mask >= count_x:
            break
        total = keep + came
        width = total.shape[1] // 2
        keep, send = total[:, :width], total[:, width:]
    core, = call(last_core, [(rank // count_x, 4, ranks_y, ranks_z)], [keep, came], limit=16)
    return pressure, corrected, core


def solution(mesh):
    placed = (
        P(None, "gx", "gy", "gz"),
        P("gx", "gy", "gz"),
        P("gx", None),
        P("gy", None),
        P("gz", None),
    )
    return jax.shard_map(
        per_device,
        mesh=mesh,
        in_specs=placed,
        out_specs=(P("gx", "gy", "gz"), P(None, "gx", "gy", "gz"), P("gx", None, "gy", "gz")),
        check_vma=False,
    )
```

```python
import functools
import math

import jax
import jax.numpy as jnp
from jax import lax
from jax.experimental import pallas as pl
from jax.experimental.pallas import tpu as pltpu
from jax.sharding import PartitionSpec as P

ITERS = 4
SHIFT = 0.1
AXES = ("gx", "gy", "gz")

REACH = ITERS
LAYERS = ITERS + 1
WIDE = 8
SLOT = 16
STRIP = 2 * LAYERS
SPAN = 32
ROWS = 24
NEWTON = (0.5, 0.5, 0.5)
PAIRS = [(a, b) for a in range(ITERS) for b in range(a, ITERS)]
VMEM = pl.BlockSpec(memory_space=pltpu.VMEM)
SMEM = pl.BlockSpec(memory_space=pltpu.SMEM)
HBM = pl.BlockSpec(memory_space=pltpu.HBM)
F32 = jnp.float32
BF16 = jnp.bfloat16


def call(body, outs, operands, scratch=(), smem=0, limit=12, cost=None, far_in=(), far_out=(), sems=0):
    scratch = [pltpu.VMEM(shape, F32) if isinstance(shape, tuple) else shape for shape in scratch]
    return pl.pallas_call(
        body,
        out_shape=[
            pltpu.HBM(shape, F32) if n in far_out else jax.ShapeDtypeStruct(shape, F32)
            for n, shape in enumerate(outs)
        ],
        in_specs=[SMEM if n < smem else HBM if n in far_in else VMEM for n in range(len(operands))],
        out_specs=[HBM if n in far_out else VMEM for n in range(len(outs))],
        scratch_shapes=scratch + ([pltpu.SemaphoreType.DMA((sems,))] if sems else []),
        compiler_params=pltpu.CompilerParams(vmem_limit_bytes=limit * 2**20),
        cost_estimate=cost
        and pl.CostEstimate(flops=cost[0], bytes_accessed=cost[1], transcendentals=0),
    )(
        *(
            pltpu.with_memory_space_constraint(one, pltpu.HBM) if n in far_in else one
            for n, one in enumerate(operands)
        )
    )


def cost_of(shape):
    return 4 * math.prod(shape)


def lanes(shape):
    return lax.broadcasted_iota(jnp.int32, shape, len(shape) - 1)


def sublanes(shape):
    return lax.broadcasted_iota(jnp.int32, shape, len(shape) - 2)


def exchange(up, down, axis):
    count = lax.axis_size(axis)
    ends = count - 1
    below = lax.ppermute(up, axis, [(i, i + 1) for i in range(ends)])
    above = lax.ppermute(down, axis, [(i + 1, i) for i in range(ends)])
    return below, above


def source(velocity, x, nx):
    ny, nz = velocity.shape[2:]
    shape = (ny, nz)
    before = jnp.where(x == 0, 0.0, velocity[0, jnp.maximum(x - 1, 0)])
    after = jnp.where(x == nx - 1, 0.0, velocity[0, jnp.minimum(x + 1, nx - 1)])
    along_y = velocity[1, x]
    along_z = velocity[2, x]
    total = after - before
    total = total + jnp.where(sublanes(shape) == ny - 1, 0.0, pltpu.roll(along_y, ny - 1, 0))
    total = total - jnp.where(sublanes(shape) == 0, 0.0, pltpu.roll(along_y, 1, 0))
    total = total + jnp.where(lanes(shape) == nz - 1, 0.0, pltpu.roll(along_z, nz - 1, 1))
    total = total - jnp.where(lanes(shape) == 0, 0.0, pltpu.roll(along_z, 1, 1))
    return -0.5 * total


def sources(velocity, rhs):
    nx = rhs.shape[0]

    def plane(x, carry):
        rhs[x] = source(velocity, x, nx)
        return carry

    lax.fori_loop(0, nx, plane, 0, unroll=4)


def pack_x(index, velocity_far, inv_far, *refs):
    velocity, inv, sems = refs[-3:]
    messages = refs[:-3]
    layers, ny, nz = inv.shape[1:]
    far = inv_far.shape[0] - layers
    shape = (ny, nz)
    only = len(messages) == 1
    first = index[0] == 0

    def copies(n):
        start = jnp.where(first, far, 0) if only else (far, 0)[n]
        part = pl.ds(start, layers)
        yield pltpu.make_async_copy(inv_far.at[part], inv.at[n], sems.at[4 * n])
        for d in range(3):
            yield pltpu.make_async_copy(velocity_far.at[d, part], velocity.at[n, d], sems.at[4 * n + d + 1])

    for n in range(len(messages)):
        for copy in copies(n):
            copy.start()

    def fill(n, start, own, sign):
        message, near = messages[n], velocity.at[n]
        for k in range(REACH):
            message[k * ny : (k + 1) * ny, :] = source(near, start + k, layers)
        base = REACH * ny
        message[base : base + ny, :] = sign * near[0, own]
        base += ny
        for k in range(LAYERS):
            message[base : base + ny, :] = inv[n, k]
            base += ny
        ends = jnp.zeros(shape, F32)
        for k in range(REACH):
            plane_z = near[2, start + k]
            ends = jnp.where(lanes(shape) == 2 * k, plane_z[:, 0:1], ends)
            ends = jnp.where(lanes(shape) == 2 * k + 1, plane_z[:, nz - 1 : nz], ends)
        message[base : base + ny, :] = ends
        base += ny
        for k in range(REACH):
            message[base + 2 * k : base + 2 * k + 1, :] = near[1, start + k, 0:1, :]
            message[base + 2 * k + 1 : base + 2 * k + 2, :] = near[1, start + k, ny - 1 : ny, :]

    for n in range(len(messages)):
        for copy in copies(n):
            copy.wait()
    upper = (1, layers - 1, 0.5)
    lower = (0, 0, -0.5)
    if only:
        fill(0, *(jnp.where(first, one, two) for one, two in zip(upper, lower)))
    else:
        fill(0, *upper)
        fill(1, *lower)


class Scaled:
    def __init__(self, ref, factor):
        self.ref, self.factor = ref, factor

    def __getitem__(self, where):
        return self.ref[where] * self.factor


def sides_x(index, messages):
    if len(messages) == 2:
        return messages
    first = jnp.where(index[0] == 0, 1.0, 0.0)
    return Scaled(messages[0], 1.0 - first), Scaled(messages[0], first)


def pack_y(index, velocity, inv, rhs, *refs):
    (below, above), (up, down) = sides_x(index, refs[:-2]), refs[-2:]
    nx, ny, nz = inv.shape
    each = REACH + 1 + LAYERS + 1

    def put(pair, parity, rows_rhs, ghost, rows_inv, first, last):
        offset = parity * each
        for message, part in ((up, 1), (down, 0)):
            message[pair, pl.ds(offset, REACH), :] = rows_rhs[part]
            message[pair, pl.ds(offset + REACH, 1), :] = (0.5 if part else -0.5) * ghost[part]
            message[pair, pl.ds(offset + REACH + 1, LAYERS), :] = rows_inv[part]
            ends = jnp.zeros((1, nz), F32)
            for k in range(REACH):
                ends = jnp.where(lanes((1, nz)) == 2 * k, first[part][k : k + 1], ends)
                ends = jnp.where(lanes((1, nz)) == 2 * k + 1, last[part][k : k + 1], ends)
            message[pair, pl.ds(offset + each - 1, 1), :] = ends

    def halo(x, message, k_rhs, k_inv, extra):
        base = (REACH + 1 + k_inv) * ny
        rows_inv = (message[pl.ds(base, LAYERS), :], message[pl.ds(base + ny - LAYERS, LAYERS), :])
        zero_row = jnp.zeros((1, nz), F32)
        zero = jnp.zeros((REACH, nz), F32)
        if k_rhs is None:
            column = jnp.zeros((REACH, 1), F32)
            put(x // 2, x % 2, (zero, zero), (zero_row, zero_row), rows_inv, (column, column), (column, column))
            return
        low, high = message[pl.ds(k_rhs * ny, REACH), :], message[pl.ds((k_rhs + 1) * ny - REACH, REACH), :]
        if extra is not None:
            sign, source = extra
            low = low + sign * velocity[0, source, 0:REACH, :]
            high = high + sign * velocity[0, source, ny - REACH : ny, :]
        ends = (REACH + 1 + LAYERS) * ny
        lines = ends + ny + 2 * k_rhs
        ghost = (message[pl.ds(lines, 1), :], message[pl.ds(lines + 1, 1), :])
        head, tail = message[pl.ds(ends, REACH), :], message[pl.ds(ends + ny - REACH, REACH), :]
        first = (head[:, 2 * k_rhs : 2 * k_rhs + 1], tail[:, 2 * k_rhs : 2 * k_rhs + 1])
        last = (head[:, 2 * k_rhs + 1 : 2 * k_rhs + 2], tail[:, 2 * k_rhs + 1 : 2 * k_rhs + 2])
        put(x // 2, x % 2, (low, high), ghost, rows_inv, first, last)

    for k in range(LAYERS):
        halo(k, below, k - 1 if k else None, k, (-0.5, 0) if k == LAYERS - 1 else None)
        halo(
            nx + LAYERS + k,
            above,
            k if k < REACH else None,
            k,
            (0.5, nx - 1) if k == 0 else None,
        )

    def own(x, pair, parity, extra):
        low, high = rhs[x, 0:REACH, :], rhs[x, ny - REACH : ny, :]
        if extra is not None:
            low = low + extra[pl.ds(REACH * ny, REACH), :]
            high = high + extra[pl.ds((REACH + 1) * ny - REACH, REACH), :]
        ghost = (velocity[1, x, 0:1, :], velocity[1, x, ny - 1 : ny, :])
        rows_inv = (inv[x, 0:LAYERS, :], inv[x, ny - LAYERS : ny, :])
        head, tail = velocity[2, x, 0:REACH, :], velocity[2, x, ny - REACH : ny, :]
        first = (head[:, 0:1], tail[:, 0:1])
        last = (head[:, nz - 1 : nz], tail[:, nz - 1 : nz])
        put(pair, parity, (low, high), ghost, rows_inv, first, last)

    def at(x, extra):
        own(x, (x + LAYERS) // 2, (x + LAYERS) % 2, extra)

    at(0, below)
    at(nx - 1, above)
    begin = 1 + (1 + LAYERS) % 2
    finish = begin + (nx - 1 - begin) // 2 * 2
    for x in (*range(1, begin), *range(finish, nx - 1)):
        at(x, None)

    def planes(n, carry):
        for parity in range(2):
            own(begin + 2 * n + parity, (begin + LAYERS) // 2 + n, parity, None)
        return carry

    lax.fori_loop(0, (finish - begin) // 2, planes, 0, unroll=3)


def pack_z(index, velocity, inv, rhs, *refs):
    (below, above), before, after = sides_x(index, refs[:-14]), refs[-14], refs[-13]
    rhs_far, inv_far, up, down, strip_rhs_far, strip_inv_far = refs[-12:-6]
    rhs_wide, inv_wide, ends, strip_rhs, strip_inv, sems = refs[-6:]
    nx, ny, nz = inv.shape
    wide = nx + 2 * LAYERS
    rows = ny + 2 * WIDE
    each = REACH + 1 + LAYERS + 1
    mine = pl.ds(WIDE, ny)
    edge = (WIDE, nz)
    groups = strip_rhs.shape[0]

    for k in range(LAYERS):
        for message, x, layer in ((below, k, k - 1), (above, nx + LAYERS + k, k if k < REACH else -1)):
            base = (REACH + 1 + k) * ny
            inv_wide[x, mine, :] = message[pl.ds(base, ny), :]
            if layer < 0:
                rhs_wide[x, mine, :] = jnp.zeros((ny, nz), F32)
                ends[x, mine, :] = jnp.zeros((ny, nz), F32)
                continue
            part = message[pl.ds(layer * ny, ny), :]
            if x == LAYERS - 1:
                part = part - 0.5 * velocity[0, 0]
            if x == nx + LAYERS:
                part = part + 0.5 * velocity[0, nx - 1]
            rhs_wide[x, mine, :] = part
            line = message[pl.ds((REACH + 1 + LAYERS) * ny, ny), :]
            ends[x, mine, :] = jnp.where(
                lanes((ny, nz)) == 0, line[:, 2 * layer : 2 * layer + 1], line[:, 2 * layer + 1 : 2 * layer + 2]
            )

    def plane(x, carry):
        inv_wide[x + LAYERS, mine, :] = inv[x]
        rhs_wide[x + LAYERS, mine, :] = rhs[x]
        ends[x + LAYERS, mine, :] = velocity[2, x]
        return carry

    lax.fori_loop(0, nx, plane, 0, unroll=4)
    rhs_wide[LAYERS, mine, :] += below[pl.ds(REACH * ny, ny), :]
    rhs_wide[LAYERS + nx - 1, mine, :] += above[pl.ds(REACH * ny, ny), :]
    for ref in (rhs_wide, inv_wide, ends):
        for x in range(wide, ref.shape[0]):
            ref[x] = jnp.zeros((rows, nz), F32)

    def finish(x, ghost_low, ghost_high):
        low, high = before[x // 2], after[x // 2]
        low = jnp.where(x % 2 == 0, low, pltpu.roll(low, ROWS - each, 0))[0:SLOT]
        high = jnp.where(x % 2 == 0, high, pltpu.roll(high, ROWS - each, 0))[0:SLOT]
        part = pltpu.roll(low, WIDE - REACH, 0)[0:WIDE]
        part = jnp.where(sublanes(edge) >= WIDE - REACH, part, 0.0)
        part = part - jnp.where(sublanes(edge) == WIDE - 1, 0.5 * ghost_low, 0.0)
        rhs_wide[x, 0:WIDE, :] = part
        part = pltpu.roll(low, SLOT - (REACH + 1) + WIDE - LAYERS, 0)[0:WIDE]
        inv_wide[x, 0:WIDE, :] = jnp.where(sublanes(edge) >= WIDE - LAYERS, part, 0.0)
        part = jnp.where(sublanes(edge) < REACH, high[0:WIDE], 0.0)
        part = part + jnp.where(sublanes(edge) == 0, 0.5 * ghost_high, 0.0)
        rhs_wide[x, WIDE + ny : rows, :] = part
        part = pltpu.roll(high, SLOT - (REACH + 1), 0)[0:WIDE]
        inv_wide[x, WIDE + ny : rows, :] = jnp.where(sublanes(edge) < LAYERS, part, 0.0)
        head = rhs_wide[x, WIDE : 2 * WIDE, :]
        rhs_wide[x, WIDE : 2 * WIDE, :] = head + jnp.where(sublanes(edge) == 0, low[REACH : REACH + 1], 0.0)
        tail = rhs_wide[x, ny : WIDE + ny, :]
        rhs_wide[x, ny : WIDE + ny, :] = tail + jnp.where(
            sublanes(edge) == WIDE - 1, high[REACH : REACH + 1], 0.0
        )
        for message, start, place in ((low, WIDE - REACH, 0), (high, 0, WIDE + ny)):
            line = message[each - 1 : each]
            one = jnp.zeros(edge, F32)
            two = jnp.zeros(edge, F32)
            for k in range(REACH):
                here = sublanes(edge) == start + k
                one = jnp.where(here, line[:, 2 * k : 2 * k + 1], one)
                two = jnp.where(here, line[:, 2 * k + 1 : 2 * k + 2], two)
            ends[x, place : place + WIDE, :] = jnp.where(lanes(edge) == 0, one, two)

    for k in range(LAYERS):
        for message, x, layer in ((below, k, k - 1), (above, nx + LAYERS + k, k if k < REACH else -1)):
            lines = (REACH + 1 + LAYERS + 1) * ny + 2 * layer
            if layer < 0:
                zero = jnp.zeros((1, nz), F32)
                finish(x, zero, zero)
            else:
                finish(x, message[pl.ds(lines, 1), :], message[pl.ds(lines + 1, 1), :])

    def middle(x, carry):
        finish(x + LAYERS, velocity[1, x, 0:1, :], velocity[1, x, ny - 1 : ny, :])
        return carry

    lax.fori_loop(0, nx, middle, 0, unroll=4)
    copies = [
        pltpu.make_async_copy(ref.at[pl.ds(0, wide)], far, sems.at[n])
        for n, (ref, far) in enumerate(((rhs_wide, rhs_far), (inv_wide, inv_far)))
    ]
    for copy in copies:
        copy.start()

    whole = (rows, nz)
    lane = lanes(whole)
    place = lane % SPAN

    def back(value, step):
        return pltpu.roll(value, nz - step, 1)

    def gather(ref, g):
        value = None
        for n in range(nz // SPAN):
            moved = pltpu.roll(ref[g + n * groups], n * SPAN + STRIP, 1)
            value = moved if value is None else jnp.where(lane >= n * SPAN, moved, value)
        return value

    def pack(g):
        r, i, e = gather(rhs_wide, g), gather(inv_wide, g), gather(ends, g)
        apart = SPAN - 2 * STRIP
        for ref, value in ((strip_rhs, r), (strip_inv, i)):
            out = jnp.where(place < STRIP, value, 0.0)
            ref[g] = jnp.where(place >= SPAN - STRIP, pltpu.roll(value, apart, 1), out)
        ghost = jnp.where(place == STRIP, 0.5 * pltpu.roll(e, 1, 1), 0.0)
        ghost = jnp.where(place == SPAN - STRIP - 1, -0.5 * pltpu.roll(e, apart - 1, 1), ghost)
        strip_rhs[g] += ghost
        out = jnp.where(place < REACH, back(r, STRIP - REACH), 0.0)
        out = jnp.where(place == REACH, 0.5 * back(e, STRIP - 1 - REACH), out)
        here = (place > REACH) & (place <= REACH + LAYERS)
        higher = jnp.where(here, pltpu.roll(i, (nz + REACH + 1 + LAYERS - STRIP) % nz, 1), out)
        out = jnp.where(place < REACH, back(r, STRIP), 0.0)
        out = jnp.where(place == REACH, -0.5 * back(e, STRIP - REACH), out)
        return higher, jnp.where(here, back(i, STRIP - REACH - 1), out)

    halves = up.shape[0]

    def both(n, carry):
        one, two = pack(n)
        up[n] = one
        down[n] = two
        return carry

    lax.fori_loop(0, halves, both, 0, unroll=2)

    def more(n, carry):
        one, two = pack(n + halves)
        up[n] += pltpu.roll(one, SPAN // 2, 1)
        down[n] += pltpu.roll(two, SPAN // 2, 1)
        return carry

    lax.fori_loop(0, groups - halves, more, 0, unroll=2)
    for ref, far in ((strip_rhs, strip_rhs_far), (strip_inv, strip_inv_far)):
        copies.append(pltpu.make_async_copy(ref, far, sems.at[len(copies)]))
        copies[-1].start()
    for copy in copies:
        copy.wait()


def shifted(ref, x, t, step):
    rows = ref.shape[1]
    start = t * WIDE + step
    if start < 0:
        return pltpu.roll(ref[x, 0:WIDE, :], 1, 0)
    if start + WIDE > rows:
        return pltpu.roll(ref[x, rows - WIDE : rows, :], WIDE - 1, 0)
    return ref[x, start : start + WIDE, :]


class Stencil:
    def __init__(self, inv, root, ax, ay, az, vs, planes, edges=None):
        self.inv, self.root, self.ax, self.ay, self.az, self.vs = inv, root, ax, ay, az, vs
        self.planes, self.edges = planes, edges or (lambda ref: None)
        self.count, self.rows, self.nz = inv.shape
        self.tiles = self.rows // WIDE

    def here(self, t):
        return slice(t * WIDE, (t + 1) * WIDE)

    def right(self, value):
        return pltpu.roll(value, self.nz - 1, 1)

    def left(self, value):
        return pltpu.roll(value, 1, 1)

    def prepare(self, rhs):
        inv, root = self.inv, self.root
        self.edges(inv)

        def scales(x, carry):
            writes = []
            for t in range(self.tiles):
                here = self.here(t)
                c = inv[x, here, :]
                total = (inv[x + 1, here, :] + inv[x - 1, here, :]) + (self.right(c) + self.left(c))
                total = total + (shifted(inv, x, t, 1) + shifted(inv, x, t, -1))
                value = jnp.where(c > 0.0, lax.rsqrt(SHIFT + 0.5 * (6.0 * c + total)), 0.0)
                writes.append((here, value, rhs[x, here, :] * value))
            for here, one, two in writes:
                root[x, here, :] = one
                self.vs[0][x, here, :] = two
            return carry

        lax.fori_loop(1, self.count - 1, scales, 0, unroll=4)
        zero = jnp.zeros((self.rows, self.nz), F32)
        for ref in (root, self.vs[0]):
            ref[0] = zero
            ref[self.count - 1] = zero
            self.edges(ref)

        def couplings(x, carry):
            writes = []
            for t in range(self.tiles):
                here = self.here(t)
                c, d = inv[x, here, :], root[x, here, :]
                half = 0.5 * d
                writes.append(
                    (
                        here,
                        (c + inv[x + 1, here, :]) * (half * root[x + 1, here, :]),
                        (c + shifted(inv, x, t, 1)) * (half * shifted(root, x, t, 1)),
                        (c + self.right(c)) * (half * self.right(d)),
                    )
                )
            for here, x_face, y_face, z_face in writes:
                self.ax[x, here, :] = x_face
                self.ay[x, here, :] = y_face
                self.az[x, here, :] = z_face
            return carry

        lax.fori_loop(1, self.count - 1, couplings, 0, unroll=4)
        self.ax[0] = zero
        self.edges(self.ax)

    def couple(self, k, x, t):
        here = self.here(t)
        v, ax, ay = self.vs[k], self.ax, self.ay
        c, f = v[x, here, :], self.az[x, here, :]
        total = ax[x, here, :] * v[x + 1, here, :] + ax[x - 1, here, :] * v[x - 1, here, :]
        total = total + (f * self.right(c) + self.left(f * c))
        total = total + ay[x, here, :] * shifted(v, x, t, 1)
        return c, total + shifted(ay, x, t, -1) * shifted(v, x, t, -1)

    def extend(self, k):
        scale = 1.0 - NEWTON[k]

        def step(x, carry):
            writes = []
            for t in range(self.tiles):
                c, total = self.couple(k, x, t)
                writes.append((t, scale * c - total if scale else -total))
            for t, value in writes:
                self.vs[k + 1][x, self.here(t), :] = value
            return carry

        start, stop = self.planes(k)
        lax.fori_loop(start, stop, step, 0, unroll=4)
        self.edges(self.vs[k + 1])

    def products(self, start, stop, mask):
        def measure(x, sums):
            sums = list(sums)
            for t in range(1, self.tiles - 1):
                keep = mask(x)
                v = [self.vs[k][x, self.here(t), :] for k in range(ITERS)]
                own, total = self.couple(ITERS - 1, x, t)
                kept = [jnp.where(keep, one, 0.0) for one in v]
                for n, (a, b) in enumerate(PAIRS):
                    sums[n] = sums[n] + v[a] * kept[b]
                sums[-1] = sums[-1] + kept[-1] * (own - total)
            return tuple(sums)

        zero = jnp.zeros((WIDE, self.nz), F32)
        return lax.fori_loop(start, stop, measure, (zero,) * (len(PAIRS) + 1), unroll=2)


def basis_main(far_rhs, far_inv, *refs):
    outs, sums = refs[: ITERS + 1], refs[ITERS + 1]
    rhs, inv, root, ax, ay, az = refs[ITERS + 2 : ITERS + 8]
    vs, sems = refs[ITERS + 8 : -1], refs[-1]
    wide, rows, nz = ax.shape
    nx = wide - 2 * LAYERS
    loads = [
        pltpu.make_async_copy(far, ref, sems.at[n]) for n, (far, ref) in enumerate(((far_rhs, rhs), (far_inv, inv)))
    ]
    for load in loads:
        load.start()
    for load in loads:
        load.wait()
    stencil = Stencil(inv, root, ax, ay, az, vs, lambda k: (2 + k, wide - 2 - k))
    copies = []

    def send(n, ref):
        copy = pltpu.make_async_copy(ref.at[pl.ds(LAYERS - 1, nx + 2)], outs[n], sems.at[2 + n])
        copy.start()
        copies.append(copy)

    stencil.prepare(rhs)
    send(ITERS, root)
    send(0, vs[0])
    for k in range(ITERS - 1):
        stencil.extend(k)
        send(k + 1, vs[k + 1])
    lane = lanes((WIDE, nz))
    inner = (lane > REACH) & (lane < nz - 1 - REACH)
    for n, one in enumerate(stencil.products(LAYERS, LAYERS + nx, lambda x: inner)):
        sums[n] = one
    for copy in copies:
        copy.wait()


def basis_strips(nx, rhs_far, inv_far, before, after, sums, *refs):
    outs, dots = refs[:ITERS], refs[ITERS]
    rhs, inv, root, ax, ay, az = refs[ITERS + 1 : ITERS + 7]
    vs, strip_rhs, strip_inv, sems = refs[ITERS + 7 : -3], *refs[-3:]
    groups, rows, nz = strip_inv.shape
    loads = [
        pltpu.make_async_copy(far, ref, sems.at[ITERS + n])
        for n, (far, ref) in enumerate(((rhs_far, strip_rhs), (inv_far, strip_inv)))
    ]
    for load in loads:
        load.start()
    for load in loads:
        load.wait()
    halves = before.shape[0]
    whole = (rows, nz)
    place = lanes(whole) % SPAN

    def edges(ref):
        ref[0] = pltpu.roll(ref[groups], SPAN, 1)
        ref[groups + 1] = pltpu.roll(ref[1], nz - SPAN, 1)

    def receive(g, low, high):
        start = SPAN - STRIP - LAYERS
        moved = pltpu.roll(low, start + 1, 1)
        r = strip_rhs[g] + jnp.where((place > start) & (place <= SPAN - STRIP), moved, 0.0)
        moved = pltpu.roll(low, start - REACH - 1, 1)
        i = strip_inv[g] + jnp.where((place >= start) & (place < SPAN - STRIP), moved, 0.0)
        moved = pltpu.roll(high, STRIP, 1)
        r = r + jnp.where((place >= STRIP) & (place < STRIP + REACH), moved, 0.0)
        moved = pltpu.roll(high, STRIP - REACH - 1, 1)
        r = r + jnp.where(place == STRIP - 1, moved, 0.0)
        i = i + jnp.where((place >= STRIP) & (place < STRIP + LAYERS), moved, 0.0)
        rhs[g + 1] = r
        inv[g + 1] = i

    def first(n, carry):
        receive(n, before[n], after[n])
        return carry

    def second(n, carry):
        half = nz - SPAN // 2
        receive(n + halves, pltpu.roll(before[n], half, 1), pltpu.roll(after[n], half, 1))
        return carry

    lax.fori_loop(0, halves, first, 0, unroll=3)
    lax.fori_loop(0, groups - halves, second, 0, unroll=3)
    stencil = Stencil(inv, root, ax, ay, az, vs, lambda k: (1, groups + 1), edges)
    stencil.prepare(rhs)
    for k in range(ITERS - 1):
        stencil.extend(k)
    lane = lanes((WIDE, nz))
    part = lane // SPAN
    spot = lane % SPAN
    ends = ((spot >= STRIP - LAYERS) & (spot < STRIP)) | (
        (spot >= SPAN - STRIP) & (spot < SPAN - STRIP + LAYERS)
    )

    def mask(x):
        plane = x - 1 + part * groups
        return ends & (plane >= LAYERS) & (plane < LAYERS + nx)

    totals = []
    for n, one in enumerate(stencil.products(1, groups + 1, mask)):
        line = jnp.sum(one + sums[n], axis=0, keepdims=True)
        totals.append(line + pltpu.roll(line, nz // 2, 1))
    row = sublanes((WIDE, nz))
    message = jnp.zeros((WIDE, nz), F32)
    for n, line in enumerate(totals):
        half = lane < nz // 2 if n < WIDE else lane >= nz // 2
        message = jnp.where((row == n % WIDE) & half, line, message)

    def send(n, carry):
        dots[n] = message
        return carry

    lax.fori_loop(0, dots.shape[0], send, 0, unroll=8)

    def result(g, carry):
        for k in range(ITERS):
            vs[k][g] = vs[k][g] * root[g]
        return carry

    lax.fori_loop(1, groups + 1, result, 0, unroll=4)
    copies = [pltpu.make_async_copy(vs[k].at[pl.ds(1, groups)], outs[k], sems.at[k]) for k in range(ITERS)]
    for copy in copies:
        copy.start()
    for copy in copies:
        copy.wait()


def coefficients(dots):
    half = lanes(dots.shape) < dots.shape[1] // 2
    one = jnp.sum(jnp.where(half, dots, 0.0), axis=1, keepdims=True)
    two = jnp.sum(jnp.where(half, 0.0, dots), axis=1, keepdims=True)

    def entry(n):
        return one[n : n + 1] if n < WIDE else two[n - WIDE : n - WIDE + 1]

    gram = {}
    for n, (a, b) in enumerate(PAIRS):
        gram[a, b] = gram[b, a] = entry(n)
    last = ITERS - 1
    image = {}
    for b in range(last):
        for a in range(ITERS):
            image[a, b] = gram[a, b + 1]
            if NEWTON[b]:
                image[a, b] = image[a, b] + NEWTON[b] * gram[a, b]
    for a in range(last):
        image[a, last] = image[last, a]
    image[last, last] = entry(len(PAIRS))

    def product(table, one, two):
        total = None
        for a, left in enumerate(one):
            for b, right in enumerate(two):
                term = left * right * table[a, b]
                total = term if total is None else total + term
        return total

    unit = jnp.ones((1, 1), F32)
    pressure = []
    precond = [unit]
    direction = [unit]
    rz = gram[0, 0]
    for iteration in range(ITERS):
        alpha = rz / product(image, direction, direction)
        pressure = [
            (pressure[n] if n < len(pressure) else 0.0) + alpha * one for n, one in enumerate(direction)
        ]
        if iteration == last:
            break
        moved = []
        for n in range(len(direction) + 1):
            value = None
            if n < len(direction) and NEWTON[n]:
                value = NEWTON[n] * direction[n]
            if n > 0:
                value = direction[n - 1] if value is None else value + direction[n - 1]
            moved.append(value)
        fresh_precond = []
        for n, one in enumerate(moved):
            old = precond[n] if n < len(precond) else None
            if one is None:
                fresh_precond.append(old)
            else:
                fresh_precond.append(-alpha * one if old is None else old - alpha * one)
        precond = fresh_precond
        fresh = product(gram, precond, precond)
        beta = fresh / rz
        direction = [
            one + beta * direction[n] if n < len(direction) else one for n, one in enumerate(precond)
        ]
        rz = fresh
    return pressure


def finish(dots, columns, *refs):
    inputs = 2 * ITERS + 3
    pressure_far, corrected_far, keep, keep_more, send, p, gaps, mixed, cut, pressure, corrected = refs[inputs : inputs + 11]
    held, sems = refs[inputs + 11 : -1], refs[-1]
    loads = [pltpu.make_async_copy(far, ref, sems.at[n]) for n, (far, ref) in enumerate(zip(refs, held))]
    for load in loads:
        load.start()
    strips, spans, roots = held[:ITERS], held[ITERS : 2 * ITERS], held[2 * ITERS]
    velocity, inv = held[2 * ITERS + 1 :]
    nx, ny, nz = inv.shape
    shape = (ny, nz)
    groups = mixed.shape[0]
    total = dots[0]
    for n in range(1, dots.shape[0]):
        total = total + dots[n]
    weights = coefficients(total)

    def strip(g, carry):
        value = weights[0] * strips[0][g]
        for k in range(1, ITERS):
            value = value + weights[k] * strips[k][g]
        mixed[g] = value
        return carry

    for load in loads[:ITERS]:
        load.wait()
    lax.fori_loop(0, groups, strip, 0, unroll=4)
    for load in loads[ITERS : 2 * ITERS + 1]:
        load.wait()
    mine = slice(WIDE, WIDE + ny)
    lane = lanes(spans[0].shape[1:])

    def combine(x, carry):
        value = weights[0] * spans[0][x]
        for k in range(1, ITERS):
            value = value + weights[k] * spans[k][x]
        value = value * roots[x]
        plane = x + LAYERS - 1
        ends = mixed[plane % groups]
        start = plane // groups * SPAN
        last = pltpu.roll(ends, lax.rem(2 * nz - STRIP - start, nz), 1)
        first = pltpu.roll(ends, lax.rem(nz + STRIP - SPAN - start + nz, nz), 1)
        value = jnp.where(lane < LAYERS, first, jnp.where(lane >= nz - LAYERS, last, value))
        p[x] = value
        after = pltpu.roll(jnp.where(lane == 0, last, value), nz - 1, 1)
        before = pltpu.roll(jnp.where(lane == nz - 1, first, value), 1, 1)
        gaps[x] = (after - before)[mine]
        return carry

    lax.fori_loop(0, nx + 2, combine, 0, unroll=4)
    half = columns.shape[0] // 2
    for load in loads[2 * ITERS + 1 :]:
        load.wait()
    batch = 4
    each = nx // batch
    stores = []

    def pair(n, carry):
        for which in range(2):
            x = 2 * n + which
            centre = p[x + 1, mine, :]
            pressure[x] = centre
            half_inv = 0.5 * inv[x]
            slopes = (
                p[x + 2, mine, :] - p[x, mine, :],
                p[x + 1, WIDE + 1 : WIDE + 1 + ny, :] - p[x + 1, WIDE - 1 : WIDE - 1 + ny, :],
                gaps[x + 1],
            )
            fields = [velocity[d, x] - half_inv * slopes[d] for d in range(3)] + [centre]
            for d in range(3):
                corrected[d, x] = fields[d]
            for f, field in enumerate(fields):
                high = field.astype(BF16)
                low = (field - high.astype(F32)).astype(BF16)
                cut[f, which * ny : (which + 1) * ny, 0:nz] = high
                cut[f, which * ny : (which + 1) * ny, nz : 2 * nz] = low
        for f in range(4):
            out = lax.dot_general(
                columns[...], cut[f], (((1,), (1,)), ((), ())), preferred_element_type=F32
            )
            out = out[:half] + out[half:]
            block = f * (nx // 2) + n
            quarter = half // 4
            keep[block] = out[0:quarter]
            keep_more[block] = out[quarter : 2 * quarter]
            send[0, block] = out[2 * quarter : 3 * quarter]
            send[1, block] = out[3 * quarter :]
        return carry

    for n in range(batch):
        lax.fori_loop(n * each // 2, (n + 1) * each // 2, pair, 0, unroll=2)
        part = pl.ds(n * each, each)
        for ref, far in [(pressure.at[part], pressure_far.at[part])] + [
            (corrected.at[d, part], corrected_far.at[d, part]) for d in range(3)
        ]:
            store = pltpu.make_async_copy(ref, far, sems.at[len(loads) + len(stores)])
            store.start()
            stores.append(store)
    for store in stores:
        store.wait()


def tables(factor_y, factor_x, y_high, y_low, x_high, x_low, spread_high, spread_low):
    ny, rank = factor_y.shape
    nx = factor_x.shape[0]
    planes = y_high.shape[0] // ny
    nz = x_high.shape[1] // rank * planes
    count = y_high.shape[1] // nz
    ranks = rank // count
    wide = jnp.concatenate([factor_y[...], jnp.zeros((ny, nz - rank), F32)], axis=1)
    lane = lanes((ny, nz))
    for h in range(count):
        value = pltpu.roll(wide, (nz - h * ranks) % nz, 1)
        value = jnp.where(lane < ranks, value, 0.0)
        step = ranks
        while step < nz:
            value = value + pltpu.roll(value, step, 1)
            step *= 2
        for n in range(planes):
            high, low = split(jnp.where(lane // ranks == n, value, 0.0))
            y_high[n * ny : (n + 1) * ny, h * nz : (h + 1) * nz] = high
            y_low[n * ny : (n + 1) * ny, h * nz : (h + 1) * nz] = low
    width = x_high.shape[1]
    shape = (rank, width)
    copy = jnp.where(lanes(shape) // ranks == sublanes(shape), 1.0, 0.0).astype(BF16)
    for ref, value in zip((spread_high, spread_low), split(factor_x[...])):
        ref[...] = jnp.dot(value, copy, preferred_element_type=F32)
    shape = (ranks, width)
    here = lanes(shape) % ranks == sublanes(shape)

    def row(i, carry):
        at = pl.ds(pl.multiple_of(i * ranks, ranks), ranks)
        x_high[at, :] = jnp.where(here, spread_high[pl.ds(i, 1), :], 0.0).astype(BF16)
        x_low[at, :] = jnp.where(here, spread_low[pl.ds(i, 1), :], 0.0).astype(BF16)
        return carry

    lax.fori_loop(0, nx, row, 0, unroll=4)


def split(value):
    high = value.astype(BF16)
    return high, (value - high.astype(F32)).astype(BF16)


def split_table(value):
    high = lax.reduce_precision(value, exponent_bits=8, mantissa_bits=7)
    return high.astype(BF16), (value - high).astype(BF16)


def three(a, b, dims=(((1,), (0,)), ((), ()))):
    dot = functools.partial(lax.dot_general, dimension_numbers=dims, preferred_element_type=F32)
    (ah, al), (bh, bl) = a, b
    return dot(ah, bh) + (dot(al, bh) + dot(ah, bl))


def rank_y(kept, came, wide_high, wide_low, keep, keep_more, send):
    blocks, ranks, nz = kept.shape
    group = wide_high.shape[0] // nz
    parts = []
    for n in range(blocks // group):
        parts.append(
            jnp.concatenate(
                [kept[n * group + q] + came[n * group + q] for q in range(group)], axis=1
            )
        )
    x = jnp.concatenate(parts, axis=0)
    out = three(split(x), (wide_high[...], wide_low[...]))
    quarter = out.shape[1] // 4
    keep[...] = out[:, 0:quarter]
    keep_more[...] = out[:, quarter : 2 * quarter]
    send[0] = out[:, 2 * quarter : 3 * quarter]
    send[1] = out[:, 3 * quarter :]


def rank_x(ranks, kept, came, wide_high, wide_low, *outs):
    u = kept[...] + came[...]
    rows, nz = u.shape
    group = wide_high.shape[0] // nz
    parts = []
    for f in range(rows // ranks // group):
        parts.append(
            jnp.concatenate(
                [u[(f * group + q) * ranks : (f * group + q + 1) * ranks] for q in range(group)], axis=1
            )
        )
    x = jnp.concatenate(parts, axis=0)
    out = three(split(x), (wide_high[...], wide_low[...]))
    width = out.shape[1] // len(outs)
    for n, ref in enumerate(outs):
        ref[...] = out[:, n * width : (n + 1) * width]


def last_core(kept, came, core):
    ranks_x, fields, ranks_y, ranks_z = core.shape
    z = jnp.transpose(kept[...] + came[...])
    for f in range(fields):
        core[:, f] = z[:, f * ranks_z : (f + 1) * ranks_z].reshape(ranks_x, ranks_y, ranks_z)


def relative(factor, axis):
    count = lax.axis_size(axis)
    order = [0]
    step = 1
    while step < count:
        order = order + [n + step for n in order]
        step *= 2
    bits = count.bit_length() - 1
    order = [sum(((n >> b) & 1) << (bits - 1 - b) for b in range(bits)) for n in range(count)]
    blocks = factor.reshape(factor.shape[0], count, factor.shape[1] // count)
    here = lax.axis_index(axis)
    picked = [
        lax.dynamic_index_in_dim(blocks, jnp.bitwise_xor(here, n), axis=1, keepdims=False) for n in order
    ]
    return jnp.stack(picked, axis=1)


def swap(value, axis, mask):
    count = lax.axis_size(axis)
    return lax.ppermute(value, axis, [(i, i ^ mask) for i in range(count)])


def per_device(velocity, inv_density, factor_x, factor_y, factor_z):
    nx, ny, nz = inv_density.shape
    wide, rows = nx + 2 * LAYERS, ny + 2 * WIDE
    count_x, count_y, count_z = (lax.axis_size(axis) for axis in AXES)
    devices = count_x * count_y * count_z
    cells = (nx, ny, nz)
    rank = factor_x.shape[1]
    index = lax.axis_index("gx").reshape(1)

    shape = (((REACH + 1 + LAYERS + 1) * ny + 2 * REACH), nz)
    number = 1 if count_x == 2 else 2
    sent = call(
        pack_x,
        [shape] * number,
        [index, velocity, inv_density],
        scratch=[(number, 3, LAYERS, ny, nz), (number, LAYERS, ny, nz)],
        smem=1,
        far_in=(1, 2),
        sems=4 * number,
    )
    near = [swap(sent[0], "gx", 1)] if count_x == 2 else list(exchange(*sent, "gx"))
    rhs, = call(sources, [cells], [velocity], cost=(nx * ny * nz * 10, 4 * cost_of(cells)))
    shape = (wide // 2, ROWS, nz)
    up, down = call(pack_y, [shape, shape], [index, velocity, inv_density, rhs, *near], smem=1)
    before, after = exchange(up, down, "gy")
    parts = nz // SPAN
    groups = -(-wide // parts)
    message = (-(-groups // 2), rows, nz)
    whole = (groups * parts, rows, nz)
    strip = (groups, rows, nz)
    rhs_wide, inv_wide, up, down, strip_rhs, strip_inv = call(
        pack_z,
        [(wide, rows, nz)] * 2 + [message, message, strip, strip],
        [index, velocity, inv_density, rhs, *near, before, after],
        scratch=[whole] * 3 + [strip] * 2,
        smem=1,
        limit=18,
        far_out=(0, 1, 4, 5),
        sems=4,
    )
    before, after = exchange(up, down, "gz")
    span = (nx + 2, rows, nz)
    whole = (wide, rows, nz)
    *spans, sums = call(
        basis_main,
        [span] * (ITERS + 1) + [(len(PAIRS) + 1, WIDE, nz)],
        [rhs_wide, inv_wide],
        scratch=[whole] * (6 + ITERS),
        limit=22,
        cost=(wide * rows * nz * 100, 7 * cost_of(whole)),
        far_in=(0, 1),
        far_out=range(ITERS + 1),
        sems=ITERS + 3,
    )
    padded = (groups + 2, rows, nz)
    *strips, dots = call(
        functools.partial(basis_strips, nx),
        [strip] * ITERS + [(devices, WIDE, nz)],
        [strip_rhs, strip_inv, before, after, sums],
        scratch=[padded] * (6 + ITERS) + [strip] * 2,
        far_in=(0, 1),
        far_out=range(ITERS),
        sems=ITERS + 2,
    )
    dots = lax.all_to_all(dots, AXES, 0, 0, tiled=True)

    ranks_y, ranks_z = rank // count_y, rank // count_z
    planes = nz // ranks_y
    table_y, table_x = (planes * ny, count_y * nz), (nx * ranks_y, rank * ranks_y)
    y_high, y_low, x_high, x_low = pl.pallas_call(
        tables,
        out_shape=[jax.ShapeDtypeStruct(one, BF16) for one in (table_y, table_y, table_x, table_x)],
        in_specs=[VMEM] * 2,
        out_specs=[VMEM] * 4,
        scratch_shapes=[pltpu.VMEM((nx, rank * ranks_y), F32)] * 2,
        compiler_params=pltpu.CompilerParams(vmem_limit_bytes=16 * 2**20),
        cost_estimate=pl.CostEstimate(
            flops=4 * nx * ranks_y * rank * ranks_y, bytes_accessed=6 * 2**20, transcendentals=0
        ),
    )(relative(factor_y, "gy").reshape(ny, rank), relative(factor_x, "gx").reshape(nx, rank))
    columns = relative(factor_z, "gz")
    columns = jnp.transpose(columns.reshape(nz, -1))
    high, low = split_table(columns)
    columns = jnp.concatenate(
        [jnp.concatenate([high, high], axis=1), jnp.concatenate([low, low], axis=1)], axis=0
    )
    piece = (4 * nx // 2, ranks_z, nz)
    far = [*strips, *spans, velocity, inv_density]
    pressure, corrected, keep, keep_more, send = call(
        finish,
        [cells, (3,) + cells, piece, piece, (2,) + piece],
        [dots, columns, *far],
        scratch=[span, (nx + 2, ny, nz), strip, pltpu.VMEM((4, 2 * ny, 2 * nz), BF16), cells, (3,) + cells]
        + [one.shape for one in far],
        limit=32,
        far_in=range(2, 2 + len(far)),
        far_out=(0, 1),
        sems=len(far) + 16,
    )

    came = swap(send, "gz", 1)
    send = keep_more + came[1]
    keep = keep + came[0]
    came = swap(send, "gz", 2)

    shape = (4 * nx // planes * ranks_z, nz)
    keep, keep_more, send = call(
        rank_y, [shape] * 2 + [(2,) + shape], [keep, came, y_high, y_low], limit=16
    )
    came = swap(send, "gy", 1)
    send = keep_more + came[1]
    keep = keep + came[0]
    came = swap(send, "gy", 2)

    half = (4 * ranks_z, rank * ranks_y // 2)
    keep, send = call(
        functools.partial(rank_x, ranks_z), [half] * 2, [keep, came, x_high, x_low], limit=16
    )
    mask = 1
    while True:
        came = swap(send, "gx", mask)
        mask *= 2
        if mask >= count_x:
            break
        total = keep + came
        width = total.shape[1] // 2
        keep, send = total[:, :width], total[:, width:]
    core, = call(last_core, [(rank // count_x, 4, ranks_y, ranks_z)], [keep, came], limit=16)
    return pressure, corrected, core


def solution(mesh):
    placed = (
        P(None, "gx", "gy", "gz"),
        P("gx", "gy", "gz"),
        P("gx", None),
        P("gy", None),
        P("gz", None),
    )
    return jax.shard_map(
        per_device,
        mesh=mesh,
        in_specs=placed,
        out_specs=(P("gx", "gy", "gz"), P(None, "gx", "gy", "gz"), P("gx", None, "gy", "gz")),
        check_vma=False,
    )
```

```python
import functools
import math

import jax
import jax.numpy as jnp
from jax import lax
from jax.experimental import pallas as pl
from jax.experimental.pallas import tpu as pltpu
from jax.sharding import PartitionSpec as P

ITERS = 4
SHIFT = 0.1
AXES = ("gx", "gy", "gz")

REACH = ITERS
LAYERS = ITERS + 1
WIDE = 8
SLOT = 16
STRIP = 2 * LAYERS
SPAN = 32
ROWS = 24
NEWTON = (0.5, 0.5, 0.5)
PAIRS = [(a, b) for a in range(ITERS) for b in range(a, ITERS)]
VMEM = pl.BlockSpec(memory_space=pltpu.VMEM)
SMEM = pl.BlockSpec(memory_space=pltpu.SMEM)
HBM = pl.BlockSpec(memory_space=pltpu.HBM)
F32 = jnp.float32
BF16 = jnp.bfloat16


def call(body, outs, operands, scratch=(), smem=0, limit=12, cost=None, far_in=(), far_out=(), pinned=(), sems=0):
    scratch = [pltpu.VMEM(shape, F32) if isinstance(shape, tuple) else shape for shape in scratch]
    return pl.pallas_call(
        body,
        out_shape=[
            pltpu.HBM(shape, F32)
            if n in far_out or n in pinned
            else jax.ShapeDtypeStruct(shape, F32)
            for n, shape in enumerate(outs)
        ],
        in_specs=[SMEM if n < smem else HBM if n in far_in else VMEM for n in range(len(operands))],
        out_specs=[HBM if n in far_out else VMEM for n in range(len(outs))],
        scratch_shapes=scratch + ([pltpu.SemaphoreType.DMA((sems,))] if sems else []),
        compiler_params=pltpu.CompilerParams(vmem_limit_bytes=limit * 2**20),
        cost_estimate=cost
        and pl.CostEstimate(flops=cost[0], bytes_accessed=cost[1], transcendentals=0),
    )(
        *(
            pltpu.with_memory_space_constraint(one, pltpu.HBM)
            if n in far_in
            else one
            for n, one in enumerate(operands)
        )
    )


def cost_of(shape):
    return 4 * math.prod(shape)


def lanes(shape):
    return lax.broadcasted_iota(jnp.int32, shape, len(shape) - 1)


def sublanes(shape):
    return lax.broadcasted_iota(jnp.int32, shape, len(shape) - 2)


def exchange(up, down, axis):
    count = lax.axis_size(axis)
    ends = count - 1
    below = lax.ppermute(up, axis, [(i, i + 1) for i in range(ends)])
    above = lax.ppermute(down, axis, [(i + 1, i) for i in range(ends)])
    return below, above


def source(velocity, x, nx):
    ny, nz = velocity.shape[2:]
    shape = (ny, nz)
    before = jnp.where(x == 0, 0.0, velocity[0, jnp.maximum(x - 1, 0)])
    after = jnp.where(x == nx - 1, 0.0, velocity[0, jnp.minimum(x + 1, nx - 1)])
    along_y = velocity[1, x]
    along_z = velocity[2, x]
    total = after - before
    total = total + jnp.where(sublanes(shape) == ny - 1, 0.0, pltpu.roll(along_y, ny - 1, 0))
    total = total - jnp.where(sublanes(shape) == 0, 0.0, pltpu.roll(along_y, 1, 0))
    total = total + jnp.where(lanes(shape) == nz - 1, 0.0, pltpu.roll(along_z, nz - 1, 1))
    total = total - jnp.where(lanes(shape) == 0, 0.0, pltpu.roll(along_z, 1, 1))
    return -0.5 * total


def sources(velocity, rhs):
    nx = rhs.shape[0]

    def plane(x, carry):
        rhs[x] = source(velocity, x, nx)
        return carry

    lax.fori_loop(0, nx, plane, 0, unroll=4)


def pack_x(index, velocity_far, inv_far, *refs):
    velocity, inv, sems = refs[-3:]
    messages = refs[:-3]
    layers, ny, nz = inv.shape[1:]
    far = inv_far.shape[0] - layers
    shape = (ny, nz)
    only = len(messages) == 1
    first = index[0] == 0

    def copies(n):
        start = jnp.where(first, far, 0) if only else (far, 0)[n]
        part = pl.ds(start, layers)
        yield pltpu.make_async_copy(inv_far.at[part], inv.at[n], sems.at[4 * n])
        for d in range(3):
            yield pltpu.make_async_copy(velocity_far.at[d, part], velocity.at[n, d], sems.at[4 * n + d + 1])

    for n in range(len(messages)):
        for copy in copies(n):
            copy.start()

    def fill(n, start, own, sign):
        message, near = messages[n], velocity.at[n]
        for k in range(REACH):
            message[k * ny : (k + 1) * ny, :] = source(near, start + k, layers)
        base = REACH * ny
        message[base : base + ny, :] = sign * near[0, own]
        base += ny
        for k in range(LAYERS):
            message[base : base + ny, :] = inv[n, k]
            base += ny
        ends = jnp.zeros(shape, F32)
        for k in range(REACH):
            plane_z = near[2, start + k]
            ends = jnp.where(lanes(shape) == 2 * k, plane_z[:, 0:1], ends)
            ends = jnp.where(lanes(shape) == 2 * k + 1, plane_z[:, nz - 1 : nz], ends)
        message[base : base + ny, :] = ends
        base += ny
        for k in range(REACH):
            message[base + 2 * k : base + 2 * k + 1, :] = near[1, start + k, 0:1, :]
            message[base + 2 * k + 1 : base + 2 * k + 2, :] = near[1, start + k, ny - 1 : ny, :]

    for n in range(len(messages)):
        for copy in copies(n):
            copy.wait()
    upper = (1, layers - 1, 0.5)
    lower = (0, 0, -0.5)
    if only:
        fill(0, *(jnp.where(first, one, two) for one, two in zip(upper, lower)))
    else:
        fill(0, *upper)
        fill(1, *lower)


class Scaled:
    def __init__(self, ref, factor):
        self.ref, self.factor = ref, factor

    def __getitem__(self, where):
        return self.ref[where] * self.factor


def sides_x(index, messages):
    if len(messages) == 2:
        return messages
    first = jnp.where(index[0] == 0, 1.0, 0.0)
    return Scaled(messages[0], 1.0 - first), Scaled(messages[0], first)


def pack_y(index, velocity, inv, rhs, *refs):
    (below, above), (up, down) = sides_x(index, refs[:-2]), refs[-2:]
    nx, ny, nz = inv.shape
    each = REACH + 1 + LAYERS + 1

    def put(pair, parity, rows_rhs, ghost, rows_inv, first, last):
        offset = parity * each
        for message, part in ((up, 1), (down, 0)):
            message[pair, pl.ds(offset, REACH), :] = rows_rhs[part]
            message[pair, pl.ds(offset + REACH, 1), :] = (0.5 if part else -0.5) * ghost[part]
            message[pair, pl.ds(offset + REACH + 1, LAYERS), :] = rows_inv[part]
            ends = jnp.zeros((1, nz), F32)
            for k in range(REACH):
                ends = jnp.where(lanes((1, nz)) == 2 * k, first[part][k : k + 1], ends)
                ends = jnp.where(lanes((1, nz)) == 2 * k + 1, last[part][k : k + 1], ends)
            message[pair, pl.ds(offset + each - 1, 1), :] = ends

    def halo(x, message, k_rhs, k_inv, extra):
        base = (REACH + 1 + k_inv) * ny
        rows_inv = (message[pl.ds(base, LAYERS), :], message[pl.ds(base + ny - LAYERS, LAYERS), :])
        zero_row = jnp.zeros((1, nz), F32)
        zero = jnp.zeros((REACH, nz), F32)
        if k_rhs is None:
            column = jnp.zeros((REACH, 1), F32)
            put(x // 2, x % 2, (zero, zero), (zero_row, zero_row), rows_inv, (column, column), (column, column))
            return
        low, high = message[pl.ds(k_rhs * ny, REACH), :], message[pl.ds((k_rhs + 1) * ny - REACH, REACH), :]
        if extra is not None:
            sign, source = extra
            low = low + sign * velocity[0, source, 0:REACH, :]
            high = high + sign * velocity[0, source, ny - REACH : ny, :]
        ends = (REACH + 1 + LAYERS) * ny
        lines = ends + ny + 2 * k_rhs
        ghost = (message[pl.ds(lines, 1), :], message[pl.ds(lines + 1, 1), :])
        head, tail = message[pl.ds(ends, REACH), :], message[pl.ds(ends + ny - REACH, REACH), :]
        first = (head[:, 2 * k_rhs : 2 * k_rhs + 1], tail[:, 2 * k_rhs : 2 * k_rhs + 1])
        last = (head[:, 2 * k_rhs + 1 : 2 * k_rhs + 2], tail[:, 2 * k_rhs + 1 : 2 * k_rhs + 2])
        put(x // 2, x % 2, (low, high), ghost, rows_inv, first, last)

    for k in range(LAYERS):
        halo(k, below, k - 1 if k else None, k, (-0.5, 0) if k == LAYERS - 1 else None)
        halo(
            nx + LAYERS + k,
            above,
            k if k < REACH else None,
            k,
            (0.5, nx - 1) if k == 0 else None,
        )

    def own(x, pair, parity, extra):
        low, high = rhs[x, 0:REACH, :], rhs[x, ny - REACH : ny, :]
        if extra is not None:
            low = low + extra[pl.ds(REACH * ny, REACH), :]
            high = high + extra[pl.ds((REACH + 1) * ny - REACH, REACH), :]
        ghost = (velocity[1, x, 0:1, :], velocity[1, x, ny - 1 : ny, :])
        rows_inv = (inv[x, 0:LAYERS, :], inv[x, ny - LAYERS : ny, :])
        head, tail = velocity[2, x, 0:REACH, :], velocity[2, x, ny - REACH : ny, :]
        first = (head[:, 0:1], tail[:, 0:1])
        last = (head[:, nz - 1 : nz], tail[:, nz - 1 : nz])
        put(pair, parity, (low, high), ghost, rows_inv, first, last)

    def at(x, extra):
        own(x, (x + LAYERS) // 2, (x + LAYERS) % 2, extra)

    at(0, below)
    at(nx - 1, above)
    begin = 1 + (1 + LAYERS) % 2
    finish = begin + (nx - 1 - begin) // 2 * 2
    for x in (*range(1, begin), *range(finish, nx - 1)):
        at(x, None)

    def planes(n, carry):
        for parity in range(2):
            own(begin + 2 * n + parity, (begin + LAYERS) // 2 + n, parity, None)
        return carry

    lax.fori_loop(0, (finish - begin) // 2, planes, 0, unroll=3)


def pack_z(index, velocity, inv, rhs, *refs):
    (below, above), before, after = sides_x(index, refs[:-14]), refs[-14], refs[-13]
    rhs_far, inv_far, up, down, strip_rhs_far, strip_inv_far = refs[-12:-6]
    rhs_wide, inv_wide, ends, strip_rhs, strip_inv, sems = refs[-6:]
    nx, ny, nz = inv.shape
    wide = nx + 2 * LAYERS
    rows = ny + 2 * WIDE
    each = REACH + 1 + LAYERS + 1
    mine = pl.ds(WIDE, ny)
    edge = (WIDE, nz)
    groups = strip_rhs.shape[0]

    for k in range(LAYERS):
        for message, x, layer in ((below, k, k - 1), (above, nx + LAYERS + k, k if k < REACH else -1)):
            base = (REACH + 1 + k) * ny
            inv_wide[x, mine, :] = message[pl.ds(base, ny), :]
            if layer < 0:
                rhs_wide[x, mine, :] = jnp.zeros((ny, nz), F32)
                ends[x, mine, :] = jnp.zeros((ny, nz), F32)
                continue
            part = message[pl.ds(layer * ny, ny), :]
            if x == LAYERS - 1:
                part = part - 0.5 * velocity[0, 0]
            if x == nx + LAYERS:
                part = part + 0.5 * velocity[0, nx - 1]
            rhs_wide[x, mine, :] = part
            line = message[pl.ds((REACH + 1 + LAYERS) * ny, ny), :]
            ends[x, mine, :] = jnp.where(
                lanes((ny, nz)) == 0, line[:, 2 * layer : 2 * layer + 1], line[:, 2 * layer + 1 : 2 * layer + 2]
            )

    def plane(x, carry):
        inv_wide[x + LAYERS, mine, :] = inv[x]
        rhs_wide[x + LAYERS, mine, :] = rhs[x]
        ends[x + LAYERS, mine, :] = velocity[2, x]
        return carry

    lax.fori_loop(0, nx, plane, 0, unroll=4)
    rhs_wide[LAYERS, mine, :] += below[pl.ds(REACH * ny, ny), :]
    rhs_wide[LAYERS + nx - 1, mine, :] += above[pl.ds(REACH * ny, ny), :]
    for ref in (rhs_wide, inv_wide, ends):
        for x in range(wide, ref.shape[0]):
            ref[x] = jnp.zeros((rows, nz), F32)

    def finish(x, ghost_low, ghost_high):
        low, high = before[x // 2], after[x // 2]
        low = jnp.where(x % 2 == 0, low, pltpu.roll(low, ROWS - each, 0))[0:SLOT]
        high = jnp.where(x % 2 == 0, high, pltpu.roll(high, ROWS - each, 0))[0:SLOT]
        part = pltpu.roll(low, WIDE - REACH, 0)[0:WIDE]
        part = jnp.where(sublanes(edge) >= WIDE - REACH, part, 0.0)
        part = part - jnp.where(sublanes(edge) == WIDE - 1, 0.5 * ghost_low, 0.0)
        rhs_wide[x, 0:WIDE, :] = part
        part = pltpu.roll(low, SLOT - (REACH + 1) + WIDE - LAYERS, 0)[0:WIDE]
        inv_wide[x, 0:WIDE, :] = jnp.where(sublanes(edge) >= WIDE - LAYERS, part, 0.0)
        part = jnp.where(sublanes(edge) < REACH, high[0:WIDE], 0.0)
        part = part + jnp.where(sublanes(edge) == 0, 0.5 * ghost_high, 0.0)
        rhs_wide[x, WIDE + ny : rows, :] = part
        part = pltpu.roll(high, SLOT - (REACH + 1), 0)[0:WIDE]
        inv_wide[x, WIDE + ny : rows, :] = jnp.where(sublanes(edge) < LAYERS, part, 0.0)
        head = rhs_wide[x, WIDE : 2 * WIDE, :]
        rhs_wide[x, WIDE : 2 * WIDE, :] = head + jnp.where(sublanes(edge) == 0, low[REACH : REACH + 1], 0.0)
        tail = rhs_wide[x, ny : WIDE + ny, :]
        rhs_wide[x, ny : WIDE + ny, :] = tail + jnp.where(
            sublanes(edge) == WIDE - 1, high[REACH : REACH + 1], 0.0
        )
        for message, start, place in ((low, WIDE - REACH, 0), (high, 0, WIDE + ny)):
            line = message[each - 1 : each]
            one = jnp.zeros(edge, F32)
            two = jnp.zeros(edge, F32)
            for k in range(REACH):
                here = sublanes(edge) == start + k
                one = jnp.where(here, line[:, 2 * k : 2 * k + 1], one)
                two = jnp.where(here, line[:, 2 * k + 1 : 2 * k + 2], two)
            ends[x, place : place + WIDE, :] = jnp.where(lanes(edge) == 0, one, two)

    for k in range(LAYERS):
        for message, x, layer in ((below, k, k - 1), (above, nx + LAYERS + k, k if k < REACH else -1)):
            lines = (REACH + 1 + LAYERS + 1) * ny + 2 * layer
            if layer < 0:
                zero = jnp.zeros((1, nz), F32)
                finish(x, zero, zero)
            else:
                finish(x, message[pl.ds(lines, 1), :], message[pl.ds(lines + 1, 1), :])

    def middle(x, carry):
        finish(x + LAYERS, velocity[1, x, 0:1, :], velocity[1, x, ny - 1 : ny, :])
        return carry

    lax.fori_loop(0, nx, middle, 0, unroll=4)
    copies = [
        pltpu.make_async_copy(ref.at[pl.ds(0, wide)], far, sems.at[n])
        for n, (ref, far) in enumerate(((rhs_wide, rhs_far), (inv_wide, inv_far)))
    ]
    for copy in copies:
        copy.start()

    whole = (rows, nz)
    lane = lanes(whole)
    place = lane % SPAN

    def back(value, step):
        return pltpu.roll(value, nz - step, 1)

    def gather(ref, g):
        value = None
        for n in range(nz // SPAN):
            moved = pltpu.roll(ref[g + n * groups], n * SPAN + STRIP, 1)
            value = moved if value is None else jnp.where(lane >= n * SPAN, moved, value)
        return value

    def pack(g):
        r, i, e = gather(rhs_wide, g), gather(inv_wide, g), gather(ends, g)
        apart = SPAN - 2 * STRIP
        for ref, value in ((strip_rhs, r), (strip_inv, i)):
            out = jnp.where(place < STRIP, value, 0.0)
            ref[g] = jnp.where(place >= SPAN - STRIP, pltpu.roll(value, apart, 1), out)
        ghost = jnp.where(place == STRIP, 0.5 * pltpu.roll(e, 1, 1), 0.0)
        ghost = jnp.where(place == SPAN - STRIP - 1, -0.5 * pltpu.roll(e, apart - 1, 1), ghost)
        strip_rhs[g] += ghost
        out = jnp.where(place < REACH, back(r, STRIP - REACH), 0.0)
        out = jnp.where(place == REACH, 0.5 * back(e, STRIP - 1 - REACH), out)
        here = (place > REACH) & (place <= REACH + LAYERS)
        higher = jnp.where(here, pltpu.roll(i, (nz + REACH + 1 + LAYERS - STRIP) % nz, 1), out)
        out = jnp.where(place < REACH, back(r, STRIP), 0.0)
        out = jnp.where(place == REACH, -0.5 * back(e, STRIP - REACH), out)
        return higher, jnp.where(here, back(i, STRIP - REACH - 1), out)

    halves = up.shape[0]

    def both(n, carry):
        one, two = pack(n)
        up[n] = one
        down[n] = two
        return carry

    lax.fori_loop(0, halves, both, 0, unroll=2)

    def more(n, carry):
        one, two = pack(n + halves)
        up[n] += pltpu.roll(one, SPAN // 2, 1)
        down[n] += pltpu.roll(two, SPAN // 2, 1)
        return carry

    lax.fori_loop(0, groups - halves, more, 0, unroll=2)
    for ref, far in ((strip_rhs, strip_rhs_far), (strip_inv, strip_inv_far)):
        copies.append(pltpu.make_async_copy(ref, far, sems.at[len(copies)]))
        copies[-1].start()
    for copy in copies:
        copy.wait()


def shifted(ref, x, t, step):
    rows = ref.shape[1]
    start = t * WIDE + step
    if start < 0:
        return pltpu.roll(ref[x, 0:WIDE, :], 1, 0)
    if start + WIDE > rows:
        return pltpu.roll(ref[x, rows - WIDE : rows, :], WIDE - 1, 0)
    return ref[x, start : start + WIDE, :]


class Stencil:
    def __init__(self, inv, root, ax, ay, az, vs, planes, edges=None, unroll=4):
        self.inv, self.root, self.ax, self.ay, self.az, self.vs = inv, root, ax, ay, az, vs
        self.planes, self.edges, self.unroll = planes, edges or (lambda ref: None), unroll
        self.count, self.rows, self.nz = inv.shape
        self.tiles = self.rows // WIDE

    def here(self, t):
        return slice(t * WIDE, (t + 1) * WIDE)

    def right(self, value):
        return pltpu.roll(value, self.nz - 1, 1)

    def left(self, value):
        return pltpu.roll(value, 1, 1)

    def prepare(self, rhs, parts=None):
        inv, root = self.inv, self.root
        self.edges(inv)

        def scales(x, carry):
            writes = []
            for t in range(self.tiles):
                here = self.here(t)
                c = inv[x, here, :]
                total = (inv[x + 1, here, :] + inv[x - 1, here, :]) + (self.right(c) + self.left(c))
                total = total + (shifted(inv, x, t, 1) + shifted(inv, x, t, -1))
                value = jnp.where(c > 0.0, lax.rsqrt(SHIFT + 0.5 * (6.0 * c + total)), 0.0)
                writes.append((here, value, rhs[x, here, :] * value))
            for here, one, two in writes:
                root[x, here, :] = one
                self.vs[0][x, here, :] = two
            return carry

        for start, stop in parts or [(1, self.count - 1)]:
            lax.fori_loop(start, stop, scales, 0, unroll=self.unroll)
        zero = jnp.zeros((self.rows, self.nz), F32)
        for ref in (root, self.vs[0]):
            ref[0] = zero
            ref[self.count - 1] = zero
            self.edges(ref)

        def couplings(x, carry):
            writes = []
            for t in range(self.tiles):
                here = self.here(t)
                c, d = inv[x, here, :], root[x, here, :]
                half = 0.5 * d
                writes.append(
                    (
                        here,
                        (c + inv[x + 1, here, :]) * (half * root[x + 1, here, :]),
                        (c + shifted(inv, x, t, 1)) * (half * shifted(root, x, t, 1)),
                        (c + self.right(c)) * (half * self.right(d)),
                    )
                )
            for here, x_face, y_face, z_face in writes:
                self.ax[x, here, :] = x_face
                self.ay[x, here, :] = y_face
                self.az[x, here, :] = z_face
            return carry

        lax.fori_loop(1, self.count - 1, couplings, 0, unroll=self.unroll)
        self.ax[0] = zero
        self.edges(self.ax)

    def couple(self, k, x, t):
        here = self.here(t)
        v, ax, ay = self.vs[k], self.ax, self.ay
        c, f = v[x, here, :], self.az[x, here, :]
        total = ax[x, here, :] * v[x + 1, here, :] + ax[x - 1, here, :] * v[x - 1, here, :]
        total = total + (f * self.right(c) + self.left(f * c))
        total = total + ay[x, here, :] * shifted(v, x, t, 1)
        return c, total + shifted(ay, x, t, -1) * shifted(v, x, t, -1)

    def extend(self, k):
        scale = 1.0 - NEWTON[k]

        def step(x, carry):
            writes = []
            for t in range(self.tiles):
                c, total = self.couple(k, x, t)
                writes.append((t, scale * c - total if scale else -total))
            for t, value in writes:
                self.vs[k + 1][x, self.here(t), :] = value
            return carry

        start, stop = self.planes(k)
        lax.fori_loop(start, stop, step, 0, unroll=self.unroll)
        self.edges(self.vs[k + 1])

    def products(self, start, stop, mask):
        def measure(x, sums):
            sums = list(sums)
            for t in range(1, self.tiles - 1):
                keep = mask(x)
                v = [self.vs[k][x, self.here(t), :] for k in range(ITERS)]
                own, total = self.couple(ITERS - 1, x, t)
                kept = [jnp.where(keep, one, 0.0) for one in v]
                for n, (a, b) in enumerate(PAIRS):
                    sums[n] = sums[n] + v[a] * kept[b]
                sums[-1] = sums[-1] + kept[-1] * (own - total)
            return tuple(sums)

        zero = jnp.zeros((WIDE, self.nz), F32)
        return lax.fori_loop(start, stop, measure, (zero,) * (len(PAIRS) + 1), unroll=2)


def basis_main(rhs_far, inv_far, *refs):
    outs, sums = refs[: ITERS + 1], refs[ITERS + 1]
    rhs, inv, root, ax, ay, az = refs[ITERS + 2 : ITERS + 8]
    vs, sems = refs[ITERS + 8 : -1], refs[-1]
    wide, rows, nz = ax.shape
    nx = wide - 2 * LAYERS
    batch = 4
    bounds = [n * wide // batch for n in range(batch + 1)]
    loads = []
    for n in range(batch):
        part = pl.ds(bounds[n], bounds[n + 1] - bounds[n])
        for far, ref in ((inv_far, inv), (rhs_far, rhs)):
            loads.append(pltpu.make_async_copy(far.at[part], ref.at[part], sems.at[ITERS + 1 + len(loads)]))
            loads[-1].start()

    def ready():
        for n in range(batch):
            for load in loads[2 * n : 2 * n + 2]:
                load.wait()
            yield max(bounds[n] - 1, 1), bounds[n + 1] - 1

    stencil = Stencil(inv, root, ax, ay, az, vs, lambda k: (2 + k, wide - 2 - k))
    copies = []

    def send(n, ref):
        copy = pltpu.make_async_copy(ref.at[pl.ds(LAYERS - 1, nx + 2)], outs[n], sems.at[n])
        copy.start()
        copies.append(copy)

    stencil.prepare(rhs, ready())
    send(ITERS, root)
    send(0, vs[0])
    for k in range(ITERS - 1):
        stencil.extend(k)
        send(k + 1, vs[k + 1])
    lane = lanes((WIDE, nz))
    inner = (lane > REACH) & (lane < nz - 1 - REACH)
    for n, one in enumerate(stencil.products(LAYERS, LAYERS + nx, lambda x: inner)):
        sums[n] = one
    for copy in copies:
        copy.wait()


def basis_strips(nx, rhs_far, inv_far, before, after, sums, *refs):
    outs, dots = refs[:ITERS], refs[ITERS]
    rhs, inv, root, ax, ay, az = refs[ITERS + 1 : ITERS + 7]
    vs, outs_near = refs[ITERS + 7 : 2 * ITERS + 7], refs[2 * ITERS + 7 : 3 * ITERS + 7]
    strip_rhs, strip_inv, sems = refs[-3:]
    groups, rows, nz = strip_inv.shape
    loads = [
        pltpu.make_async_copy(far, ref, sems.at[ITERS + n])
        for n, (far, ref) in enumerate(((rhs_far, strip_rhs), (inv_far, strip_inv)))
    ]
    for load in loads:
        load.start()
    for load in loads:
        load.wait()
    halves = before.shape[0]
    whole = (rows, nz)
    place = lanes(whole) % SPAN

    def edges(ref):
        ref[0] = pltpu.roll(ref[groups], SPAN, 1)
        ref[groups + 1] = pltpu.roll(ref[1], nz - SPAN, 1)

    def receive(g, low, high):
        start = SPAN - STRIP - LAYERS
        moved = pltpu.roll(low, start + 1, 1)
        r = strip_rhs[g] + jnp.where((place > start) & (place <= SPAN - STRIP), moved, 0.0)
        moved = pltpu.roll(low, start - REACH - 1, 1)
        i = strip_inv[g] + jnp.where((place >= start) & (place < SPAN - STRIP), moved, 0.0)
        moved = pltpu.roll(high, STRIP, 1)
        r = r + jnp.where((place >= STRIP) & (place < STRIP + REACH), moved, 0.0)
        moved = pltpu.roll(high, STRIP - REACH - 1, 1)
        r = r + jnp.where(place == STRIP - 1, moved, 0.0)
        i = i + jnp.where((place >= STRIP) & (place < STRIP + LAYERS), moved, 0.0)
        rhs[g + 1] = r
        inv[g + 1] = i

    def first(n, carry):
        receive(n, before[n], after[n])
        return carry

    def second(n, carry):
        half = nz - SPAN // 2
        receive(n + halves, pltpu.roll(before[n], half, 1), pltpu.roll(after[n], half, 1))
        return carry

    lax.fori_loop(0, halves, first, 0, unroll=3)
    lax.fori_loop(0, groups - halves, second, 0, unroll=3)
    stencil = Stencil(inv, root, ax, ay, az, vs, lambda k: (1, groups + 1), edges, groups)
    stencil.prepare(rhs)
    copies = []

    def result(k):
        ref = outs_near[k]

        def plane(g, carry):
            ref[g] = vs[k][g] * root[g]
            return carry

        lax.fori_loop(1, groups + 1, plane, 0, unroll=groups)
        copies.append(pltpu.make_async_copy(ref.at[pl.ds(1, groups)], outs[k], sems.at[k]))
        copies[-1].start()

    result(0)
    for k in range(ITERS - 1):
        stencil.extend(k)
        result(k + 1)
    lane = lanes((WIDE, nz))
    part = lane // SPAN
    spot = lane % SPAN
    ends = ((spot >= STRIP - LAYERS) & (spot < STRIP)) | (
        (spot >= SPAN - STRIP) & (spot < SPAN - STRIP + LAYERS)
    )

    def mask(x):
        plane = x - 1 + part * groups
        return ends & (plane >= LAYERS) & (plane < LAYERS + nx)

    totals = []
    for n, one in enumerate(stencil.products(1, groups + 1, mask)):
        line = jnp.sum(one + sums[n], axis=0, keepdims=True)
        totals.append(line + pltpu.roll(line, nz // 2, 1))
    row = sublanes((WIDE, nz))
    message = jnp.zeros((WIDE, nz), F32)
    for n, line in enumerate(totals):
        half = lane < nz // 2 if n < WIDE else lane >= nz // 2
        message = jnp.where((row == n % WIDE) & half, line, message)

    def send(n, carry):
        dots[n] = message
        return carry

    lax.fori_loop(0, dots.shape[0], send, 0, unroll=8)

    for copy in copies:
        copy.wait()


def coefficients(dots):
    half = lanes(dots.shape) < dots.shape[1] // 2
    one = jnp.sum(jnp.where(half, dots, 0.0), axis=1, keepdims=True)
    two = jnp.sum(jnp.where(half, 0.0, dots), axis=1, keepdims=True)

    def entry(n):
        return one[n : n + 1] if n < WIDE else two[n - WIDE : n - WIDE + 1]

    gram = {}
    for n, (a, b) in enumerate(PAIRS):
        gram[a, b] = gram[b, a] = entry(n)
    last = ITERS - 1
    image = {}
    for b in range(last):
        for a in range(ITERS):
            image[a, b] = gram[a, b + 1]
            if NEWTON[b]:
                image[a, b] = image[a, b] + NEWTON[b] * gram[a, b]
    for a in range(last):
        image[a, last] = image[last, a]
    image[last, last] = entry(len(PAIRS))

    def product(table, one, two):
        total = None
        for a, left in enumerate(one):
            for b, right in enumerate(two):
                term = left * right * table[a, b]
                total = term if total is None else total + term
        return total

    unit = jnp.ones((1, 1), F32)
    pressure = []
    precond = [unit]
    direction = [unit]
    rz = gram[0, 0]
    for iteration in range(ITERS):
        alpha = rz / product(image, direction, direction)
        pressure = [
            (pressure[n] if n < len(pressure) else 0.0) + alpha * one for n, one in enumerate(direction)
        ]
        if iteration == last:
            break
        moved = []
        for n in range(len(direction) + 1):
            value = None
            if n < len(direction) and NEWTON[n]:
                value = NEWTON[n] * direction[n]
            if n > 0:
                value = direction[n - 1] if value is None else value + direction[n - 1]
            moved.append(value)
        fresh_precond = []
        for n, one in enumerate(moved):
            old = precond[n] if n < len(precond) else None
            if one is None:
                fresh_precond.append(old)
            else:
                fresh_precond.append(-alpha * one if old is None else old - alpha * one)
        precond = fresh_precond
        fresh = product(gram, precond, precond)
        beta = fresh / rz
        direction = [
            one + beta * direction[n] if n < len(direction) else one for n, one in enumerate(precond)
        ]
        rz = fresh
    return pressure


def finish(dots, columns, *refs):
    inputs = 2 * ITERS + 3
    pressure_far, corrected_far, keep, keep_more, send, p, gaps, mixed, cut, pressure, corrected = refs[inputs : inputs + 11]
    held, sems = refs[inputs + 11 : -1], refs[-1]
    strips, spans, roots = held[:ITERS], held[ITERS : 2 * ITERS], held[2 * ITERS]
    velocity, inv = held[2 * ITERS + 1 :]
    nx, ny, nz = inv.shape
    batch = 4
    each = nx // batch
    used = 0

    def start(far, ref):
        nonlocal used
        copy = pltpu.make_async_copy(far, ref, sems.at[used])
        used += 1
        copy.start()
        return copy

    strip_loads = [start(far, ref) for far, ref in zip(refs[:ITERS], strips)]
    span_loads, other_loads, bounds = [], [], []
    for n in range(batch):
        low, high = (n * each + 2 if n else 0), (n + 1) * each + 2
        bounds.append((low, high))
        part = pl.ds(low, high - low)
        pairs = zip(refs[ITERS : 2 * ITERS + 1], held[ITERS : 2 * ITERS + 1])
        span_loads.append([start(far.at[part], ref.at[part]) for far, ref in pairs])
        part = pl.ds(n * each, each)
        other_loads.append(
            [start(refs[2 * ITERS + 1].at[d, part], velocity.at[d, part]) for d in range(3)]
            + [start(refs[2 * ITERS + 2].at[part], inv.at[part])]
        )
    shape = (ny, nz)
    groups = mixed.shape[0]
    total = dots[0]
    for n in range(1, dots.shape[0]):
        total = total + dots[n]
    weights = coefficients(total)

    def strip(g, carry):
        value = weights[0] * strips[0][g]
        for k in range(1, ITERS):
            value = value + weights[k] * strips[k][g]
        mixed[g] = value
        return carry

    for load in strip_loads:
        load.wait()
    lax.fori_loop(0, groups, strip, 0, unroll=4)
    mine = slice(WIDE, WIDE + ny)
    lane = lanes(spans[0].shape[1:])

    def combine(x, carry):
        value = weights[0] * spans[0][x]
        for k in range(1, ITERS):
            value = value + weights[k] * spans[k][x]
        value = value * roots[x]
        plane = x + LAYERS - 1
        ends = mixed[plane % groups]
        start = plane // groups * SPAN
        last = pltpu.roll(ends, lax.rem(2 * nz - STRIP - start, nz), 1)
        first = pltpu.roll(ends, lax.rem(nz + STRIP - SPAN - start + nz, nz), 1)
        value = jnp.where(lane < LAYERS, first, jnp.where(lane >= nz - LAYERS, last, value))
        p[x] = value
        after = pltpu.roll(jnp.where(lane == 0, last, value), nz - 1, 1)
        before = pltpu.roll(jnp.where(lane == nz - 1, first, value), 1, 1)
        gaps[x] = (after - before)[mine]
        return carry

    half = columns.shape[0] // 2

    def pair(n, carry):
        for which in range(2):
            x = 2 * n + which
            centre = p[x + 1, mine, :]
            pressure[x] = centre
            half_inv = 0.5 * inv[x]
            slopes = (
                p[x + 2, mine, :] - p[x, mine, :],
                p[x + 1, WIDE + 1 : WIDE + 1 + ny, :] - p[x + 1, WIDE - 1 : WIDE - 1 + ny, :],
                gaps[x + 1],
            )
            fields = [velocity[d, x] - half_inv * slopes[d] for d in range(3)] + [centre]
            for d in range(3):
                corrected[d, x] = fields[d]
            for f, field in enumerate(fields):
                high = field.astype(BF16)
                low = (field - high.astype(F32)).astype(BF16)
                cut[f, which * ny : (which + 1) * ny, 0:nz] = high
                cut[f, which * ny : (which + 1) * ny, nz : 2 * nz] = low
        for f in range(4):
            out = lax.dot_general(
                columns[...], cut[f], (((1,), (1,)), ((), ())), preferred_element_type=F32
            )
            out = out[:half] + out[half:]
            block = f * (nx // 2) + n
            quarter = half // 4
            keep[block] = out[0:quarter]
            keep_more[block] = out[quarter : 2 * quarter]
            send[0, block] = out[2 * quarter : 3 * quarter]
            send[1, block] = out[3 * quarter :]
        return carry

    stores = []
    for n in range(batch):
        for load in span_loads[n]:
            load.wait()
        lax.fori_loop(*bounds[n], combine, 0, unroll=4)
        for load in other_loads[n]:
            load.wait()
        lax.fori_loop(n * each // 2, (n + 1) * each // 2, pair, 0, unroll=2)
        part = pl.ds(n * each, each)
        stores.append(start(pressure.at[part], pressure_far.at[part]))
        for d in range(3):
            stores.append(start(corrected.at[d, part], corrected_far.at[d, part]))
    for store in stores:
        store.wait()


def tables(count_x, factor_y, factor_x, y_high, y_low, x_high, x_low, spread_high, spread_low):
    ny, rank = factor_y.shape
    nx = factor_x.shape[0]
    planes = y_high.shape[0] // ny
    nz = x_high.shape[1] // rank * planes
    count = y_high.shape[1] // nz
    ranks = rank // count
    wide = jnp.concatenate([factor_y[...], jnp.zeros((ny, nz - rank), F32)], axis=1)
    lane = lanes((ny, nz))
    for h in range(count):
        value = pltpu.roll(wide, (nz - h * ranks) % nz, 1)
        value = jnp.where(lane < ranks, value, 0.0)
        step = ranks
        while step < nz:
            value = value + pltpu.roll(value, step, 1)
            step *= 2
        for n in range(planes):
            high, low = split(jnp.where(lane // ranks == n, value, 0.0))
            y_high[n * ny : (n + 1) * ny, h * nz : (h + 1) * nz] = high
            y_low[n * ny : (n + 1) * ny, h * nz : (h + 1) * nz] = low
    width = x_high.shape[1]
    shape = (rank, width)
    own = rank // count_x
    lane = lanes(shape)
    copy = lane // (ranks * own) * own + lane % own == sublanes(shape)
    copy = jnp.where(copy, 1.0, 0.0).astype(BF16)
    for ref, value in zip((spread_high, spread_low), split(factor_x[...])):
        ref[...] = jnp.dot(value, copy, preferred_element_type=F32)
    shape = (ranks, width)
    here = lanes(shape) // own % ranks == sublanes(shape)

    def row(i, carry):
        at = pl.ds(pl.multiple_of(i * ranks, ranks), ranks)
        x_high[at, :] = jnp.where(here, spread_high[pl.ds(i, 1), :], 0.0).astype(BF16)
        x_low[at, :] = jnp.where(here, spread_low[pl.ds(i, 1), :], 0.0).astype(BF16)
        return carry

    lax.fori_loop(0, nx, row, 0, unroll=4)


def split(value):
    high = value.astype(BF16)
    return high, (value - high.astype(F32)).astype(BF16)


def split_table(value):
    high = lax.reduce_precision(value, exponent_bits=8, mantissa_bits=7)
    return high.astype(BF16), (value - high).astype(BF16)


def three(a, b, dims=(((1,), (0,)), ((), ()))):
    dot = functools.partial(lax.dot_general, dimension_numbers=dims, preferred_element_type=F32)
    (ah, al), (bh, bl) = a, b
    return dot(ah, bh) + (dot(al, bh) + dot(ah, bl))


def rank_y(x, table):
    blocks, ranks, nz = x.shape
    group = table[0].shape[0] // nz
    parts = [
        jnp.concatenate([x[n * group + q] for q in range(group)], axis=1) for n in range(blocks // group)
    ]
    out = three(split(jnp.concatenate(parts, axis=0)), table)
    return [out[:, n * nz : (n + 1) * nz] for n in range(out.shape[1] // nz)]


def tail_one(kept, more, came, high, low, p_send, p_keep, q_send, q_keep, q_more):
    half = kept.shape[0] // 2
    p_send[...] = more[0:half] + came[1, 0:half]
    p_keep[...] = kept[0:half] + came[0, 0:half]
    x = jnp.concatenate([kept[half:] + came[0, half:], more[half:] + came[1, half:]], axis=0)
    q_keep[...], q_more[...], q_send[0], q_send[1] = rank_y(x, (high[...], low[...]))


def tail_two(p_kept, p_came, q_kept, q_more, q_came, high, low, p_send, p_keep, p_more, q_send, q_keep):
    q_send[...] = q_more[...] + q_came[1]
    q_keep[...] = q_kept[...] + q_came[0]
    parts = rank_y(p_kept[...] + p_came[...], (high[...], low[...]))
    p_keep[...], p_more[...], p_send[0], p_send[1] = parts


def tail_three(p_kept, p_more, p_came, q_kept, q_came, p_send, p_keep, q_send, q_keep):
    half = q_keep.shape[0]
    p_send[...] = p_more[...] + p_came[1]
    p_keep[...] = p_kept[...] + p_came[0]
    q_send[...] = q_kept[half:] + q_came[half:]
    q_keep[...] = q_kept[0:half] + q_came[0:half]


def rank_x(ranks, p_kept, p_came, q_kept, q_came, wide_high, wide_low, *outs):
    u = jnp.concatenate([p_kept[...] + p_came[...], q_kept[...] + q_came[...]], axis=0)
    rows, nz = u.shape
    group = wide_high.shape[0] // nz
    parts = []
    for f in range(rows // ranks // group):
        parts.append(
            jnp.concatenate(
                [u[(f * group + q) * ranks : (f * group + q + 1) * ranks] for q in range(group)], axis=1
            )
        )
    x = jnp.concatenate(parts, axis=0)
    out = three(split(x), (wide_high[...], wide_low[...]))
    width = out.shape[1] // len(outs)
    for n, ref in enumerate(outs):
        ref[...] = out[:, n * width : (n + 1) * width]


def last_core(kept, came, core):
    fields, ranks_y, ranks_z, ranks_x = core.shape
    z = kept[...] + came[...]
    for f in range(fields):
        for b in range(ranks_y):
            core[f, b] = z[f * ranks_z : (f + 1) * ranks_z, b * ranks_x : (b + 1) * ranks_x]


def relative(factor, axis):
    count = lax.axis_size(axis)
    order = [0]
    step = 1
    while step < count:
        order = order + [n + step for n in order]
        step *= 2
    bits = count.bit_length() - 1
    order = [sum(((n >> b) & 1) << (bits - 1 - b) for b in range(bits)) for n in range(count)]
    blocks = factor.reshape(factor.shape[0], count, factor.shape[1] // count)
    here = lax.axis_index(axis)
    picked = [
        lax.dynamic_index_in_dim(blocks, jnp.bitwise_xor(here, n), axis=1, keepdims=False) for n in order
    ]
    return jnp.stack(picked, axis=1)


def swap(value, axis, mask):
    count = lax.axis_size(axis)
    return lax.ppermute(value, axis, [(i, i ^ mask) for i in range(count)])


def per_device(velocity, inv_density, factor_x, factor_y, factor_z):
    nx, ny, nz = inv_density.shape
    wide, rows = nx + 2 * LAYERS, ny + 2 * WIDE
    count_x, count_y, count_z = (lax.axis_size(axis) for axis in AXES)
    devices = count_x * count_y * count_z
    cells = (nx, ny, nz)
    rank = factor_x.shape[1]
    index = lax.axis_index("gx").reshape(1)

    shape = (((REACH + 1 + LAYERS + 1) * ny + 2 * REACH), nz)
    number = 1 if count_x == 2 else 2
    sent = call(
        pack_x,
        [shape] * number,
        [index, velocity, inv_density],
        scratch=[(number, 3, LAYERS, ny, nz), (number, LAYERS, ny, nz)],
        smem=1,
        far_in=(1, 2),
        sems=4 * number,
    )
    near = [swap(sent[0], "gx", 1)] if count_x == 2 else list(exchange(*sent, "gx"))
    rhs, = call(sources, [cells], [velocity], cost=(nx * ny * nz * 10, 4 * cost_of(cells)))
    shape = (wide // 2, ROWS, nz)
    up, down = call(pack_y, [shape, shape], [index, velocity, inv_density, rhs, *near], smem=1)
    before, after = exchange(up, down, "gy")
    parts = nz // SPAN
    groups = -(-wide // parts)
    message = (-(-groups // 2), rows, nz)
    whole = (groups * parts, rows, nz)
    strip = (groups, rows, nz)
    rhs_wide, inv_wide, up, down, strip_rhs, strip_inv = call(
        pack_z,
        [(wide, rows, nz)] * 2 + [message, message, strip, strip],
        [index, velocity, inv_density, rhs, *near, before, after],
        scratch=[whole] * 3 + [strip] * 2,
        smem=1,
        limit=18,
        far_out=(0, 1, 4, 5),
        sems=4,
    )
    before, after = exchange(up, down, "gz")
    span = (nx + 2, rows, nz)
    whole = (wide, rows, nz)
    *spans, sums = call(
        basis_main,
        [span] * (ITERS + 1) + [(len(PAIRS) + 1, WIDE, nz)],
        [rhs_wide, inv_wide],
        scratch=[whole] * (6 + ITERS),
        limit=22,
        cost=(wide * rows * nz * 100, 7 * cost_of(whole)),
        far_in=(0, 1),
        far_out=range(ITERS + 1),
        sems=ITERS + 9,
    )
    padded = (groups + 2, rows, nz)
    *strips, dots = call(
        functools.partial(basis_strips, nx),
        [strip] * ITERS + [(devices, WIDE, nz)],
        [strip_rhs, strip_inv, before, after, sums],
        scratch=[padded] * (6 + 2 * ITERS) + [strip] * 2,
        far_in=(0, 1),
        far_out=range(ITERS),
        sems=ITERS + 2,
    )
    dots = lax.all_to_all(dots, AXES, 0, 0, tiled=True)

    ranks_y, ranks_z = rank // count_y, rank // count_z
    planes = nz // ranks_y
    table_y, table_x = (planes * ny, count_y * nz), (nx * ranks_y, rank * ranks_y)
    y_high, y_low, x_high, x_low = pl.pallas_call(
        functools.partial(tables, count_x),
        out_shape=[jax.ShapeDtypeStruct(one, BF16) for one in (table_y, table_y, table_x, table_x)],
        in_specs=[VMEM] * 2,
        out_specs=[VMEM] * 4,
        scratch_shapes=[pltpu.VMEM((nx, rank * ranks_y), F32)] * 2,
        compiler_params=pltpu.CompilerParams(vmem_limit_bytes=16 * 2**20),
        cost_estimate=pl.CostEstimate(
            flops=4 * nx * ranks_y * rank * ranks_y, bytes_accessed=6 * 2**20, transcendentals=0
        ),
    )(relative(factor_y, "gy").reshape(ny, rank), relative(factor_x, "gx").reshape(nx, rank))
    columns = relative(factor_z, "gz")
    columns = jnp.transpose(columns.reshape(nz, -1))
    high, low = split_table(columns)
    columns = jnp.concatenate(
        [jnp.concatenate([high, high], axis=1), jnp.concatenate([low, low], axis=1)], axis=0
    )
    piece = (4 * nx // 2, ranks_z, nz)
    far = [*strips, *spans, velocity, inv_density]
    pressure, corrected, keep, keep_more, send = call(
        finish,
        [cells, (3,) + cells, piece, piece, (2,) + piece],
        [dots, columns, *far],
        scratch=[span, (nx + 2, ny, nz), strip, pltpu.VMEM((4, 2 * ny, 2 * nz), BF16), cells, (3,) + cells]
        + [one.shape for one in far],
        limit=32,
        far_in=range(2, 2 + len(far)),
        far_out=(0, 1),
        sems=ITERS + 4 * (ITERS + 5) + 16,
    )

    came = swap(send, "gz", 1)
    table = [y_high, y_low]
    part = (piece[0] // 2, ranks_z, nz)
    half = (2 * nx // planes * ranks_z, nz)
    full = (2 * half[0], nz)
    p_send, p_keep, q_send, q_keep, q_more = call(
        tail_one, [part, part, (2,) + full, full, full], [keep, keep_more, came, *table], limit=16
    )
    p_came, q_came = swap(p_send, "gz", 2), swap(q_send, "gy", 1)
    p_send, p_keep, p_more, q_send, q_keep = call(
        tail_two,
        [(2,) + half, half, half, full, full],
        [p_keep, p_came, q_keep, q_more, q_came, *table],
        limit=16,
    )
    p_came, q_came = swap(p_send, "gy", 1), swap(q_send, "gy", 2)
    p_send, p_keep, q_send, q_keep = call(
        tail_three, [half] * 4, [p_keep, p_more, p_came, q_keep, q_came]
    )
    p_came, q_came = swap(p_send, "gy", 2), swap(q_send, "gz", 2)
    half = (4 * ranks_z, rank * ranks_y // 2)
    keep, send = call(
        functools.partial(rank_x, ranks_z),
        [half] * 2,
        [p_keep, p_came, q_keep, q_came, x_high, x_low],
        limit=16,
    )
    mask = 1
    while True:
        came = swap(send, "gx", mask)
        mask *= 2
        if mask >= count_x:
            break
        total = keep + came
        width = total.shape[1] // 2
        keep, send = total[:, :width], total[:, width:]
    core, = call(last_core, [(4, ranks_y, ranks_z, rank // count_x)], [keep, came], limit=16, pinned=(0,))
    return pressure, corrected, jnp.transpose(core, (3, 0, 1, 2))


def solution(mesh):
    placed = (
        P(None, "gx", "gy", "gz"),
        P("gx", "gy", "gz"),
        P("gx", None),
        P("gy", None),
        P("gz", None),
    )
    return jax.shard_map(
        per_device,
        mesh=mesh,
        in_specs=placed,
        out_specs=(P("gx", "gy", "gz"), P(None, "gx", "gy", "gz"), P("gx", None, "gy", "gz")),
        check_vma=False,
    )
```

```python
import functools
import math

import jax
import jax.numpy as jnp
from jax import lax
from jax.experimental import pallas as pl
from jax.experimental.pallas import tpu as pltpu
from jax.sharding import PartitionSpec as P

ITERS = 4
SHIFT = 0.1
AXES = ("gx", "gy", "gz")

REACH = ITERS
LAYERS = ITERS + 1
WIDE = 8
SLOT = 16
STRIP = 2 * LAYERS
SPAN = 32
ROWS = 24
NEWTON = (0.5, 0.5, 0.5)
PAIRS = [(a, b) for a in range(ITERS) for b in range(a, ITERS)]
VMEM = pl.BlockSpec(memory_space=pltpu.VMEM)
SMEM = pl.BlockSpec(memory_space=pltpu.SMEM)
HBM = pl.BlockSpec(memory_space=pltpu.HBM)
F32 = jnp.float32
BF16 = jnp.bfloat16


def call(body, outs, operands, scratch=(), smem=0, limit=12, cost=None, far_in=(), far_out=(), pinned=(), sems=0):
    scratch = [pltpu.VMEM(shape, F32) if isinstance(shape, tuple) else shape for shape in scratch]
    return pl.pallas_call(
        body,
        out_shape=[
            pltpu.HBM(shape, F32)
            if n in far_out or n in pinned
            else jax.ShapeDtypeStruct(shape, F32)
            for n, shape in enumerate(outs)
        ],
        in_specs=[SMEM if n < smem else HBM if n in far_in else VMEM for n in range(len(operands))],
        out_specs=[HBM if n in far_out else VMEM for n in range(len(outs))],
        scratch_shapes=scratch + ([pltpu.SemaphoreType.DMA((sems,))] if sems else []),
        compiler_params=pltpu.CompilerParams(vmem_limit_bytes=limit * 2**20),
        cost_estimate=cost
        and pl.CostEstimate(flops=cost[0], bytes_accessed=cost[1], transcendentals=0),
    )(
        *(
            pltpu.with_memory_space_constraint(one, pltpu.HBM)
            if n in far_in
            else one
            for n, one in enumerate(operands)
        )
    )


def cost_of(shape):
    return 4 * math.prod(shape)


def lanes(shape):
    return lax.broadcasted_iota(jnp.int32, shape, len(shape) - 1)


def sublanes(shape):
    return lax.broadcasted_iota(jnp.int32, shape, len(shape) - 2)


def exchange(up, down, axis):
    count = lax.axis_size(axis)
    ends = count - 1
    below = lax.ppermute(up, axis, [(i, i + 1) for i in range(ends)])
    above = lax.ppermute(down, axis, [(i + 1, i) for i in range(ends)])
    return below, above


def source(velocity, x, nx):
    ny, nz = velocity.shape[2:]
    shape = (ny, nz)
    before = jnp.where(x == 0, 0.0, velocity[0, jnp.maximum(x - 1, 0)])
    after = jnp.where(x == nx - 1, 0.0, velocity[0, jnp.minimum(x + 1, nx - 1)])
    along_y = velocity[1, x]
    along_z = velocity[2, x]
    total = after - before
    total = total + jnp.where(sublanes(shape) == ny - 1, 0.0, pltpu.roll(along_y, ny - 1, 0))
    total = total - jnp.where(sublanes(shape) == 0, 0.0, pltpu.roll(along_y, 1, 0))
    total = total + jnp.where(lanes(shape) == nz - 1, 0.0, pltpu.roll(along_z, nz - 1, 1))
    total = total - jnp.where(lanes(shape) == 0, 0.0, pltpu.roll(along_z, 1, 1))
    return -0.5 * total


def ring(one, two, axis, closed=True):
    count = lax.axis_size(axis)
    near = [(i, i ^ 1) for i in range(count)]
    far = [(i, (i + 1 if i % 2 else i - 1) % count) for i in range(count)]
    if not closed:
        far = [(i, j) for i, j in far if abs(i - j) == 1]
    return lax.ppermute(one, axis, near), lax.ppermute(two, axis, far)


def pack_x(index, velocity_far, inv_far, *refs):
    velocity, inv, sems = refs[-3:]
    messages = refs[:-3]
    layers, ny, nz = inv.shape[1:]
    far = inv_far.shape[0] - layers
    shape = (ny, nz)
    only = len(messages) == 1
    first = index[0] == 0

    def copies(n):
        start = jnp.where(first, far, 0) if only else (far, 0)[n]
        part = pl.ds(start, layers)
        yield pltpu.make_async_copy(inv_far.at[part], inv.at[n], sems.at[4 * n])
        for d in range(3):
            yield pltpu.make_async_copy(velocity_far.at[d, part], velocity.at[n, d], sems.at[4 * n + d + 1])

    for n in range(len(messages)):
        for copy in copies(n):
            copy.start()

    def fill(n, start, own, sign):
        message, near = messages[n], velocity.at[n]
        for k in range(REACH):
            message[k * ny : (k + 1) * ny, :] = source(near, start + k, layers)
        base = REACH * ny
        message[base : base + ny, :] = sign * near[0, own]
        base += ny
        for k in range(LAYERS):
            message[base : base + ny, :] = inv[n, k]
            base += ny
        ends = jnp.zeros(shape, F32)
        for k in range(REACH):
            plane_z = near[2, start + k]
            ends = jnp.where(lanes(shape) == 2 * k, plane_z[:, 0:1], ends)
            ends = jnp.where(lanes(shape) == 2 * k + 1, plane_z[:, nz - 1 : nz], ends)
        message[base : base + ny, :] = ends
        base += ny
        for k in range(REACH):
            message[base + 2 * k : base + 2 * k + 1, :] = near[1, start + k, 0:1, :]
            message[base + 2 * k + 1 : base + 2 * k + 2, :] = near[1, start + k, ny - 1 : ny, :]

    for n in range(len(messages)):
        for copy in copies(n):
            copy.wait()
    upper = (1, layers - 1, 0.5)
    lower = (0, 0, -0.5)
    if only:
        fill(0, *(jnp.where(first, one, two) for one, two in zip(upper, lower)))
    else:
        fill(0, *upper)
        fill(1, *lower)


class Scaled:
    def __init__(self, ref, factor):
        self.ref, self.factor = ref, factor

    def __getitem__(self, where):
        return self.ref[where] * self.factor


class Picked:
    def __init__(self, first, one, two, there):
        self.first, self.one, self.two, self.factor = first, one, two, jnp.where(there, 1.0, 0.0)

    def __getitem__(self, where):
        return jnp.where(self.first, self.one[where], self.two[where]) * self.factor


def sides(index, axis, messages):
    here, count = index[2 * axis], index[2 * axis + 1]
    same, (one, two) = here % 2 == 0, messages
    return Picked(same, two, one, here > 0), Picked(same, one, two, here < count - 1)


def sides_x(index, messages):
    if len(messages) == 2:
        return messages
    first = jnp.where(index[0] == 0, 1.0, 0.0)
    return Scaled(messages[0], 1.0 - first), Scaled(messages[0], first)


EARLY = (LAYERS + 1) // 2
EACH = REACH + 1 + LAYERS + 1


def put(up, down, pair, parity, rows_rhs, ghost, rows_inv, first, last, same=None):
    offset = parity * EACH
    row = (1, up.shape[2])

    def store(start, count, lower, upper):
        if same is not None:
            lower, upper = jnp.where(same, lower, upper), jnp.where(same, upper, lower)
        up[pair, pl.ds(offset + start, count), :] = upper
        down[pair, pl.ds(offset + start, count), :] = lower

    store(0, REACH, *rows_rhs)
    store(REACH, 1, -0.5 * ghost[0], 0.5 * ghost[1])
    store(REACH + 1, LAYERS, *rows_inv)
    both = []
    for part in range(2):
        ends = jnp.zeros(row, F32)
        for k in range(REACH):
            ends = jnp.where(lanes(row) == 2 * k, first[part][k : k + 1], ends)
            ends = jnp.where(lanes(row) == 2 * k + 1, last[part][k : k + 1], ends)
        both.append(ends)
    store(EACH - 1, 1, *both)


def put_own(up, down, velocity, inv, rhs, x, pair, parity, extra, same=None):
    ny, nz = inv.shape[1:]
    low, high = rhs[x, 0:REACH, :], rhs[x, ny - REACH : ny, :]
    if extra is not None:
        low = low + extra[pl.ds(REACH * ny, REACH), :]
        high = high + extra[pl.ds((REACH + 1) * ny - REACH, REACH), :]
    ghost = (velocity[1, x, 0:1, :], velocity[1, x, ny - 1 : ny, :])
    rows_inv = (inv[x, 0:LAYERS, :], inv[x, ny - LAYERS : ny, :])
    head, tail = velocity[2, x, 0:REACH, :], velocity[2, x, ny - REACH : ny, :]
    first = (head[:, 0:1], tail[:, 0:1])
    last = (head[:, nz - 1 : nz], tail[:, nz - 1 : nz])
    put(up, down, pair, parity, (low, high), ghost, rows_inv, first, last, same)


def pack_y_own(index, velocity, inv, rhs, up, down):
    nx = rhs.shape[0]
    same = index[2] % 2 == 0

    def plane(x, carry):
        rhs[x] = source(velocity, x, nx)
        return carry

    lax.fori_loop(0, nx, plane, 0, unroll=4)

    def planes(n, carry):
        for parity in range(2):
            put_own(up, down, velocity, inv, rhs, 1 + 2 * n + parity, n, parity, None, same)
        return carry

    lax.fori_loop(0, up.shape[0], planes, 0, unroll=3)


def pack_y_halo(index, velocity, inv, rhs, *refs):
    (below, above), (up, down) = sides_x(index, refs[:-2]), refs[-2:]
    same = index[2] % 2 == 0
    nx, ny, nz = inv.shape
    skip = (nx + 2 * LAYERS) // 2 - 2 * EARLY

    def halo(x, message, k_rhs, k_inv, extra):
        pair = x // 2 if x // 2 < EARLY else x // 2 - skip
        base = (REACH + 1 + k_inv) * ny
        rows_inv = (message[pl.ds(base, LAYERS), :], message[pl.ds(base + ny - LAYERS, LAYERS), :])
        zero_row = jnp.zeros((1, nz), F32)
        zero = jnp.zeros((REACH, nz), F32)
        if k_rhs is None:
            column = jnp.zeros((REACH, 1), F32)
            put(up, down, pair, x % 2, (zero, zero), (zero_row, zero_row), rows_inv, (column, column), (column, column), same)
            return
        low, high = message[pl.ds(k_rhs * ny, REACH), :], message[pl.ds((k_rhs + 1) * ny - REACH, REACH), :]
        if extra is not None:
            sign, source = extra
            low = low + sign * velocity[0, source, 0:REACH, :]
            high = high + sign * velocity[0, source, ny - REACH : ny, :]
        ends = (REACH + 1 + LAYERS) * ny
        lines = ends + ny + 2 * k_rhs
        ghost = (message[pl.ds(lines, 1), :], message[pl.ds(lines + 1, 1), :])
        head, tail = message[pl.ds(ends, REACH), :], message[pl.ds(ends + ny - REACH, REACH), :]
        first = (head[:, 2 * k_rhs : 2 * k_rhs + 1], tail[:, 2 * k_rhs : 2 * k_rhs + 1])
        last = (head[:, 2 * k_rhs + 1 : 2 * k_rhs + 2], tail[:, 2 * k_rhs + 1 : 2 * k_rhs + 2])
        put(up, down, pair, x % 2, (low, high), ghost, rows_inv, first, last, same)

    for k in range(LAYERS):
        halo(k, below, k - 1 if k else None, k, (-0.5, 0) if k == LAYERS - 1 else None)
        halo(
            nx + LAYERS + k,
            above,
            k if k < REACH else None,
            k,
            (0.5, nx - 1) if k == 0 else None,
        )
    put_own(up, down, velocity, inv, rhs, 0, EARLY - 1, 1, below, same)
    put_own(up, down, velocity, inv, rhs, nx - 1, EARLY, 0, above, same)


def pack_z(index, velocity, inv, rhs, *refs):
    (below, above), received = sides_x(index, refs[:-16]), refs[-16:-12]
    received = [*sides(index, 1, received[:2]), *sides(index, 1, received[2:])]
    same = index[4] % 2 == 0
    rhs_far, inv_far, up, down, strip_rhs_far, strip_inv_far = refs[-12:-6]
    rhs_wide, inv_wide, ends, strip_rhs, strip_inv, sems = refs[-6:]
    nx, ny, nz = inv.shape
    wide = nx + 2 * LAYERS
    rows = ny + 2 * WIDE
    mine = pl.ds(WIDE, ny)
    edge = (WIDE, nz)
    groups = strip_rhs.shape[0]

    for k in range(LAYERS):
        for message, x, layer in ((below, k, k - 1), (above, nx + LAYERS + k, k if k < REACH else -1)):
            base = (REACH + 1 + k) * ny
            inv_wide[x, mine, :] = message[pl.ds(base, ny), :]
            if layer < 0:
                rhs_wide[x, mine, :] = jnp.zeros((ny, nz), F32)
                ends[x, mine, :] = jnp.zeros((ny, nz), F32)
                continue
            part = message[pl.ds(layer * ny, ny), :]
            if x == LAYERS - 1:
                part = part - 0.5 * velocity[0, 0]
            if x == nx + LAYERS:
                part = part + 0.5 * velocity[0, nx - 1]
            rhs_wide[x, mine, :] = part
            line = message[pl.ds((REACH + 1 + LAYERS) * ny, ny), :]
            ends[x, mine, :] = jnp.where(
                lanes((ny, nz)) == 0, line[:, 2 * layer : 2 * layer + 1], line[:, 2 * layer + 1 : 2 * layer + 2]
            )

    def plane(x, carry):
        inv_wide[x + LAYERS, mine, :] = inv[x]
        rhs_wide[x + LAYERS, mine, :] = rhs[x]
        ends[x + LAYERS, mine, :] = velocity[2, x]
        return carry

    lax.fori_loop(0, nx, plane, 0, unroll=4)
    rhs_wide[LAYERS, mine, :] += below[pl.ds(REACH * ny, ny), :]
    rhs_wide[LAYERS + nx - 1, mine, :] += above[pl.ds(REACH * ny, ny), :]
    for ref in (rhs_wide, inv_wide, ends):
        for x in range(wide, ref.shape[0]):
            ref[x] = jnp.zeros((rows, nz), F32)

    def finish(x, ghost_low, ghost_high):
        pair = x // 2
        if not isinstance(x, int):
            low, high = (ref[pair - EARLY] for ref in received[:2])
        else:
            pair = pair if pair < EARLY else pair - (wide // 2 - 2 * EARLY)
            low, high = (ref[pair] for ref in received[2:])
        low = jnp.where(x % 2 == 0, low, pltpu.roll(low, ROWS - EACH, 0))[0:SLOT]
        high = jnp.where(x % 2 == 0, high, pltpu.roll(high, ROWS - EACH, 0))[0:SLOT]
        part = pltpu.roll(low, WIDE - REACH, 0)[0:WIDE]
        part = jnp.where(sublanes(edge) >= WIDE - REACH, part, 0.0)
        part = part - jnp.where(sublanes(edge) == WIDE - 1, 0.5 * ghost_low, 0.0)
        rhs_wide[x, 0:WIDE, :] = part
        part = pltpu.roll(low, SLOT - (REACH + 1) + WIDE - LAYERS, 0)[0:WIDE]
        inv_wide[x, 0:WIDE, :] = jnp.where(sublanes(edge) >= WIDE - LAYERS, part, 0.0)
        part = jnp.where(sublanes(edge) < REACH, high[0:WIDE], 0.0)
        part = part + jnp.where(sublanes(edge) == 0, 0.5 * ghost_high, 0.0)
        rhs_wide[x, WIDE + ny : rows, :] = part
        part = pltpu.roll(high, SLOT - (REACH + 1), 0)[0:WIDE]
        inv_wide[x, WIDE + ny : rows, :] = jnp.where(sublanes(edge) < LAYERS, part, 0.0)
        head = rhs_wide[x, WIDE : 2 * WIDE, :]
        rhs_wide[x, WIDE : 2 * WIDE, :] = head + jnp.where(sublanes(edge) == 0, low[REACH : REACH + 1], 0.0)
        tail = rhs_wide[x, ny : WIDE + ny, :]
        rhs_wide[x, ny : WIDE + ny, :] = tail + jnp.where(
            sublanes(edge) == WIDE - 1, high[REACH : REACH + 1], 0.0
        )
        for message, start, place in ((low, WIDE - REACH, 0), (high, 0, WIDE + ny)):
            line = message[EACH - 1 : EACH]
            one = jnp.zeros(edge, F32)
            two = jnp.zeros(edge, F32)
            for k in range(REACH):
                here = sublanes(edge) == start + k
                one = jnp.where(here, line[:, 2 * k : 2 * k + 1], one)
                two = jnp.where(here, line[:, 2 * k + 1 : 2 * k + 2], two)
            ends[x, place : place + WIDE, :] = jnp.where(lanes(edge) == 0, one, two)

    for k in range(LAYERS):
        for message, x, layer in ((below, k, k - 1), (above, nx + LAYERS + k, k if k < REACH else -1)):
            lines = (REACH + 1 + LAYERS + 1) * ny + 2 * layer
            if layer < 0:
                zero = jnp.zeros((1, nz), F32)
                finish(x, zero, zero)
            else:
                finish(x, message[pl.ds(lines, 1), :], message[pl.ds(lines + 1, 1), :])

    def middle(x, carry):
        finish(x + LAYERS, velocity[1, x, 0:1, :], velocity[1, x, ny - 1 : ny, :])
        return carry

    lax.fori_loop(1, nx - 1, middle, 0, unroll=10)
    for x in (0, nx - 1):
        finish(x + LAYERS, velocity[1, x, 0:1, :], velocity[1, x, ny - 1 : ny, :])
    copies = [
        pltpu.make_async_copy(ref.at[pl.ds(0, wide)], far, sems.at[n])
        for n, (ref, far) in enumerate(((rhs_wide, rhs_far), (inv_wide, inv_far)))
    ]
    for copy in copies:
        copy.start()

    whole = (rows, nz)
    lane = lanes(whole)
    place = lane % SPAN

    def back(value, step):
        return pltpu.roll(value, nz - step, 1)

    def gather(ref, g):
        value = None
        for n in range(nz // SPAN):
            moved = pltpu.roll(ref[g + n * groups], n * SPAN + STRIP, 1)
            value = moved if value is None else jnp.where(lane >= n * SPAN, moved, value)
        return value

    def pack(g):
        r, i, e = gather(rhs_wide, g), gather(inv_wide, g), gather(ends, g)
        apart = SPAN - 2 * STRIP
        for ref, value in ((strip_rhs, r), (strip_inv, i)):
            out = jnp.where(place < STRIP, value, 0.0)
            ref[g] = jnp.where(place >= SPAN - STRIP, pltpu.roll(value, apart, 1), out)
        ghost = jnp.where(place == STRIP, 0.5 * pltpu.roll(e, 1, 1), 0.0)
        ghost = jnp.where(place == SPAN - STRIP - 1, -0.5 * pltpu.roll(e, apart - 1, 1), ghost)
        strip_rhs[g] += ghost
        out = jnp.where(place < REACH, back(r, STRIP - REACH), 0.0)
        out = jnp.where(place == REACH, 0.5 * back(e, STRIP - 1 - REACH), out)
        here = (place > REACH) & (place <= REACH + LAYERS)
        higher = jnp.where(here, pltpu.roll(i, (nz + REACH + 1 + LAYERS - STRIP) % nz, 1), out)
        out = jnp.where(place < REACH, back(r, STRIP), 0.0)
        out = jnp.where(place == REACH, -0.5 * back(e, STRIP - REACH), out)
        return higher, jnp.where(here, back(i, STRIP - REACH - 1), out)

    halves = up.shape[0]

    def both(n, carry):
        one, two = pack(n)
        up[n] = jnp.where(same, one, two)
        down[n] = jnp.where(same, two, one)
        return carry

    lax.fori_loop(0, halves, both, 0, unroll=2)

    def more(n, carry):
        one, two = pack(n + halves)
        up[n] += pltpu.roll(jnp.where(same, one, two), SPAN // 2, 1)
        down[n] += pltpu.roll(jnp.where(same, two, one), SPAN // 2, 1)
        return carry

    lax.fori_loop(0, groups - halves, more, 0, unroll=2)
    for ref, far in ((strip_rhs, strip_rhs_far), (strip_inv, strip_inv_far)):
        copies.append(pltpu.make_async_copy(ref, far, sems.at[len(copies)]))
        copies[-1].start()
    for copy in copies:
        copy.wait()


def shifted(ref, x, t, step):
    rows = ref.shape[1]
    start = t * WIDE + step
    if start < 0:
        return pltpu.roll(ref[x, 0:WIDE, :], 1, 0)
    if start + WIDE > rows:
        return pltpu.roll(ref[x, rows - WIDE : rows, :], WIDE - 1, 0)
    return ref[x, start : start + WIDE, :]


class Stencil:
    def __init__(self, inv, root, ax, ay, az, vs, planes, edges=None, unroll=6):
        self.inv, self.root, self.ax, self.ay, self.az, self.vs = inv, root, ax, ay, az, vs
        self.planes, self.edges, self.unroll = planes, edges or (lambda ref: None), unroll
        self.count, self.rows, self.nz = inv.shape
        self.tiles = self.rows // WIDE

    def here(self, t):
        return slice(t * WIDE, (t + 1) * WIDE)

    def right(self, value):
        return pltpu.roll(value, self.nz - 1, 1)

    def left(self, value):
        return pltpu.roll(value, 1, 1)

    def prepare(self, rhs, parts=None):
        inv, root = self.inv, self.root
        self.edges(inv)

        def scales(x, carry):
            writes = []
            for t in range(self.tiles):
                here = self.here(t)
                c = inv[x, here, :]
                total = (inv[x + 1, here, :] + inv[x - 1, here, :]) + (self.right(c) + self.left(c))
                total = total + (shifted(inv, x, t, 1) + shifted(inv, x, t, -1))
                value = jnp.where(c > 0.0, lax.rsqrt(SHIFT + 0.5 * (6.0 * c + total)), 0.0)
                writes.append((here, value, rhs[x, here, :] * value))
            for here, one, two in writes:
                root[x, here, :] = one
                self.vs[0][x, here, :] = two
            return carry

        for start, stop in parts or [(1, self.count - 1)]:
            lax.fori_loop(start, stop, scales, 0, unroll=self.unroll)
        zero = jnp.zeros((self.rows, self.nz), F32)
        for ref in (root, self.vs[0]):
            ref[0] = zero
            ref[self.count - 1] = zero
            self.edges(ref)

        def couplings(x, carry):
            writes = []
            for t in range(self.tiles):
                here = self.here(t)
                c, d = inv[x, here, :], root[x, here, :]
                half = 0.5 * d
                writes.append(
                    (
                        here,
                        (c + inv[x + 1, here, :]) * (half * root[x + 1, here, :]),
                        (c + shifted(inv, x, t, 1)) * (half * shifted(root, x, t, 1)),
                        (c + self.right(c)) * (half * self.right(d)),
                    )
                )
            for here, x_face, y_face, z_face in writes:
                self.ax[x, here, :] = x_face
                self.ay[x, here, :] = y_face
                self.az[x, here, :] = z_face
            return carry

        lax.fori_loop(1, self.count - 1, couplings, 0, unroll=self.unroll)
        self.ax[0] = zero
        self.edges(self.ax)

    def couple(self, k, x, t):
        here = self.here(t)
        v, ax, ay = self.vs[k], self.ax, self.ay
        c, f = v[x, here, :], self.az[x, here, :]
        total = ax[x, here, :] * v[x + 1, here, :] + ax[x - 1, here, :] * v[x - 1, here, :]
        total = total + (f * self.right(c) + self.left(f * c))
        total = total + ay[x, here, :] * shifted(v, x, t, 1)
        return c, total + shifted(ay, x, t, -1) * shifted(v, x, t, -1)

    def extend(self, k):
        scale = 1.0 - NEWTON[k]

        def step(x, carry):
            writes = []
            for t in range(self.tiles):
                c, total = self.couple(k, x, t)
                writes.append((t, scale * c - total if scale else -total))
            for t, value in writes:
                self.vs[k + 1][x, self.here(t), :] = value
            return carry

        start, stop = self.planes(k)
        lax.fori_loop(start, stop, step, 0, unroll=self.unroll)
        self.edges(self.vs[k + 1])

    def products(self, start, stop, mask):
        def measure(x, sums):
            sums = list(sums)
            for t in range(1, self.tiles - 1):
                keep = mask(x)
                v = [self.vs[k][x, self.here(t), :] for k in range(ITERS)]
                own, total = self.couple(ITERS - 1, x, t)
                kept = [jnp.where(keep, one, 0.0) for one in v]
                for n, (a, b) in enumerate(PAIRS):
                    sums[n] = sums[n] + v[a] * kept[b]
                sums[-1] = sums[-1] + kept[-1] * (own - total)
            return tuple(sums)

        zero = jnp.zeros((WIDE, self.nz), F32)
        return lax.fori_loop(start, stop, measure, (zero,) * (len(PAIRS) + 1), unroll=4)


def basis_main(rhs_far, inv_far, *refs):
    outs, sums = refs[: ITERS + 1], refs[ITERS + 1]
    rhs, inv, root, ax, ay, az = refs[ITERS + 2 : ITERS + 8]
    vs, sems = refs[ITERS + 8 : -1], refs[-1]
    wide, rows, nz = ax.shape
    nx = wide - 2 * LAYERS
    batch = 4
    bounds = [n * wide // batch for n in range(batch + 1)]
    loads = []
    for n in range(batch):
        part = pl.ds(bounds[n], bounds[n + 1] - bounds[n])
        for far, ref in ((inv_far, inv), (rhs_far, rhs)):
            loads.append(pltpu.make_async_copy(far.at[part], ref.at[part], sems.at[ITERS + 1 + len(loads)]))
            loads[-1].start()

    def ready():
        for n in range(batch):
            for load in loads[2 * n : 2 * n + 2]:
                load.wait()
            yield max(bounds[n] - 1, 1), bounds[n + 1] - 1

    stencil = Stencil(inv, root, ax, ay, az, vs, lambda k: (2 + k, wide - 2 - k))
    copies = []

    def send(n, ref):
        copy = pltpu.make_async_copy(ref.at[pl.ds(LAYERS - 1, nx + 2)], outs[n], sems.at[n])
        copy.start()
        copies.append(copy)

    stencil.prepare(rhs, ready())
    send(ITERS, root)
    send(0, vs[0])
    for k in range(ITERS - 1):
        stencil.extend(k)
        send(k + 1, vs[k + 1])
    lane = lanes((WIDE, nz))
    inner = (lane > REACH) & (lane < nz - 1 - REACH)
    for n, one in enumerate(stencil.products(LAYERS, LAYERS + nx, lambda x: inner)):
        sums[n] = one
    for copy in copies:
        copy.wait()


def basis_strips(nx, index, rhs_far, inv_far, one, two, sums, *refs):
    before, after = sides(index, 2, (one, two))
    outs, dots = refs[:ITERS], refs[ITERS]
    rhs, inv, root, ax, ay, az = refs[ITERS + 1 : ITERS + 7]
    vs, outs_near = refs[ITERS + 7 : 2 * ITERS + 7], refs[2 * ITERS + 7 : 3 * ITERS + 7]
    strip_rhs, strip_inv, sems = refs[-3:]
    groups, rows, nz = strip_inv.shape
    loads = [
        pltpu.make_async_copy(far, ref, sems.at[ITERS + n])
        for n, (far, ref) in enumerate(((rhs_far, strip_rhs), (inv_far, strip_inv)))
    ]
    for load in loads:
        load.start()
    for load in loads:
        load.wait()
    halves = one.shape[0]
    whole = (rows, nz)
    place = lanes(whole) % SPAN

    def edges(ref):
        ref[0] = pltpu.roll(ref[groups], SPAN, 1)
        ref[groups + 1] = pltpu.roll(ref[1], nz - SPAN, 1)

    def receive(g, low, high):
        start = SPAN - STRIP - LAYERS
        moved = pltpu.roll(low, start + 1, 1)
        r = strip_rhs[g] + jnp.where((place > start) & (place <= SPAN - STRIP), moved, 0.0)
        moved = pltpu.roll(low, start - REACH - 1, 1)
        i = strip_inv[g] + jnp.where((place >= start) & (place < SPAN - STRIP), moved, 0.0)
        moved = pltpu.roll(high, STRIP, 1)
        r = r + jnp.where((place >= STRIP) & (place < STRIP + REACH), moved, 0.0)
        moved = pltpu.roll(high, STRIP - REACH - 1, 1)
        r = r + jnp.where(place == STRIP - 1, moved, 0.0)
        i = i + jnp.where((place >= STRIP) & (place < STRIP + LAYERS), moved, 0.0)
        rhs[g + 1] = r
        inv[g + 1] = i

    def first(n, carry):
        receive(n, before[n], after[n])
        return carry

    def second(n, carry):
        half = nz - SPAN // 2
        receive(n + halves, pltpu.roll(before[n], half, 1), pltpu.roll(after[n], half, 1))
        return carry

    lax.fori_loop(0, halves, first, 0, unroll=3)
    lax.fori_loop(0, groups - halves, second, 0, unroll=3)
    stencil = Stencil(inv, root, ax, ay, az, vs, lambda k: (1, groups + 1), edges, groups)
    stencil.prepare(rhs)
    copies = []

    def result(k):
        ref = outs_near[k]

        def plane(g, carry):
            ref[g] = vs[k][g] * root[g]
            return carry

        lax.fori_loop(1, groups + 1, plane, 0, unroll=groups)
        copies.append(pltpu.make_async_copy(ref.at[pl.ds(1, groups)], outs[k], sems.at[k]))
        copies[-1].start()

    result(0)
    for k in range(ITERS - 1):
        stencil.extend(k)
        result(k + 1)
    lane = lanes((WIDE, nz))
    part = lane // SPAN
    spot = lane % SPAN
    ends = ((spot >= STRIP - LAYERS) & (spot < STRIP)) | (
        (spot >= SPAN - STRIP) & (spot < SPAN - STRIP + LAYERS)
    )

    def mask(x):
        plane = x - 1 + part * groups
        return ends & (plane >= LAYERS) & (plane < LAYERS + nx)

    totals = []
    for n, one in enumerate(stencil.products(1, groups + 1, mask)):
        line = jnp.sum(one + sums[n], axis=0, keepdims=True)
        totals.append(line + pltpu.roll(line, nz // 2, 1))
    row = sublanes((WIDE, nz))
    message = jnp.zeros((WIDE, nz), F32)
    for n, line in enumerate(totals):
        half = lane < nz // 2 if n < WIDE else lane >= nz // 2
        message = jnp.where((row == n % WIDE) & half, line, message)

    def send(n, carry):
        dots[n] = message
        return carry

    lax.fori_loop(0, dots.shape[0], send, 0, unroll=8)

    for copy in copies:
        copy.wait()


def coefficients(dots):
    half = lanes(dots.shape) < dots.shape[1] // 2
    one = jnp.sum(jnp.where(half, dots, 0.0), axis=1, keepdims=True)
    two = jnp.sum(jnp.where(half, 0.0, dots), axis=1, keepdims=True)

    def entry(n):
        return one[n : n + 1] if n < WIDE else two[n - WIDE : n - WIDE + 1]

    gram = {}
    for n, (a, b) in enumerate(PAIRS):
        gram[a, b] = gram[b, a] = entry(n)
    last = ITERS - 1
    image = {}
    for b in range(last):
        for a in range(ITERS):
            image[a, b] = gram[a, b + 1]
            if NEWTON[b]:
                image[a, b] = image[a, b] + NEWTON[b] * gram[a, b]
    for a in range(last):
        image[a, last] = image[last, a]
    image[last, last] = entry(len(PAIRS))

    def product(table, one, two):
        total = None
        for a, left in enumerate(one):
            for b, right in enumerate(two):
                term = left * right * table[a, b]
                total = term if total is None else total + term
        return total

    unit = jnp.ones((1, 1), F32)
    pressure = []
    precond = [unit]
    direction = [unit]
    rz = gram[0, 0]
    for iteration in range(ITERS):
        alpha = rz / product(image, direction, direction)
        pressure = [
            (pressure[n] if n < len(pressure) else 0.0) + alpha * one for n, one in enumerate(direction)
        ]
        if iteration == last:
            break
        moved = []
        for n in range(len(direction) + 1):
            value = None
            if n < len(direction) and NEWTON[n]:
                value = NEWTON[n] * direction[n]
            if n > 0:
                value = direction[n - 1] if value is None else value + direction[n - 1]
            moved.append(value)
        fresh_precond = []
        for n, one in enumerate(moved):
            old = precond[n] if n < len(precond) else None
            if one is None:
                fresh_precond.append(old)
            else:
                fresh_precond.append(-alpha * one if old is None else old - alpha * one)
        precond = fresh_precond
        fresh = product(gram, precond, precond)
        beta = fresh / rz
        direction = [
            one + beta * direction[n] if n < len(direction) else one for n, one in enumerate(precond)
        ]
        rz = fresh
    return pressure


def finish(dots, columns, *refs):
    inputs = 2 * ITERS + 3
    pressure_far, corrected_far, keep, keep_more, send, p, gaps, mixed, cut, pressure, corrected = refs[inputs : inputs + 11]
    held, sems = refs[inputs + 11 : -1], refs[-1]
    strips, spans, roots = held[:ITERS], held[ITERS : 2 * ITERS], held[2 * ITERS]
    velocity, inv = held[2 * ITERS + 1 :]
    nx, ny, nz = inv.shape
    batch = 4
    each = nx // batch
    used = 0

    def start(far, ref):
        nonlocal used
        copy = pltpu.make_async_copy(far, ref, sems.at[used])
        used += 1
        copy.start()
        return copy

    strip_loads = [start(far, ref) for far, ref in zip(refs[:ITERS], strips)]
    span_loads, other_loads, bounds = [], [], []
    for n in range(batch):
        low, high = (n * each + 2 if n else 0), (n + 1) * each + 2
        bounds.append((low, high))
        part = pl.ds(low, high - low)
        pairs = zip(refs[ITERS : 2 * ITERS + 1], held[ITERS : 2 * ITERS + 1])
        span_loads.append([start(far.at[part], ref.at[part]) for far, ref in pairs])
        part = pl.ds(n * each, each)
        other_loads.append(
            [start(refs[2 * ITERS + 1].at[d, part], velocity.at[d, part]) for d in range(3)]
            + [start(refs[2 * ITERS + 2].at[part], inv.at[part])]
        )
    shape = (ny, nz)
    groups = mixed.shape[0]
    total = dots[0]
    for n in range(1, dots.shape[0]):
        total = total + dots[n]
    weights = coefficients(total)

    def strip(g, carry):
        value = weights[0] * strips[0][g]
        for k in range(1, ITERS):
            value = value + weights[k] * strips[k][g]
        mixed[g] = value
        return carry

    for load in strip_loads:
        load.wait()
    lax.fori_loop(0, groups, strip, 0, unroll=4)
    mine = slice(WIDE, WIDE + ny)
    lane = lanes(spans[0].shape[1:])

    def combine(x, carry):
        value = weights[0] * spans[0][x]
        for k in range(1, ITERS):
            value = value + weights[k] * spans[k][x]
        value = value * roots[x]
        plane = x + LAYERS - 1
        ends = mixed[plane % groups]
        start = plane // groups * SPAN
        last = pltpu.roll(ends, lax.rem(2 * nz - STRIP - start, nz), 1)
        first = pltpu.roll(ends, lax.rem(nz + STRIP - SPAN - start + nz, nz), 1)
        value = jnp.where(lane < LAYERS, first, jnp.where(lane >= nz - LAYERS, last, value))
        p[x] = value
        after = pltpu.roll(jnp.where(lane == 0, last, value), nz - 1, 1)
        before = pltpu.roll(jnp.where(lane == nz - 1, first, value), 1, 1)
        gaps[x] = (after - before)[mine]
        return carry

    half = columns.shape[0] // 2

    def pair(n, carry):
        for which in range(2):
            x = 2 * n + which
            centre = p[x + 1, mine, :]
            pressure[x] = centre
            half_inv = 0.5 * inv[x]
            slopes = (
                p[x + 2, mine, :] - p[x, mine, :],
                p[x + 1, WIDE + 1 : WIDE + 1 + ny, :] - p[x + 1, WIDE - 1 : WIDE - 1 + ny, :],
                gaps[x + 1],
            )
            fields = [velocity[d, x] - half_inv * slopes[d] for d in range(3)] + [centre]
            for d in range(3):
                corrected[d, x] = fields[d]
            for f, field in enumerate(fields):
                high = field.astype(BF16)
                low = (field - high.astype(F32)).astype(BF16)
                cut[f, which * ny : (which + 1) * ny, 0:nz] = high
                cut[f, which * ny : (which + 1) * ny, nz : 2 * nz] = low
        for f in range(4):
            out = lax.dot_general(
                columns[...], cut[f], (((1,), (1,)), ((), ())), preferred_element_type=F32
            )
            out = out[:half] + out[half:]
            block = f * (nx // 2) + n
            quarter = half // 4
            keep[block] = out[0:quarter]
            keep_more[block] = out[quarter : 2 * quarter]
            send[0, block] = out[2 * quarter : 3 * quarter]
            send[1, block] = out[3 * quarter :]
        return carry

    stores = []
    for n in range(batch):
        for load in span_loads[n]:
            load.wait()
        lax.fori_loop(*bounds[n], combine, 0, unroll=4)
        for load in other_loads[n]:
            load.wait()
        lax.fori_loop(n * each // 2, (n + 1) * each // 2, pair, 0, unroll=4)
        part = pl.ds(n * each, each)
        stores.append(start(pressure.at[part], pressure_far.at[part]))
        for d in range(3):
            stores.append(start(corrected.at[d, part], corrected_far.at[d, part]))
    for store in stores:
        store.wait()


def tables(count_x, factor_y, factor_x, y_high, y_low, x_high, x_low, spread_high, spread_low):
    ny, rank = factor_y.shape
    nx = factor_x.shape[0]
    planes = y_high.shape[0] // ny
    nz = x_high.shape[1] // rank * planes
    count = y_high.shape[1] // nz
    ranks = rank // count
    wide = jnp.concatenate([factor_y[...], jnp.zeros((ny, nz - rank), F32)], axis=1)
    lane = lanes((ny, nz))
    for h in range(count):
        value = pltpu.roll(wide, (nz - h * ranks) % nz, 1)
        value = jnp.where(lane < ranks, value, 0.0)
        step = ranks
        while step < nz:
            value = value + pltpu.roll(value, step, 1)
            step *= 2
        for n in range(planes):
            high, low = split(jnp.where(lane // ranks == n, value, 0.0))
            y_high[n * ny : (n + 1) * ny, h * nz : (h + 1) * nz] = high
            y_low[n * ny : (n + 1) * ny, h * nz : (h + 1) * nz] = low
    width = x_high.shape[1]
    shape = (rank, width)
    own = rank // count_x
    lane = lanes(shape)
    copy = lane // (ranks * own) * own + lane % own == sublanes(shape)
    copy = jnp.where(copy, 1.0, 0.0).astype(BF16)
    for ref, value in zip((spread_high, spread_low), split(factor_x[...])):
        ref[...] = jnp.dot(value, copy, preferred_element_type=F32)
    shape = (ranks, width)
    here = lanes(shape) // own % ranks == sublanes(shape)

    def row(i, carry):
        at = pl.ds(pl.multiple_of(i * ranks, ranks), ranks)
        x_high[at, :] = jnp.where(here, spread_high[pl.ds(i, 1), :], 0.0).astype(BF16)
        x_low[at, :] = jnp.where(here, spread_low[pl.ds(i, 1), :], 0.0).astype(BF16)
        return carry

    lax.fori_loop(0, nx, row, 0, unroll=4)


def split(value):
    high = value.astype(BF16)
    return high, (value - high.astype(F32)).astype(BF16)


def split_table(value):
    high = lax.reduce_precision(value, exponent_bits=8, mantissa_bits=7)
    return high.astype(BF16), (value - high).astype(BF16)


def three(a, b, dims=(((1,), (0,)), ((), ()))):
    dot = functools.partial(lax.dot_general, dimension_numbers=dims, preferred_element_type=F32)
    (ah, al), (bh, bl) = a, b
    return dot(ah, bh) + (dot(al, bh) + dot(ah, bl))


def rank_y(x, table):
    blocks, ranks, nz = x.shape
    group = table[0].shape[0] // nz
    parts = [
        jnp.concatenate([x[n * group + q] for q in range(group)], axis=1) for n in range(blocks // group)
    ]
    out = three(split(jnp.concatenate(parts, axis=0)), table)
    return [out[:, n * nz : (n + 1) * nz] for n in range(out.shape[1] // nz)]


def tail_one(kept, more, came, high, low, p_send, p_keep, q_send, q_keep, q_more):
    half = kept.shape[0] // 2
    p_send[...] = more[0:half] + came[1, 0:half]
    p_keep[...] = kept[0:half] + came[0, 0:half]
    x = jnp.concatenate([kept[half:] + came[0, half:], more[half:] + came[1, half:]], axis=0)
    q_keep[...], q_more[...], q_send[0], q_send[1] = rank_y(x, (high[...], low[...]))


def tail_two(p_kept, p_came, q_kept, q_more, q_came, high, low, p_send, p_keep, p_more, q_send, q_keep):
    q_send[...] = q_more[...] + q_came[1]
    q_keep[...] = q_kept[...] + q_came[0]
    parts = rank_y(p_kept[...] + p_came[...], (high[...], low[...]))
    p_keep[...], p_more[...], p_send[0], p_send[1] = parts


def tail_three(p_kept, p_more, p_came, q_kept, q_came, p_send, p_keep, q_send, q_keep):
    half = q_keep.shape[0]
    p_send[...] = p_more[...] + p_came[1]
    p_keep[...] = p_kept[...] + p_came[0]
    q_send[...] = q_kept[half:] + q_came[half:]
    q_keep[...] = q_kept[0:half] + q_came[0:half]


def rank_x(ranks, p_kept, p_came, q_kept, q_came, wide_high, wide_low, *outs):
    u = jnp.concatenate([p_kept[...] + p_came[...], q_kept[...] + q_came[...]], axis=0)
    rows, nz = u.shape
    group = wide_high.shape[0] // nz
    parts = []
    for f in range(rows // ranks // group):
        parts.append(
            jnp.concatenate(
                [u[(f * group + q) * ranks : (f * group + q + 1) * ranks] for q in range(group)], axis=1
            )
        )
    x = jnp.concatenate(parts, axis=0)
    out = three(split(x), (wide_high[...], wide_low[...]))
    width = out.shape[1] // len(outs)
    for n, ref in enumerate(outs):
        ref[...] = out[:, n * width : (n + 1) * width]


def last_core(kept, came, core):
    fields, ranks_y, ranks_z, ranks_x = core.shape
    z = kept[...] + came[...]
    for f in range(fields):
        for b in range(ranks_y):
            core[f, b] = z[f * ranks_z : (f + 1) * ranks_z, b * ranks_x : (b + 1) * ranks_x]


def relative(factor, axis):
    count = lax.axis_size(axis)
    order = [0]
    step = 1
    while step < count:
        order = order + [n + step for n in order]
        step *= 2
    bits = count.bit_length() - 1
    order = [sum(((n >> b) & 1) << (bits - 1 - b) for b in range(bits)) for n in range(count)]
    blocks = factor.reshape(factor.shape[0], count, factor.shape[1] // count)
    here = lax.axis_index(axis)
    picked = [
        lax.dynamic_index_in_dim(blocks, jnp.bitwise_xor(here, n), axis=1, keepdims=False) for n in order
    ]
    return jnp.stack(picked, axis=1)


def swap(value, axis, mask):
    count = lax.axis_size(axis)
    return lax.ppermute(value, axis, [(i, i ^ mask) for i in range(count)])


def per_device(velocity, inv_density, factor_x, factor_y, factor_z):
    nx, ny, nz = inv_density.shape
    wide, rows = nx + 2 * LAYERS, ny + 2 * WIDE
    count_x, count_y, count_z = (lax.axis_size(axis) for axis in AXES)
    devices = count_x * count_y * count_z
    cells = (nx, ny, nz)
    rank = factor_x.shape[1]
    index_x = lax.axis_index("gx").reshape(1)
    index = jnp.stack([jnp.int32(f(axis)) for axis in AXES for f in (lax.axis_index, lax.axis_size)])

    shape = (((REACH + 1 + LAYERS + 1) * ny + 2 * REACH), nz)
    number = 1 if count_x == 2 else 2
    sent = call(
        pack_x,
        [shape] * number,
        [index_x, velocity, inv_density],
        scratch=[(number, 3, LAYERS, ny, nz), (number, LAYERS, ny, nz)],
        smem=1,
        far_in=(1, 2),
        sems=4 * number,
    )
    near = [swap(sent[0], "gx", 1)] if count_x == 2 else list(exchange(*sent, "gx"))
    pairs = wide // 2 - 2 * EARLY
    shape = (pairs, ROWS, nz)
    rhs, up, down = call(
        pack_y_own,
        [cells, shape, shape],
        [index, velocity, inv_density],
        smem=1,
        cost=(nx * ny * nz * 10, 6 * cost_of(cells)),
    )
    received = list(ring(up, down, "gy", closed=False))
    shape = (2 * EARLY, ROWS, nz)
    up, down = call(pack_y_halo, [shape, shape], [index, velocity, inv_density, rhs, *near], smem=1)
    received += ring(up, down, "gy")
    parts = nz // SPAN
    groups = -(-wide // parts)
    message = (-(-groups // 2), rows, nz)
    whole = (groups * parts, rows, nz)
    strip = (groups, rows, nz)
    rhs_wide, inv_wide, up, down, strip_rhs, strip_inv = call(
        pack_z,
        [(wide, rows, nz)] * 2 + [message, message, strip, strip],
        [index, velocity, inv_density, rhs, *near, *received],
        scratch=[whole] * 3 + [strip] * 2,
        smem=1,
        limit=18,
        far_out=(0, 1, 4, 5),
        sems=4,
    )
    came = ring(up, down, "gz")
    span = (nx + 2, rows, nz)
    whole = (wide, rows, nz)
    *spans, sums = call(
        basis_main,
        [span] * (ITERS + 1) + [(len(PAIRS) + 1, WIDE, nz)],
        [rhs_wide, inv_wide],
        scratch=[whole] * (6 + ITERS),
        limit=22,
        cost=(wide * rows * nz * 100, 7 * cost_of(whole)),
        far_in=(0, 1),
        far_out=range(ITERS + 1),
        sems=ITERS + 9,
    )
    padded = (groups + 2, rows, nz)
    *strips, dots = call(
        functools.partial(basis_strips, nx),
        [strip] * ITERS + [(devices, WIDE, nz)],
        [index, strip_rhs, strip_inv, *came, sums],
        scratch=[padded] * (6 + 2 * ITERS) + [strip] * 2,
        smem=1,
        far_in=(1, 2),
        far_out=range(ITERS),
        sems=ITERS + 2,
    )
    dots = lax.all_to_all(dots, AXES, 0, 0, tiled=True)

    ranks_y, ranks_z = rank // count_y, rank // count_z
    planes = nz // ranks_y
    table_y, table_x = (planes * ny, count_y * nz), (nx * ranks_y, rank * ranks_y)
    y_high, y_low, x_high, x_low = pl.pallas_call(
        functools.partial(tables, count_x),
        out_shape=[jax.ShapeDtypeStruct(one, BF16) for one in (table_y, table_y, table_x, table_x)],
        in_specs=[VMEM] * 2,
        out_specs=[VMEM] * 4,
        scratch_shapes=[pltpu.VMEM((nx, rank * ranks_y), F32)] * 2,
        compiler_params=pltpu.CompilerParams(vmem_limit_bytes=16 * 2**20),
        cost_estimate=pl.CostEstimate(
            flops=4 * nx * ranks_y * rank * ranks_y, bytes_accessed=6 * 2**20, transcendentals=0
        ),
    )(relative(factor_y, "gy").reshape(ny, rank), relative(factor_x, "gx").reshape(nx, rank))
    columns = relative(factor_z, "gz")
    columns = jnp.transpose(columns.reshape(nz, -1))
    high, low = split_table(columns)
    columns = jnp.concatenate(
        [jnp.concatenate([high, high], axis=1), jnp.concatenate([low, low], axis=1)], axis=0
    )
    piece = (4 * nx // 2, ranks_z, nz)
    far = [*strips, *spans, velocity, inv_density]
    pressure, corrected, keep, keep_more, send = call(
        finish,
        [cells, (3,) + cells, piece, piece, (2,) + piece],
        [dots, columns, *far],
        scratch=[span, (nx + 2, ny, nz), strip, pltpu.VMEM((4, 2 * ny, 2 * nz), BF16), cells, (3,) + cells]
        + [one.shape for one in far],
        limit=32,
        far_in=range(2, 2 + len(far)),
        far_out=(0, 1),
        sems=ITERS + 4 * (ITERS + 5) + 16,
    )

    came = swap(send, "gz", 1)
    table = [y_high, y_low]
    part = (piece[0] // 2, ranks_z, nz)
    half = (2 * nx // planes * ranks_z, nz)
    full = (2 * half[0], nz)
    p_send, p_keep, q_send, q_keep, q_more = call(
        tail_one, [part, part, (2,) + full, full, full], [keep, keep_more, came, *table], limit=16
    )
    p_came, q_came = swap(p_send, "gz", 2), swap(q_send, "gy", 1)
    p_send, p_keep, p_more, q_send, q_keep = call(
        tail_two,
        [(2,) + half, half, half, full, full],
        [p_keep, p_came, q_keep, q_more, q_came, *table],
        limit=16,
    )
    p_came, q_came = swap(p_send, "gy", 1), swap(q_send, "gy", 2)
    p_send, p_keep, q_send, q_keep = call(
        tail_three, [half] * 4, [p_keep, p_more, p_came, q_keep, q_came]
    )
    p_came, q_came = swap(p_send, "gy", 2), swap(q_send, "gz", 2)
    half = (4 * ranks_z, rank * ranks_y // 2)
    keep, send = call(
        functools.partial(rank_x, ranks_z),
        [half] * 2,
        [p_keep, p_came, q_keep, q_came, x_high, x_low],
        limit=16,
    )
    mask = 1
    while True:
        came = swap(send, "gx", mask)
        mask *= 2
        if mask >= count_x:
            break
        total = keep + came
        width = total.shape[1] // 2
        keep, send = total[:, :width], total[:, width:]
    core, = call(last_core, [(4, ranks_y, ranks_z, rank // count_x)], [keep, came], limit=16, pinned=(0,))
    return pressure, corrected, jnp.transpose(core, (3, 0, 1, 2))


def solution(mesh):
    placed = (
        P(None, "gx", "gy", "gz"),
        P("gx", "gy", "gz"),
        P("gx", None),
        P("gy", None),
        P("gz", None),
    )
    return jax.shard_map(
        per_device,
        mesh=mesh,
        in_specs=placed,
        out_specs=(P("gx", "gy", "gz"), P(None, "gx", "gy", "gz"), P("gx", None, "gy", "gz")),
        check_vma=False,
    )
```

```python
import functools
import math

import jax
import jax.numpy as jnp
from jax import lax
from jax.experimental import pallas as pl
from jax.experimental.pallas import tpu as pltpu
from jax.sharding import PartitionSpec as P

ITERS = 4
SHIFT = 0.1
AXES = ("gx", "gy", "gz")

REACH = ITERS
LAYERS = ITERS + 1
WIDE = 8
SLOT = 16
STRIP = 2 * LAYERS
SPAN = 32
ROWS = 24
NEWTON = (0.5, 0.5, 0.5)
PAIRS = [(a, b) for a in range(ITERS) for b in range(a, ITERS)]
VMEM = pl.BlockSpec(memory_space=pltpu.VMEM)
SMEM = pl.BlockSpec(memory_space=pltpu.SMEM)
HBM = pl.BlockSpec(memory_space=pltpu.HBM)
F32 = jnp.float32
BF16 = jnp.bfloat16


def call(body, outs, operands, scratch=(), smem=0, limit=12, cost=None, far_in=(), far_out=(), pinned=(), sems=0):
    scratch = [pltpu.VMEM(shape, F32) if isinstance(shape, tuple) else shape for shape in scratch]
    return pl.pallas_call(
        body,
        out_shape=[
            pltpu.HBM(shape, F32)
            if n in far_out or n in pinned
            else jax.ShapeDtypeStruct(shape, F32)
            for n, shape in enumerate(outs)
        ],
        in_specs=[SMEM if n < smem else HBM if n in far_in else VMEM for n in range(len(operands))],
        out_specs=[HBM if n in far_out else VMEM for n in range(len(outs))],
        scratch_shapes=scratch + ([pltpu.SemaphoreType.DMA((sems,))] if sems else []),
        compiler_params=pltpu.CompilerParams(vmem_limit_bytes=limit * 2**20),
        cost_estimate=cost
        and pl.CostEstimate(flops=cost[0], bytes_accessed=cost[1], transcendentals=0),
    )(
        *(
            pltpu.with_memory_space_constraint(one, pltpu.HBM)
            if n in far_in
            else one
            for n, one in enumerate(operands)
        )
    )


def cost_of(shape):
    return 4 * math.prod(shape)


def lanes(shape):
    return lax.broadcasted_iota(jnp.int32, shape, len(shape) - 1)


def sublanes(shape):
    return lax.broadcasted_iota(jnp.int32, shape, len(shape) - 2)


def exchange(up, down, axis):
    count = lax.axis_size(axis)
    ends = count - 1
    below = lax.ppermute(up, axis, [(i, i + 1) for i in range(ends)])
    above = lax.ppermute(down, axis, [(i + 1, i) for i in range(ends)])
    return below, above


def source(velocity, x, nx):
    ny, nz = velocity.shape[2:]
    shape = (ny, nz)
    before = jnp.where(x == 0, 0.0, velocity[0, jnp.maximum(x - 1, 0)])
    after = jnp.where(x == nx - 1, 0.0, velocity[0, jnp.minimum(x + 1, nx - 1)])
    along_y = velocity[1, x]
    along_z = velocity[2, x]
    total = after - before
    total = total + jnp.where(sublanes(shape) == ny - 1, 0.0, pltpu.roll(along_y, ny - 1, 0))
    total = total - jnp.where(sublanes(shape) == 0, 0.0, pltpu.roll(along_y, 1, 0))
    total = total + jnp.where(lanes(shape) == nz - 1, 0.0, pltpu.roll(along_z, nz - 1, 1))
    total = total - jnp.where(lanes(shape) == 0, 0.0, pltpu.roll(along_z, 1, 1))
    return -0.5 * total


def ring(one, two, axis, closed=True, beside=None):
    count = lax.axis_size(axis)
    near = [(i, i ^ 1) for i in range(count)]
    far = [(i, (i + 1 if i % 2 else i - 1) % count) for i in range(count)]
    if not closed:
        far = [(i, j) for i, j in far if abs(i - j) == 1]
    if beside:
        near, far = (
            [(x * count + i, (1 - x) * count + j) for x in range(2) for i, j in pairs] for pairs in (near, far)
        )
        axis = (beside, axis)
    return lax.ppermute(one, axis, near), lax.ppermute(two, axis, far)


def pack_x(index, velocity_far, inv_far, *refs):
    velocity, inv, sems = refs[-3:]
    messages = refs[:-3]
    layers, ny, nz = inv.shape[1:]
    far = inv_far.shape[0] - layers
    shape = (ny, nz)
    only = len(messages) == 1
    first = index[0] == 0

    def copies(n):
        start = jnp.where(first, far, 0) if only else (far, 0)[n]
        part = pl.ds(start, layers)
        yield pltpu.make_async_copy(inv_far.at[part], inv.at[n], sems.at[4 * n])
        for d in range(3):
            yield pltpu.make_async_copy(velocity_far.at[d, part], velocity.at[n, d], sems.at[4 * n + d + 1])

    for n in range(len(messages)):
        for copy in copies(n):
            copy.start()

    def fill(n, start, own, sign):
        message, near = messages[n], velocity.at[n]
        for k in range(REACH):
            message[k * ny : (k + 1) * ny, :] = source(near, start + k, layers)
        base = REACH * ny
        message[base : base + ny, :] = sign * near[0, own]
        base += ny
        for k in range(LAYERS):
            message[base : base + ny, :] = inv[n, k]
            base += ny
        ends = jnp.zeros(shape, F32)
        for k in range(REACH):
            plane_z = near[2, start + k]
            ends = jnp.where(lanes(shape) == 2 * k, plane_z[:, 0:1], ends)
            ends = jnp.where(lanes(shape) == 2 * k + 1, plane_z[:, nz - 1 : nz], ends)
        message[base : base + ny, :] = ends
        base += ny
        for k in range(REACH):
            message[base + 2 * k : base + 2 * k + 1, :] = near[1, start + k, 0:1, :]
            message[base + 2 * k + 1 : base + 2 * k + 2, :] = near[1, start + k, ny - 1 : ny, :]

    for n in range(len(messages)):
        for copy in copies(n):
            copy.wait()
    upper = (1, layers - 1, 0.5)
    lower = (0, 0, -0.5)
    if only:
        fill(0, *(jnp.where(first, one, two) for one, two in zip(upper, lower)))
    else:
        fill(0, *upper)
        fill(1, *lower)


class Scaled:
    def __init__(self, ref, factor):
        self.ref, self.factor = ref, factor

    def __getitem__(self, where):
        return self.ref[where] * self.factor


class Picked:
    def __init__(self, first, one, two, there):
        self.first, self.one, self.two, self.factor = first, one, two, jnp.where(there, 1.0, 0.0)

    def __getitem__(self, where):
        return jnp.where(self.first, self.one[where], self.two[where]) * self.factor


def sides(index, axis, messages):
    here, count = index[2 * axis], index[2 * axis + 1]
    same, (one, two) = here % 2 == 0, messages
    return Picked(same, two, one, here > 0), Picked(same, one, two, here < count - 1)


def sides_x(index, messages):
    if len(messages) == 2:
        return messages
    first = jnp.where(index[0] == 0, 1.0, 0.0)
    return Scaled(messages[0], 1.0 - first), Scaled(messages[0], first)


EARLY = (LAYERS + 1) // 2
EACH = REACH + 1 + LAYERS + 1


def put(up, down, pair, parity, rows_rhs, ghost, rows_inv, first, last, same=None):
    offset = parity * EACH
    row = (1, up.shape[2])

    def store(start, count, lower, upper):
        if same is not None:
            lower, upper = jnp.where(same, lower, upper), jnp.where(same, upper, lower)
        up[pair, pl.ds(offset + start, count), :] = upper
        down[pair, pl.ds(offset + start, count), :] = lower

    store(0, REACH, *rows_rhs)
    store(REACH, 1, -0.5 * ghost[0], 0.5 * ghost[1])
    store(REACH + 1, LAYERS, *rows_inv)
    both = []
    for part in range(2):
        ends = jnp.zeros(row, F32)
        for k in range(REACH):
            ends = jnp.where(lanes(row) == 2 * k, first[part][k : k + 1], ends)
            ends = jnp.where(lanes(row) == 2 * k + 1, last[part][k : k + 1], ends)
        both.append(ends)
    store(EACH - 1, 1, *both)


def put_own(up, down, velocity, inv, rhs, x, pair, parity, extra, same=None):
    ny, nz = inv.shape[1:]
    low, high = rhs[x, 0:REACH, :], rhs[x, ny - REACH : ny, :]
    if extra is not None:
        low = low + extra[pl.ds(REACH * ny, REACH), :]
        high = high + extra[pl.ds((REACH + 1) * ny - REACH, REACH), :]
    ghost = (velocity[1, x, 0:1, :], velocity[1, x, ny - 1 : ny, :])
    rows_inv = (inv[x, 0:LAYERS, :], inv[x, ny - LAYERS : ny, :])
    head, tail = velocity[2, x, 0:REACH, :], velocity[2, x, ny - REACH : ny, :]
    first = (head[:, 0:1], tail[:, 0:1])
    last = (head[:, nz - 1 : nz], tail[:, nz - 1 : nz])
    put(up, down, pair, parity, (low, high), ghost, rows_inv, first, last, same)


def put_rows(up, down, pair, start, lower, upper, same):
    up[pair, pl.ds(start, REACH), :] = jnp.where(same, upper, lower)
    down[pair, pl.ds(start, REACH), :] = jnp.where(same, lower, upper)


def pack_y_own(index, velocity, inv, sent, rhs, up, down, *across):
    del sent
    nx, ny, nz = rhs.shape
    same = index[2] % 2 == 0

    def plane(x, carry):
        rhs[x] = source(velocity, x, nx)
        return carry

    lax.fori_loop(0, nx, plane, 0, unroll=4)

    def planes(n, carry):
        for parity in range(2):
            put_own(up, down, velocity, inv, rhs, 2 * n + parity, n, parity, None, same)
        return carry

    def edge_rows(x):
        return velocity[0, x, 0:REACH, :], velocity[0, x, ny - REACH : ny, :]

    if across:
        first = index[0] == 0
        for k in range(LAYERS):
            x = jnp.where(first, nx - LAYERS + k, k)
            put_own(*across, velocity, inv, rhs, x, 0, k, None, same)
        rows = edge_rows(jnp.where(first, nx - 1, 0))
        sign = jnp.where(first, 0.5, -0.5)
        put_rows(*across, 0, LAYERS * EACH, sign * rows[0], sign * rows[1], same)
    lax.fori_loop(0, nx // 2, planes, 0, unroll=4)
    put_rows(up, down, nx // 2, 0, *edge_rows(0), same)
    put_rows(up, down, nx // 2, REACH, *edge_rows(nx - 1), same)


def pack_y_halo(index, velocity, inv, rhs, *refs):
    (below, above), (up, down) = sides_x(index, refs[:-2]), refs[-2:]
    same = index[2] % 2 == 0
    nx, ny, nz = inv.shape
    skip = (nx + 2 * LAYERS) // 2 - 2 * EARLY

    def halo(x, message, k_rhs, k_inv, extra):
        pair = x // 2 if x // 2 < EARLY else x // 2 - skip
        base = (REACH + 1 + k_inv) * ny
        rows_inv = (message[pl.ds(base, LAYERS), :], message[pl.ds(base + ny - LAYERS, LAYERS), :])
        zero_row = jnp.zeros((1, nz), F32)
        zero = jnp.zeros((REACH, nz), F32)
        if k_rhs is None:
            column = jnp.zeros((REACH, 1), F32)
            put(up, down, pair, x % 2, (zero, zero), (zero_row, zero_row), rows_inv, (column, column), (column, column), same)
            return
        low, high = message[pl.ds(k_rhs * ny, REACH), :], message[pl.ds((k_rhs + 1) * ny - REACH, REACH), :]
        if extra is not None:
            sign, source = extra
            low = low + sign * velocity[0, source, 0:REACH, :]
            high = high + sign * velocity[0, source, ny - REACH : ny, :]
        ends = (REACH + 1 + LAYERS) * ny
        lines = ends + ny + 2 * k_rhs
        ghost = (message[pl.ds(lines, 1), :], message[pl.ds(lines + 1, 1), :])
        head, tail = message[pl.ds(ends, REACH), :], message[pl.ds(ends + ny - REACH, REACH), :]
        first = (head[:, 2 * k_rhs : 2 * k_rhs + 1], tail[:, 2 * k_rhs : 2 * k_rhs + 1])
        last = (head[:, 2 * k_rhs + 1 : 2 * k_rhs + 2], tail[:, 2 * k_rhs + 1 : 2 * k_rhs + 2])
        put(up, down, pair, x % 2, (low, high), ghost, rows_inv, first, last, same)

    for k in range(LAYERS):
        halo(k, below, k - 1 if k else None, k, (-0.5, 0) if k == LAYERS - 1 else None)
        halo(
            nx + LAYERS + k,
            above,
            k if k < REACH else None,
            k,
            (0.5, nx - 1) if k == 0 else None,
        )
    put_own(up, down, velocity, inv, rhs, 0, EARLY - 1, 1, below, same)
    put_own(up, down, velocity, inv, rhs, nx - 1, EARLY, 0, above, same)


def pack_z(across, index, velocity, inv, rhs, *refs):
    (below, above), received = sides_x(index, refs[:-16]), refs[-16:-12]
    received = [*sides(index, 1, received[:2]), *sides(index, 1, received[2:])]
    same = index[4] % 2 == 0
    rhs_far, inv_far, up, down, strip_rhs_far, strip_inv_far = refs[-12:-6]
    rhs_wide, inv_wide, ends, strip_rhs, strip_inv, sems = refs[-6:]
    nx, ny, nz = inv.shape
    wide = nx + 2 * LAYERS
    rows = ny + 2 * WIDE
    mine = pl.ds(WIDE, ny)
    edge = (WIDE, nz)
    groups = strip_rhs.shape[0]

    for k in range(LAYERS):
        for message, x, layer in ((below, k, k - 1), (above, nx + LAYERS + k, k if k < REACH else -1)):
            base = (REACH + 1 + k) * ny
            inv_wide[x, mine, :] = message[pl.ds(base, ny), :]
            if layer < 0:
                rhs_wide[x, mine, :] = jnp.zeros((ny, nz), F32)
                ends[x, mine, :] = jnp.zeros((ny, nz), F32)
                continue
            part = message[pl.ds(layer * ny, ny), :]
            if x == LAYERS - 1:
                part = part - 0.5 * velocity[0, 0]
            if x == nx + LAYERS:
                part = part + 0.5 * velocity[0, nx - 1]
            rhs_wide[x, mine, :] = part
            line = message[pl.ds((REACH + 1 + LAYERS) * ny, ny), :]
            ends[x, mine, :] = jnp.where(
                lanes((ny, nz)) == 0, line[:, 2 * layer : 2 * layer + 1], line[:, 2 * layer + 1 : 2 * layer + 2]
            )

    def plane(x, carry):
        inv_wide[x + LAYERS, mine, :] = inv[x]
        rhs_wide[x + LAYERS, mine, :] = rhs[x]
        ends[x + LAYERS, mine, :] = velocity[2, x]
        return carry

    lax.fori_loop(0, nx, plane, 0, unroll=4)
    rhs_wide[LAYERS, mine, :] += below[pl.ds(REACH * ny, ny), :]
    rhs_wide[LAYERS + nx - 1, mine, :] += above[pl.ds(REACH * ny, ny), :]
    for ref in (rhs_wide, inv_wide, ends):
        for x in range(wide, ref.shape[0]):
            ref[x] = jnp.zeros((rows, nz), F32)

    first = index[0] == 0
    own, far = received[:2], received[2:]

    def from_pair(refs, pair, parity):
        values = [ref[pair] for ref in refs]
        if isinstance(parity, int):
            return [(pltpu.roll(value, ROWS - EACH, 0) if parity else value)[0:SLOT] for value in values]
        return [jnp.where(parity == 0, value, pltpu.roll(value, ROWS - EACH, 0))[0:SLOT] for value in values]

    def extra(refs, pair, start, factor):
        values = [ref[pair] for ref in refs]
        size = values[0].shape[0]
        values = [pltpu.roll(value, (size - start) % size, 0)[0:SLOT] for value in values]
        return [jnp.where(sublanes((SLOT, nz)) < REACH, factor * value, 0.0) for value in values]

    def rows_of(x):
        if not isinstance(x, int):
            return from_pair(own, (x - LAYERS) // 2, (x - LAYERS) % 2)
        inside = LAYERS <= x < LAYERS + nx
        upper = x >= LAYERS + nx - 1
        if not across:
            return from_pair(far, x // 2 - (wide // 2 - 2 * EARLY if upper else 0), x % 2)
        there = jnp.where(first, 1.0, 0.0) if upper else jnp.where(first, 0.0, 1.0)
        if inside:
            values = from_pair(own, (x - LAYERS) // 2, (x - LAYERS) % 2)
            rows_at = (0, pl.ds(LAYERS * EACH // SLOT * SLOT, SLOT), slice(None))
            more = extra(far, rows_at, LAYERS * EACH % SLOT, there)
        else:
            k = x - LAYERS - nx if upper else x
            values = [there * ref[0, pl.ds(k * EACH, SLOT), :] for ref in far]
            if x == LAYERS - 1:
                more = extra(own, nx // 2, 0, -0.5)
            elif x == LAYERS + nx:
                more = extra(own, nx // 2, REACH, 0.5)
            else:
                return values
        return [one + two for one, two in zip(values, more)]

    def finish(x, ghost_low, ghost_high):
        low, high = rows_of(x)
        part = pltpu.roll(low, WIDE - REACH, 0)[0:WIDE]
        part = jnp.where(sublanes(edge) >= WIDE - REACH, part, 0.0)
        part = part - jnp.where(sublanes(edge) == WIDE - 1, 0.5 * ghost_low, 0.0)
        rhs_wide[x, 0:WIDE, :] = part
        part = pltpu.roll(low, SLOT - (REACH + 1) + WIDE - LAYERS, 0)[0:WIDE]
        inv_wide[x, 0:WIDE, :] = jnp.where(sublanes(edge) >= WIDE - LAYERS, part, 0.0)
        part = jnp.where(sublanes(edge) < REACH, high[0:WIDE], 0.0)
        part = part + jnp.where(sublanes(edge) == 0, 0.5 * ghost_high, 0.0)
        rhs_wide[x, WIDE + ny : rows, :] = part
        part = pltpu.roll(high, SLOT - (REACH + 1), 0)[0:WIDE]
        inv_wide[x, WIDE + ny : rows, :] = jnp.where(sublanes(edge) < LAYERS, part, 0.0)
        head = rhs_wide[x, WIDE : 2 * WIDE, :]
        rhs_wide[x, WIDE : 2 * WIDE, :] = head + jnp.where(sublanes(edge) == 0, low[REACH : REACH + 1], 0.0)
        tail = rhs_wide[x, ny : WIDE + ny, :]
        rhs_wide[x, ny : WIDE + ny, :] = tail + jnp.where(
            sublanes(edge) == WIDE - 1, high[REACH : REACH + 1], 0.0
        )
        for message, start, place in ((low, WIDE - REACH, 0), (high, 0, WIDE + ny)):
            line = message[EACH - 1 : EACH]
            one = jnp.zeros(edge, F32)
            two = jnp.zeros(edge, F32)
            for k in range(REACH):
                here = sublanes(edge) == start + k
                one = jnp.where(here, line[:, 2 * k : 2 * k + 1], one)
                two = jnp.where(here, line[:, 2 * k + 1 : 2 * k + 2], two)
            ends[x, place : place + WIDE, :] = jnp.where(lanes(edge) == 0, one, two)

    for k in range(LAYERS):
        for message, x, layer in ((below, k, k - 1), (above, nx + LAYERS + k, k if k < REACH else -1)):
            lines = (REACH + 1 + LAYERS + 1) * ny + 2 * layer
            if layer < 0:
                zero = jnp.zeros((1, nz), F32)
                finish(x, zero, zero)
            else:
                finish(x, message[pl.ds(lines, 1), :], message[pl.ds(lines + 1, 1), :])

    def middle(x, carry):
        finish(x + LAYERS, velocity[1, x, 0:1, :], velocity[1, x, ny - 1 : ny, :])
        return carry

    lax.fori_loop(1, nx - 1, middle, 0, unroll=10)
    for x in (0, nx - 1):
        finish(x + LAYERS, velocity[1, x, 0:1, :], velocity[1, x, ny - 1 : ny, :])
    copies = [
        pltpu.make_async_copy(ref.at[pl.ds(0, wide)], far, sems.at[n])
        for n, (ref, far) in enumerate(((rhs_wide, rhs_far), (inv_wide, inv_far)))
    ]
    for copy in copies:
        copy.start()

    whole = (rows, nz)
    lane = lanes(whole)
    place = lane % SPAN

    def back(value, step):
        return pltpu.roll(value, nz - step, 1)

    def gather(ref, g):
        value = None
        for n in range(nz // SPAN):
            moved = pltpu.roll(ref[g + n * groups], n * SPAN + STRIP, 1)
            value = moved if value is None else jnp.where(lane >= n * SPAN, moved, value)
        return value

    def pack(g):
        r, i, e = gather(rhs_wide, g), gather(inv_wide, g), gather(ends, g)
        apart = SPAN - 2 * STRIP
        for ref, value in ((strip_rhs, r), (strip_inv, i)):
            out = jnp.where(place < STRIP, value, 0.0)
            ref[g] = jnp.where(place >= SPAN - STRIP, pltpu.roll(value, apart, 1), out)
        ghost = jnp.where(place == STRIP, 0.5 * pltpu.roll(e, 1, 1), 0.0)
        ghost = jnp.where(place == SPAN - STRIP - 1, -0.5 * pltpu.roll(e, apart - 1, 1), ghost)
        strip_rhs[g] += ghost
        out = jnp.where(place < REACH, back(r, STRIP - REACH), 0.0)
        out = jnp.where(place == REACH, 0.5 * back(e, STRIP - 1 - REACH), out)
        here = (place > REACH) & (place <= REACH + LAYERS)
        higher = jnp.where(here, pltpu.roll(i, (nz + REACH + 1 + LAYERS - STRIP) % nz, 1), out)
        out = jnp.where(place < REACH, back(r, STRIP), 0.0)
        out = jnp.where(place == REACH, -0.5 * back(e, STRIP - REACH), out)
        return higher, jnp.where(here, back(i, STRIP - REACH - 1), out)

    halves = up.shape[0]

    def both(n, carry):
        one, two = pack(n)
        up[n] = jnp.where(same, one, two)
        down[n] = jnp.where(same, two, one)
        return carry

    lax.fori_loop(0, halves, both, 0, unroll=2)

    def more(n, carry):
        one, two = pack(n + halves)
        up[n] += pltpu.roll(jnp.where(same, one, two), SPAN // 2, 1)
        down[n] += pltpu.roll(jnp.where(same, two, one), SPAN // 2, 1)
        return carry

    lax.fori_loop(0, groups - halves, more, 0, unroll=2)
    for ref, far in ((strip_rhs, strip_rhs_far), (strip_inv, strip_inv_far)):
        copies.append(pltpu.make_async_copy(ref, far, sems.at[len(copies)]))
        copies[-1].start()
    for copy in copies:
        copy.wait()


def shifted(ref, x, t, step):
    rows = ref.shape[1]
    start = t * WIDE + step
    if start < 0:
        return pltpu.roll(ref[x, 0:WIDE, :], 1, 0)
    if start + WIDE > rows:
        return pltpu.roll(ref[x, rows - WIDE : rows, :], WIDE - 1, 0)
    return ref[x, start : start + WIDE, :]


class Stencil:
    def __init__(self, inv, root, ax, ay, az, vs, planes, edges=None, unroll=6):
        self.inv, self.root, self.ax, self.ay, self.az, self.vs = inv, root, ax, ay, az, vs
        self.planes, self.edges, self.unroll = planes, edges or (lambda ref: None), unroll
        self.count, self.rows, self.nz = inv.shape
        self.tiles = self.rows // WIDE

    def here(self, t):
        return slice(t * WIDE, (t + 1) * WIDE)

    def right(self, value):
        return pltpu.roll(value, self.nz - 1, 1)

    def left(self, value):
        return pltpu.roll(value, 1, 1)

    def prepare(self, rhs, parts=None):
        inv, root = self.inv, self.root
        self.edges(inv)

        def scales(x, carry):
            writes = []
            for t in range(self.tiles):
                here = self.here(t)
                c = inv[x, here, :]
                total = (inv[x + 1, here, :] + inv[x - 1, here, :]) + (self.right(c) + self.left(c))
                total = total + (shifted(inv, x, t, 1) + shifted(inv, x, t, -1))
                value = jnp.where(c > 0.0, lax.rsqrt(SHIFT + 0.5 * (6.0 * c + total)), 0.0)
                writes.append((here, value, rhs[x, here, :] * value))
            for here, one, two in writes:
                root[x, here, :] = one
                self.vs[0][x, here, :] = two
            return carry

        for start, stop in parts or [(1, self.count - 1)]:
            lax.fori_loop(start, stop, scales, 0, unroll=self.unroll)
        zero = jnp.zeros((self.rows, self.nz), F32)
        for ref in (root, self.vs[0]):
            ref[0] = zero
            ref[self.count - 1] = zero
            self.edges(ref)

        def couplings(x, carry):
            writes = []
            for t in range(self.tiles):
                here = self.here(t)
                c, d = inv[x, here, :], root[x, here, :]
                half = 0.5 * d
                writes.append(
                    (
                        here,
                        (c + inv[x + 1, here, :]) * (half * root[x + 1, here, :]),
                        (c + shifted(inv, x, t, 1)) * (half * shifted(root, x, t, 1)),
                        (c + self.right(c)) * (half * self.right(d)),
                    )
                )
            for here, x_face, y_face, z_face in writes:
                self.ax[x, here, :] = x_face
                self.ay[x, here, :] = y_face
                self.az[x, here, :] = z_face
            return carry

        lax.fori_loop(1, self.count - 1, couplings, 0, unroll=self.unroll)
        self.ax[0] = zero
        self.edges(self.ax)

    def couple(self, k, x, t):
        here = self.here(t)
        v, ax, ay = self.vs[k], self.ax, self.ay
        c, f = v[x, here, :], self.az[x, here, :]
        total = ax[x, here, :] * v[x + 1, here, :] + ax[x - 1, here, :] * v[x - 1, here, :]
        total = total + (f * self.right(c) + self.left(f * c))
        total = total + ay[x, here, :] * shifted(v, x, t, 1)
        return c, total + shifted(ay, x, t, -1) * shifted(v, x, t, -1)

    def extend(self, k):
        scale = 1.0 - NEWTON[k]

        def step(x, carry):
            writes = []
            for t in range(self.tiles):
                c, total = self.couple(k, x, t)
                writes.append((t, scale * c - total if scale else -total))
            for t, value in writes:
                self.vs[k + 1][x, self.here(t), :] = value
            return carry

        start, stop = self.planes(k)
        lax.fori_loop(start, stop, step, 0, unroll=self.unroll)
        self.edges(self.vs[k + 1])

    def products(self, start, stop, mask):
        def measure(x, sums):
            sums = list(sums)
            for t in range(1, self.tiles - 1):
                keep = mask(x)
                v = [self.vs[k][x, self.here(t), :] for k in range(ITERS)]
                own, total = self.couple(ITERS - 1, x, t)
                kept = [jnp.where(keep, one, 0.0) for one in v]
                for n, (a, b) in enumerate(PAIRS):
                    sums[n] = sums[n] + v[a] * kept[b]
                sums[-1] = sums[-1] + kept[-1] * (own - total)
            return tuple(sums)

        zero = jnp.zeros((WIDE, self.nz), F32)
        return lax.fori_loop(start, stop, measure, (zero,) * (len(PAIRS) + 1), unroll=4)


def basis_main(rhs_far, inv_far, *refs):
    outs, sums = refs[: ITERS + 1], refs[ITERS + 1]
    rhs, inv, root, ax, ay, az = refs[ITERS + 2 : ITERS + 8]
    vs, sems = refs[ITERS + 8 : -1], refs[-1]
    wide, rows, nz = ax.shape
    nx = wide - 2 * LAYERS
    batch = 4
    bounds = [n * wide // batch for n in range(batch + 1)]
    loads = []
    for n in range(batch):
        part = pl.ds(bounds[n], bounds[n + 1] - bounds[n])
        for far, ref in ((inv_far, inv), (rhs_far, rhs)):
            loads.append(pltpu.make_async_copy(far.at[part], ref.at[part], sems.at[ITERS + 1 + len(loads)]))
            loads[-1].start()

    def ready():
        for n in range(batch):
            for load in loads[2 * n : 2 * n + 2]:
                load.wait()
            yield max(bounds[n] - 1, 1), bounds[n + 1] - 1

    stencil = Stencil(inv, root, ax, ay, az, vs, lambda k: (2 + k, wide - 2 - k))
    copies = []

    def send(n, ref):
        copy = pltpu.make_async_copy(ref.at[pl.ds(LAYERS - 1, nx + 2)], outs[n], sems.at[n])
        copy.start()
        copies.append(copy)

    stencil.prepare(rhs, ready())
    send(ITERS, root)
    send(0, vs[0])
    for k in range(ITERS - 1):
        stencil.extend(k)
        send(k + 1, vs[k + 1])
    lane = lanes((WIDE, nz))
    inner = (lane > REACH) & (lane < nz - 1 - REACH)
    for n, one in enumerate(stencil.products(LAYERS, LAYERS + nx, lambda x: inner)):
        sums[n] = one
    for copy in copies:
        copy.wait()


def basis_strips(nx, index, rhs_far, inv_far, one, two, sums, *refs):
    before, after = sides(index, 2, (one, two))
    outs, dots = refs[:ITERS], refs[ITERS]
    rhs, inv, root, ax, ay, az = refs[ITERS + 1 : ITERS + 7]
    vs, outs_near = refs[ITERS + 7 : 2 * ITERS + 7], refs[2 * ITERS + 7 : 3 * ITERS + 7]
    strip_rhs, strip_inv, sems = refs[-3:]
    groups, rows, nz = strip_inv.shape
    loads = [
        pltpu.make_async_copy(far, ref, sems.at[ITERS + n])
        for n, (far, ref) in enumerate(((rhs_far, strip_rhs), (inv_far, strip_inv)))
    ]
    for load in loads:
        load.start()
    for load in loads:
        load.wait()
    halves = one.shape[0]
    whole = (rows, nz)
    place = lanes(whole) % SPAN

    def edges(ref):
        ref[0] = pltpu.roll(ref[groups], SPAN, 1)
        ref[groups + 1] = pltpu.roll(ref[1], nz - SPAN, 1)

    def receive(g, low, high):
        start = SPAN - STRIP - LAYERS
        moved = pltpu.roll(low, start + 1, 1)
        r = strip_rhs[g] + jnp.where((place > start) & (place <= SPAN - STRIP), moved, 0.0)
        moved = pltpu.roll(low, start - REACH - 1, 1)
        i = strip_inv[g] + jnp.where((place >= start) & (place < SPAN - STRIP), moved, 0.0)
        moved = pltpu.roll(high, STRIP, 1)
        r = r + jnp.where((place >= STRIP) & (place < STRIP + REACH), moved, 0.0)
        moved = pltpu.roll(high, STRIP - REACH - 1, 1)
        r = r + jnp.where(place == STRIP - 1, moved, 0.0)
        i = i + jnp.where((place >= STRIP) & (place < STRIP + LAYERS), moved, 0.0)
        rhs[g + 1] = r
        inv[g + 1] = i

    def first(n, carry):
        receive(n, before[n], after[n])
        return carry

    def second(n, carry):
        half = nz - SPAN // 2
        receive(n + halves, pltpu.roll(before[n], half, 1), pltpu.roll(after[n], half, 1))
        return carry

    lax.fori_loop(0, halves, first, 0, unroll=3)
    lax.fori_loop(0, groups - halves, second, 0, unroll=3)
    stencil = Stencil(inv, root, ax, ay, az, vs, lambda k: (1, groups + 1), edges, groups)
    stencil.prepare(rhs)
    copies = []

    def result(k):
        ref = outs_near[k]

        def plane(g, carry):
            ref[g] = vs[k][g] * root[g]
            return carry

        lax.fori_loop(1, groups + 1, plane, 0, unroll=groups)
        copies.append(pltpu.make_async_copy(ref.at[pl.ds(1, groups)], outs[k], sems.at[k]))
        copies[-1].start()

    result(0)
    for k in range(ITERS - 1):
        stencil.extend(k)
        result(k + 1)
    lane = lanes((WIDE, nz))
    part = lane // SPAN
    spot = lane % SPAN
    ends = ((spot >= STRIP - LAYERS) & (spot < STRIP)) | (
        (spot >= SPAN - STRIP) & (spot < SPAN - STRIP + LAYERS)
    )

    def mask(x):
        plane = x - 1 + part * groups
        return ends & (plane >= LAYERS) & (plane < LAYERS + nx)

    totals = []
    for n, one in enumerate(stencil.products(1, groups + 1, mask)):
        line = jnp.sum(one + sums[n], axis=0, keepdims=True)
        totals.append(line + pltpu.roll(line, nz // 2, 1))
    row = sublanes((WIDE, nz))
    message = jnp.zeros((WIDE, nz), F32)
    for n, line in enumerate(totals):
        half = lane < nz // 2 if n < WIDE else lane >= nz // 2
        message = jnp.where((row == n % WIDE) & half, line, message)

    def send(n, carry):
        dots[n] = message
        return carry

    lax.fori_loop(0, dots.shape[0], send, 0, unroll=8)

    for copy in copies:
        copy.wait()


def coefficients(dots):
    half = lanes(dots.shape) < dots.shape[1] // 2
    one = jnp.sum(jnp.where(half, dots, 0.0), axis=1, keepdims=True)
    two = jnp.sum(jnp.where(half, 0.0, dots), axis=1, keepdims=True)

    def entry(n):
        return one[n : n + 1] if n < WIDE else two[n - WIDE : n - WIDE + 1]

    gram = {}
    for n, (a, b) in enumerate(PAIRS):
        gram[a, b] = gram[b, a] = entry(n)
    last = ITERS - 1
    image = {}
    for b in range(last):
        for a in range(ITERS):
            image[a, b] = gram[a, b + 1]
            if NEWTON[b]:
                image[a, b] = image[a, b] + NEWTON[b] * gram[a, b]
    for a in range(last):
        image[a, last] = image[last, a]
    image[last, last] = entry(len(PAIRS))

    def product(table, one, two):
        total = None
        for a, left in enumerate(one):
            for b, right in enumerate(two):
                term = left * right * table[a, b]
                total = term if total is None else total + term
        return total

    unit = jnp.ones((1, 1), F32)
    pressure = []
    precond = [unit]
    direction = [unit]
    rz = gram[0, 0]
    for iteration in range(ITERS):
        alpha = rz / product(image, direction, direction)
        pressure = [
            (pressure[n] if n < len(pressure) else 0.0) + alpha * one for n, one in enumerate(direction)
        ]
        if iteration == last:
            break
        moved = []
        for n in range(len(direction) + 1):
            value = None
            if n < len(direction) and NEWTON[n]:
                value = NEWTON[n] * direction[n]
            if n > 0:
                value = direction[n - 1] if value is None else value + direction[n - 1]
            moved.append(value)
        fresh_precond = []
        for n, one in enumerate(moved):
            old = precond[n] if n < len(precond) else None
            if one is None:
                fresh_precond.append(old)
            else:
                fresh_precond.append(-alpha * one if old is None else old - alpha * one)
        precond = fresh_precond
        fresh = product(gram, precond, precond)
        beta = fresh / rz
        direction = [
            one + beta * direction[n] if n < len(direction) else one for n, one in enumerate(precond)
        ]
        rz = fresh
    return pressure


def finish(dots, columns, *refs):
    inputs = 2 * ITERS + 3
    pressure_far, corrected_far, keep, keep_more, send, p, gaps, mixed, cut, pressure, corrected = refs[inputs : inputs + 11]
    held, sems = refs[inputs + 11 : -1], refs[-1]
    strips, spans, roots = held[:ITERS], held[ITERS : 2 * ITERS], held[2 * ITERS]
    velocity, inv = held[2 * ITERS + 1 :]
    nx, ny, nz = inv.shape
    batch = 4
    each = nx // batch
    used = 0

    def start(far, ref):
        nonlocal used
        copy = pltpu.make_async_copy(far, ref, sems.at[used])
        used += 1
        copy.start()
        return copy

    strip_loads = [start(far, ref) for far, ref in zip(refs[:ITERS], strips)]
    span_loads, other_loads, bounds = [], [], []
    for n in range(batch):
        low, high = (n * each + 2 if n else 0), (n + 1) * each + 2
        bounds.append((low, high))
        part = pl.ds(low, high - low)
        pairs = zip(refs[ITERS : 2 * ITERS + 1], held[ITERS : 2 * ITERS + 1])
        span_loads.append([start(far.at[part], ref.at[part]) for far, ref in pairs])
        part = pl.ds(n * each, each)
        other_loads.append(
            [start(refs[2 * ITERS + 1].at[d, part], velocity.at[d, part]) for d in range(3)]
            + [start(refs[2 * ITERS + 2].at[part], inv.at[part])]
        )
    shape = (ny, nz)
    groups = mixed.shape[0]
    total = dots[0]
    for n in range(1, dots.shape[0]):
        total = total + dots[n]
    weights = coefficients(total)

    def strip(g, carry):
        value = weights[0] * strips[0][g]
        for k in range(1, ITERS):
            value = value + weights[k] * strips[k][g]
        mixed[g] = value
        return carry

    for load in strip_loads:
        load.wait()
    lax.fori_loop(0, groups, strip, 0, unroll=4)
    mine = slice(WIDE, WIDE + ny)
    lane = lanes(spans[0].shape[1:])

    def combine(x, carry):
        value = weights[0] * spans[0][x]
        for k in range(1, ITERS):
            value = value + weights[k] * spans[k][x]
        value = value * roots[x]
        plane = x + LAYERS - 1
        ends = mixed[plane % groups]
        start = plane // groups * SPAN
        last = pltpu.roll(ends, lax.rem(2 * nz - STRIP - start, nz), 1)
        first = pltpu.roll(ends, lax.rem(nz + STRIP - SPAN - start + nz, nz), 1)
        value = jnp.where(lane < LAYERS, first, jnp.where(lane >= nz - LAYERS, last, value))
        p[x] = value
        after = pltpu.roll(jnp.where(lane == 0, last, value), nz - 1, 1)
        before = pltpu.roll(jnp.where(lane == nz - 1, first, value), 1, 1)
        gaps[x] = (after - before)[mine]
        return carry

    half = columns.shape[0] // 2

    def pair(n, carry):
        for which in range(2):
            x = 2 * n + which
            centre = p[x + 1, mine, :]
            pressure[x] = centre
            half_inv = 0.5 * inv[x]
            slopes = (
                p[x + 2, mine, :] - p[x, mine, :],
                p[x + 1, WIDE + 1 : WIDE + 1 + ny, :] - p[x + 1, WIDE - 1 : WIDE - 1 + ny, :],
                gaps[x + 1],
            )
            fields = [velocity[d, x] - half_inv * slopes[d] for d in range(3)] + [centre]
            for d in range(3):
                corrected[d, x] = fields[d]
            for f, field in enumerate(fields):
                high = field.astype(BF16)
                low = (field - high.astype(F32)).astype(BF16)
                cut[f, which * ny : (which + 1) * ny, 0:nz] = high
                cut[f, which * ny : (which + 1) * ny, nz : 2 * nz] = low
        for f in range(4):
            out = lax.dot_general(
                columns[...], cut[f], (((1,), (1,)), ((), ())), preferred_element_type=F32
            )
            out = out[:half] + out[half:]
            block = f * (nx // 2) + n
            quarter = half // 4
            keep[block] = out[0:quarter]
            keep_more[block] = out[quarter : 2 * quarter]
            send[0, block] = out[2 * quarter : 3 * quarter]
            send[1, block] = out[3 * quarter :]
        return carry

    stores = []
    for n in range(batch):
        for load in span_loads[n]:
            load.wait()
        lax.fori_loop(*bounds[n], combine, 0, unroll=4)
        for load in other_loads[n]:
            load.wait()
        lax.fori_loop(n * each // 2, (n + 1) * each // 2, pair, 0, unroll=4)
        part = pl.ds(n * each, each)
        stores.append(start(pressure.at[part], pressure_far.at[part]))
        for d in range(3):
            stores.append(start(corrected.at[d, part], corrected_far.at[d, part]))
    for store in stores:
        store.wait()


def tables(count_x, factor_y, factor_x, y_high, y_low, x_high, x_low, spread_high, spread_low):
    ny, rank = factor_y.shape
    nx = factor_x.shape[0]
    planes = y_high.shape[0] // ny
    nz = x_high.shape[1] // rank * planes
    count = y_high.shape[1] // nz
    ranks = rank // count
    wide = jnp.concatenate([factor_y[...], jnp.zeros((ny, nz - rank), F32)], axis=1)
    lane = lanes((ny, nz))
    for h in range(count):
        value = pltpu.roll(wide, (nz - h * ranks) % nz, 1)
        value = jnp.where(lane < ranks, value, 0.0)
        step = ranks
        while step < nz:
            value = value + pltpu.roll(value, step, 1)
            step *= 2
        for n in range(planes):
            high, low = split(jnp.where(lane // ranks == n, value, 0.0))
            y_high[n * ny : (n + 1) * ny, h * nz : (h + 1) * nz] = high
            y_low[n * ny : (n + 1) * ny, h * nz : (h + 1) * nz] = low
    width = x_high.shape[1]
    shape = (rank, width)
    own = rank // count_x
    lane = lanes(shape)
    copy = lane // (ranks * own) * own + lane % own == sublanes(shape)
    copy = jnp.where(copy, 1.0, 0.0).astype(BF16)
    for ref, value in zip((spread_high, spread_low), split(factor_x[...])):
        ref[...] = jnp.dot(value, copy, preferred_element_type=F32)
    shape = (ranks, width)
    here = lanes(shape) // own % ranks == sublanes(shape)

    def row(i, carry):
        at = pl.ds(pl.multiple_of(i * ranks, ranks), ranks)
        x_high[at, :] = jnp.where(here, spread_high[pl.ds(i, 1), :], 0.0).astype(BF16)
        x_low[at, :] = jnp.where(here, spread_low[pl.ds(i, 1), :], 0.0).astype(BF16)
        return carry

    lax.fori_loop(0, nx, row, 0, unroll=4)


def split(value):
    high = value.astype(BF16)
    return high, (value - high.astype(F32)).astype(BF16)


def split_table(value):
    high = lax.reduce_precision(value, exponent_bits=8, mantissa_bits=7)
    return high.astype(BF16), (value - high).astype(BF16)


def three(a, b, dims=(((1,), (0,)), ((), ()))):
    dot = functools.partial(lax.dot_general, dimension_numbers=dims, preferred_element_type=F32)
    (ah, al), (bh, bl) = a, b
    return dot(ah, bh) + (dot(al, bh) + dot(ah, bl))


def rank_y(x, table):
    blocks, ranks, nz = x.shape
    group = table[0].shape[0] // nz
    parts = [
        jnp.concatenate([x[n * group + q] for q in range(group)], axis=1) for n in range(blocks // group)
    ]
    out = three(split(jnp.concatenate(parts, axis=0)), table)
    return [out[:, n * nz : (n + 1) * nz] for n in range(out.shape[1] // nz)]


def tail_one(kept, more, came, high, low, p_send, p_keep, q_send, q_keep, q_more):
    half = kept.shape[0] // 2
    p_send[...] = more[0:half] + came[1, 0:half]
    p_keep[...] = kept[0:half] + came[0, 0:half]
    x = jnp.concatenate([kept[half:] + came[0, half:], more[half:] + came[1, half:]], axis=0)
    q_keep[...], q_more[...], q_send[0], q_send[1] = rank_y(x, (high[...], low[...]))


def tail_two(p_kept, p_came, q_kept, q_more, q_came, high, low, p_send, p_keep, p_more, q_send, q_keep):
    q_send[...] = q_more[...] + q_came[1]
    q_keep[...] = q_kept[...] + q_came[0]
    parts = rank_y(p_kept[...] + p_came[...], (high[...], low[...]))
    p_keep[...], p_more[...], p_send[0], p_send[1] = parts


def tail_three(p_kept, p_more, p_came, q_kept, q_came, p_send, p_keep, q_send, q_keep):
    half = q_keep.shape[0]
    p_send[...] = p_more[...] + p_came[1]
    p_keep[...] = p_kept[...] + p_came[0]
    q_send[...] = q_kept[half:] + q_came[half:]
    q_keep[...] = q_kept[0:half] + q_came[0:half]


def rank_x(ranks, p_kept, p_came, q_kept, q_came, wide_high, wide_low, *outs):
    u = jnp.concatenate([p_kept[...] + p_came[...], q_kept[...] + q_came[...]], axis=0)
    rows, nz = u.shape
    group = wide_high.shape[0] // nz
    parts = []
    for f in range(rows // ranks // group):
        parts.append(
            jnp.concatenate(
                [u[(f * group + q) * ranks : (f * group + q + 1) * ranks] for q in range(group)], axis=1
            )
        )
    x = jnp.concatenate(parts, axis=0)
    out = three(split(x), (wide_high[...], wide_low[...]))
    width = out.shape[1] // len(outs)
    for n, ref in enumerate(outs):
        ref[...] = out[:, n * width : (n + 1) * width]


def last_core(kept, came, core):
    fields, ranks_y, ranks_z, ranks_x = core.shape
    z = kept[...] + came[...]
    for f in range(fields):
        for b in range(ranks_y):
            core[f, b] = z[f * ranks_z : (f + 1) * ranks_z, b * ranks_x : (b + 1) * ranks_x]


def relative(factor, axis):
    count = lax.axis_size(axis)
    order = [0]
    step = 1
    while step < count:
        order = order + [n + step for n in order]
        step *= 2
    bits = count.bit_length() - 1
    order = [sum(((n >> b) & 1) << (bits - 1 - b) for b in range(bits)) for n in range(count)]
    blocks = factor.reshape(factor.shape[0], count, factor.shape[1] // count)
    here = lax.axis_index(axis)
    picked = [
        lax.dynamic_index_in_dim(blocks, jnp.bitwise_xor(here, n), axis=1, keepdims=False) for n in order
    ]
    return jnp.stack(picked, axis=1)


def swap(value, axis, mask):
    count = lax.axis_size(axis)
    return lax.ppermute(value, axis, [(i, i ^ mask) for i in range(count)])


def per_device(velocity, inv_density, factor_x, factor_y, factor_z):
    nx, ny, nz = inv_density.shape
    wide, rows = nx + 2 * LAYERS, ny + 2 * WIDE
    count_x, count_y, count_z = (lax.axis_size(axis) for axis in AXES)
    devices = count_x * count_y * count_z
    cells = (nx, ny, nz)
    rank = factor_x.shape[1]
    index_x = lax.axis_index("gx").reshape(1)
    index = jnp.stack([jnp.int32(f(axis)) for axis in AXES for f in (lax.axis_index, lax.axis_size)])

    shape = (((REACH + 1 + LAYERS + 1) * ny + 2 * REACH), nz)
    number = 1 if count_x == 2 else 2
    sent = call(
        pack_x,
        [shape] * number,
        [index_x, velocity, inv_density],
        scratch=[(number, 3, LAYERS, ny, nz), (number, LAYERS, ny, nz)],
        smem=1,
        far_in=(1, 2),
        sems=4 * number,
    )
    near = [swap(sent[0], "gx", 1)] if count_x == 2 else list(exchange(*sent, "gx"))
    across = count_x == 2
    shape = (nx // 2 + 1, ROWS, nz)
    corner = (1, -(-(LAYERS * EACH + REACH) // SLOT) * SLOT, nz)
    rhs, up, down, *corners = call(
        pack_y_own,
        [cells, shape, shape] + ([corner, corner] if across else []),
        [index, velocity, inv_density, sent[0]],
        smem=1,
        cost=(nx * ny * nz * 10, 6 * cost_of(cells)),
        far_in=(3,),
    )
    received = list(ring(up, down, "gy", closed=False))
    if across:
        received += ring(*corners, "gy", beside="gx", closed=False)
    else:
        shape = (2 * EARLY, ROWS, nz)
        up, down = call(pack_y_halo, [shape, shape], [index, velocity, inv_density, rhs, *near], smem=1)
        received += ring(up, down, "gy")
    parts = nz // SPAN
    groups = -(-wide // parts)
    message = (-(-groups // 2), rows, nz)
    whole = (groups * parts, rows, nz)
    strip = (groups, rows, nz)
    rhs_wide, inv_wide, up, down, strip_rhs, strip_inv = call(
        functools.partial(pack_z, across),
        [(wide, rows, nz)] * 2 + [message, message, strip, strip],
        [index, velocity, inv_density, rhs, *near, *received],
        scratch=[whole] * 3 + [strip] * 2,
        smem=1,
        limit=18,
        far_out=(0, 1, 4, 5),
        sems=4,
    )
    came = ring(up, down, "gz")
    span = (nx + 2, rows, nz)
    whole = (wide, rows, nz)
    *spans, sums = call(
        basis_main,
        [span] * (ITERS + 1) + [(len(PAIRS) + 1, WIDE, nz)],
        [rhs_wide, inv_wide],
        scratch=[whole] * (6 + ITERS),
        limit=22,
        cost=(wide * rows * nz * 100, 7 * cost_of(whole)),
        far_in=(0, 1),
        far_out=range(ITERS + 1),
        sems=ITERS + 9,
    )
    padded = (groups + 2, rows, nz)
    *strips, dots = call(
        functools.partial(basis_strips, nx),
        [strip] * ITERS + [(devices, WIDE, nz)],
        [index, strip_rhs, strip_inv, *came, sums],
        scratch=[padded] * (6 + 2 * ITERS) + [strip] * 2,
        smem=1,
        far_in=(1, 2),
        far_out=range(ITERS),
        sems=ITERS + 2,
    )
    dots = lax.all_to_all(dots, AXES, 0, 0, tiled=True)

    ranks_y, ranks_z = rank // count_y, rank // count_z
    planes = nz // ranks_y
    table_y, table_x = (planes * ny, count_y * nz), (nx * ranks_y, rank * ranks_y)
    y_high, y_low, x_high, x_low = pl.pallas_call(
        functools.partial(tables, count_x),
        out_shape=[jax.ShapeDtypeStruct(one, BF16) for one in (table_y, table_y, table_x, table_x)],
        in_specs=[VMEM] * 2,
        out_specs=[VMEM] * 4,
        scratch_shapes=[pltpu.VMEM((nx, rank * ranks_y), F32)] * 2,
        compiler_params=pltpu.CompilerParams(vmem_limit_bytes=16 * 2**20),
        cost_estimate=pl.CostEstimate(
            flops=4 * nx * ranks_y * rank * ranks_y, bytes_accessed=6 * 2**20, transcendentals=0
        ),
    )(relative(factor_y, "gy").reshape(ny, rank), relative(factor_x, "gx").reshape(nx, rank))
    columns = relative(factor_z, "gz")
    columns = jnp.transpose(columns.reshape(nz, -1))
    high, low = split_table(columns)
    columns = jnp.concatenate(
        [jnp.concatenate([high, high], axis=1), jnp.concatenate([low, low], axis=1)], axis=0
    )
    piece = (4 * nx // 2, ranks_z, nz)
    far = [*strips, *spans, velocity, inv_density]
    pressure, corrected, keep, keep_more, send = call(
        finish,
        [cells, (3,) + cells, piece, piece, (2,) + piece],
        [dots, columns, *far],
        scratch=[span, (nx + 2, ny, nz), strip, pltpu.VMEM((4, 2 * ny, 2 * nz), BF16), cells, (3,) + cells]
        + [one.shape for one in far],
        limit=32,
        far_in=range(2, 2 + len(far)),
        far_out=(0, 1),
        sems=ITERS + 4 * (ITERS + 5) + 16,
    )

    came = swap(send, "gz", 1)
    table = [y_high, y_low]
    part = (piece[0] // 2, ranks_z, nz)
    half = (2 * nx // planes * ranks_z, nz)
    full = (2 * half[0], nz)
    p_send, p_keep, q_send, q_keep, q_more = call(
        tail_one, [part, part, (2,) + full, full, full], [keep, keep_more, came, *table], limit=16
    )
    p_came, q_came = swap(p_send, "gz", 2), swap(q_send, "gy", 1)
    p_send, p_keep, p_more, q_send, q_keep = call(
        tail_two,
        [(2,) + half, half, half, full, full],
        [p_keep, p_came, q_keep, q_more, q_came, *table],
        limit=16,
    )
    p_came, q_came = swap(p_send, "gy", 1), swap(q_send, "gy", 2)
    p_send, p_keep, q_send, q_keep = call(
        tail_three, [half] * 4, [p_keep, p_more, p_came, q_keep, q_came]
    )
    p_came, q_came = swap(p_send, "gy", 2), swap(q_send, "gz", 2)
    half = (4 * ranks_z, rank * ranks_y // 2)
    keep, send = call(
        functools.partial(rank_x, ranks_z),
        [half] * 2,
        [p_keep, p_came, q_keep, q_came, x_high, x_low],
        limit=16,
    )
    mask = 1
    while True:
        came = swap(send, "gx", mask)
        mask *= 2
        if mask >= count_x:
            break
        total = keep + came
        width = total.shape[1] // 2
        keep, send = total[:, :width], total[:, width:]
    core, = call(last_core, [(4, ranks_y, ranks_z, rank // count_x)], [keep, came], limit=16, pinned=(0,))
    return pressure, corrected, jnp.transpose(core, (3, 0, 1, 2))


def solution(mesh):
    placed = (
        P(None, "gx", "gy", "gz"),
        P("gx", "gy", "gz"),
        P("gx", None),
        P("gy", None),
        P("gz", None),
    )
    return jax.shard_map(
        per_device,
        mesh=mesh,
        in_specs=placed,
        out_specs=(P("gx", "gy", "gz"), P(None, "gx", "gy", "gz"), P("gx", None, "gy", "gz")),
        check_vma=False,
    )
```

```python
import functools
import math

import jax
import jax.numpy as jnp
from jax import lax
from jax.experimental import pallas as pl
from jax.experimental.pallas import tpu as pltpu
from jax.sharding import PartitionSpec as P

ITERS = 4
SHIFT = 0.1
AXES = ("gx", "gy", "gz")

REACH = ITERS
LAYERS = ITERS + 1
WIDE = 8
SLOT = 16
STRIP = 2 * LAYERS
SPAN = 32
ROWS = 24
NEWTON = (0.5, 0.5, 0.5)
PAIRS = [(a, b) for a in range(ITERS) for b in range(a, ITERS)]
VMEM = pl.BlockSpec(memory_space=pltpu.VMEM)
SMEM = pl.BlockSpec(memory_space=pltpu.SMEM)
HBM = pl.BlockSpec(memory_space=pltpu.HBM)
F32 = jnp.float32
BF16 = jnp.bfloat16


def call(body, outs, operands, scratch=(), smem=0, limit=12, cost=None, far_in=(), far_out=(), pinned=(), sems=0):
    scratch = [pltpu.VMEM(shape, F32) if isinstance(shape, tuple) else shape for shape in scratch]
    return pl.pallas_call(
        body,
        out_shape=[
            pltpu.HBM(shape, F32)
            if n in far_out or n in pinned
            else jax.ShapeDtypeStruct(shape, F32)
            for n, shape in enumerate(outs)
        ],
        in_specs=[SMEM if n < smem else HBM if n in far_in else VMEM for n in range(len(operands))],
        out_specs=[HBM if n in far_out else VMEM for n in range(len(outs))],
        scratch_shapes=scratch + ([pltpu.SemaphoreType.DMA((sems,))] if sems else []),
        compiler_params=pltpu.CompilerParams(vmem_limit_bytes=limit * 2**20),
        cost_estimate=cost
        and pl.CostEstimate(flops=cost[0], bytes_accessed=cost[1], transcendentals=0),
    )(
        *(
            pltpu.with_memory_space_constraint(one, pltpu.HBM)
            if n in far_in
            else one
            for n, one in enumerate(operands)
        )
    )


def cost_of(shape):
    return 4 * math.prod(shape)


def lanes(shape):
    return lax.broadcasted_iota(jnp.int32, shape, len(shape) - 1)


def sublanes(shape):
    return lax.broadcasted_iota(jnp.int32, shape, len(shape) - 2)


def exchange(up, down, axis):
    count = lax.axis_size(axis)
    ends = count - 1
    below = lax.ppermute(up, axis, [(i, i + 1) for i in range(ends)])
    above = lax.ppermute(down, axis, [(i + 1, i) for i in range(ends)])
    return below, above


def source(velocity, x, nx):
    ny, nz = velocity.shape[2:]
    shape = (ny, nz)
    before = jnp.where(x == 0, 0.0, velocity[0, jnp.maximum(x - 1, 0)])
    after = jnp.where(x == nx - 1, 0.0, velocity[0, jnp.minimum(x + 1, nx - 1)])
    along_y = velocity[1, x]
    along_z = velocity[2, x]
    total = after - before
    total = total + jnp.where(sublanes(shape) == ny - 1, 0.0, pltpu.roll(along_y, ny - 1, 0))
    total = total - jnp.where(sublanes(shape) == 0, 0.0, pltpu.roll(along_y, 1, 0))
    total = total + jnp.where(lanes(shape) == nz - 1, 0.0, pltpu.roll(along_z, nz - 1, 1))
    total = total - jnp.where(lanes(shape) == 0, 0.0, pltpu.roll(along_z, 1, 1))
    return -0.5 * total


def ring(one, two, axis, closed=True, beside=None):
    count = lax.axis_size(axis)
    near = [(i, i ^ 1) for i in range(count)]
    far = [(i, (i + 1 if i % 2 else i - 1) % count) for i in range(count)]
    if not closed:
        far = [(i, j) for i, j in far if abs(i - j) == 1]
    if beside:
        near, far = (
            [(x * count + i, (1 - x) * count + j) for x in range(2) for i, j in pairs] for pairs in (near, far)
        )
        axis = (beside, axis)
    return lax.ppermute(one, axis, near), lax.ppermute(two, axis, far)


def pack_x(index, velocity_far, inv_far, *refs):
    velocity, inv, sems = refs[-3:]
    messages = refs[:-3]
    layers, ny, nz = inv.shape[1:]
    far = inv_far.shape[0] - layers
    shape = (ny, nz)
    only = len(messages) == 1
    first = index[0] == 0

    def copies(n):
        start = jnp.where(first, far, 0) if only else (far, 0)[n]
        part = pl.ds(start, layers)
        yield pltpu.make_async_copy(inv_far.at[part], inv.at[n], sems.at[4 * n])
        for d in range(3):
            yield pltpu.make_async_copy(velocity_far.at[d, part], velocity.at[n, d], sems.at[4 * n + d + 1])

    for n in range(len(messages)):
        for copy in copies(n):
            copy.start()

    def fill(n, start, own, sign):
        message, near = messages[n], velocity.at[n]
        for k in range(REACH):
            message[k * ny : (k + 1) * ny, :] = source(near, start + k, layers)
        base = REACH * ny
        message[base : base + ny, :] = sign * near[0, own]
        base += ny
        for k in range(LAYERS):
            message[base : base + ny, :] = inv[n, k]
            base += ny
        ends = jnp.zeros(shape, F32)
        for k in range(REACH):
            plane_z = near[2, start + k]
            ends = jnp.where(lanes(shape) == 2 * k, plane_z[:, 0:1], ends)
            ends = jnp.where(lanes(shape) == 2 * k + 1, plane_z[:, nz - 1 : nz], ends)
        ends = jnp.transpose(ends)[0 : 2 * REACH]
        message[base : base + 2 * REACH, :] = jnp.concatenate(
            [ends, jnp.zeros((2 * REACH, nz - ny), F32)], axis=1
        )
        base += 2 * REACH
        for k in range(REACH):
            message[base + 2 * k : base + 2 * k + 1, :] = near[1, start + k, 0:1, :]
            message[base + 2 * k + 1 : base + 2 * k + 2, :] = near[1, start + k, ny - 1 : ny, :]

    for n in range(len(messages)):
        for copy in copies(n):
            copy.wait()
    upper = (1, layers - 1, 0.5)
    lower = (0, 0, -0.5)
    if only:
        fill(0, *(jnp.where(first, one, two) for one, two in zip(upper, lower)))
    else:
        fill(0, *upper)
        fill(1, *lower)


def column_ends(message, ny, nz):
    rows = message[pl.ds((REACH + 1 + LAYERS) * ny, 2 * REACH), :]
    return jnp.transpose(jnp.concatenate([rows, jnp.zeros((nz - 2 * REACH, nz), F32)], axis=0))[0:ny]


class Scaled:
    def __init__(self, ref, factor):
        self.ref, self.factor = ref, factor

    def __getitem__(self, where):
        return self.ref[where] * self.factor


class Picked:
    def __init__(self, first, one, two, there):
        self.first, self.one, self.two, self.factor = first, one, two, jnp.where(there, 1.0, 0.0)

    def __getitem__(self, where):
        return jnp.where(self.first, self.one[where], self.two[where]) * self.factor


def sides(index, axis, messages):
    here, count = index[2 * axis], index[2 * axis + 1]
    same, (one, two) = here % 2 == 0, messages
    return Picked(same, two, one, here > 0), Picked(same, one, two, here < count - 1)


def sides_x(index, messages):
    if len(messages) == 2:
        return messages
    first = jnp.where(index[0] == 0, 1.0, 0.0)
    return Scaled(messages[0], 1.0 - first), Scaled(messages[0], first)


EARLY = (LAYERS + 1) // 2
EACH = REACH + 1 + LAYERS + 1


def put(up, down, pair, parity, rows_rhs, ghost, rows_inv, first, last, same=None):
    offset = parity * EACH
    row = (1, up.shape[2])

    def store(start, count, lower, upper):
        if same is not None:
            lower, upper = jnp.where(same, lower, upper), jnp.where(same, upper, lower)
        up[pair, pl.ds(offset + start, count), :] = upper
        down[pair, pl.ds(offset + start, count), :] = lower

    store(0, REACH, *rows_rhs)
    store(REACH, 1, -0.5 * ghost[0], 0.5 * ghost[1])
    store(REACH + 1, LAYERS, *rows_inv)
    both = []
    for part in range(2):
        ends = jnp.zeros(row, F32)
        for k in range(REACH):
            ends = jnp.where(lanes(row) == 2 * k, first[part][k : k + 1], ends)
            ends = jnp.where(lanes(row) == 2 * k + 1, last[part][k : k + 1], ends)
        both.append(ends)
    store(EACH - 1, 1, *both)


def put_own(up, down, velocity, inv, rhs, x, pair, parity, extra, same=None):
    ny, nz = inv.shape[1:]
    low, high = rhs[x, 0:REACH, :], rhs[x, ny - REACH : ny, :]
    if extra is not None:
        low = low + extra[pl.ds(REACH * ny, REACH), :]
        high = high + extra[pl.ds((REACH + 1) * ny - REACH, REACH), :]
    ghost = (velocity[1, x, 0:1, :], velocity[1, x, ny - 1 : ny, :])
    rows_inv = (inv[x, 0:LAYERS, :], inv[x, ny - LAYERS : ny, :])
    head, tail = velocity[2, x, 0:REACH, :], velocity[2, x, ny - REACH : ny, :]
    first = (head[:, 0:1], tail[:, 0:1])
    last = (head[:, nz - 1 : nz], tail[:, nz - 1 : nz])
    put(up, down, pair, parity, (low, high), ghost, rows_inv, first, last, same)


def put_rows(up, down, pair, start, lower, upper, same):
    up[pair, pl.ds(start, REACH), :] = jnp.where(same, upper, lower)
    down[pair, pl.ds(start, REACH), :] = jnp.where(same, lower, upper)


def pack_y_own(index, velocity, inv, sent, rhs, up, down, *across):
    del sent
    nx, ny, nz = rhs.shape
    same = index[2] % 2 == 0

    def plane(x, carry):
        rhs[x] = source(velocity, x, nx)
        return carry

    lax.fori_loop(0, nx, plane, 0, unroll=4)

    def planes(n, carry):
        for parity in range(2):
            put_own(up, down, velocity, inv, rhs, 2 * n + parity, n, parity, None, same)
        return carry

    def edge_rows(x):
        return velocity[0, x, 0:REACH, :], velocity[0, x, ny - REACH : ny, :]

    if across:
        first = index[0] == 0
        for k in range(LAYERS):
            x = jnp.where(first, nx - LAYERS + k, k)
            put_own(*across, velocity, inv, rhs, x, 0, k, None, same)
        rows = edge_rows(jnp.where(first, nx - 1, 0))
        sign = jnp.where(first, 0.5, -0.5)
        put_rows(*across, 0, LAYERS * EACH, sign * rows[0], sign * rows[1], same)
    lax.fori_loop(0, nx // 2, planes, 0, unroll=4)
    put_rows(up, down, nx // 2, 0, *edge_rows(0), same)
    put_rows(up, down, nx // 2, REACH, *edge_rows(nx - 1), same)


def pack_y_halo(index, velocity, inv, rhs, *refs):
    (below, above), (up, down) = sides_x(index, refs[:-2]), refs[-2:]
    same = index[2] % 2 == 0
    nx, ny, nz = inv.shape
    skip = (nx + 2 * LAYERS) // 2 - 2 * EARLY

    def halo(x, message, k_rhs, k_inv, extra):
        pair = x // 2 if x // 2 < EARLY else x // 2 - skip
        base = (REACH + 1 + k_inv) * ny
        rows_inv = (message[pl.ds(base, LAYERS), :], message[pl.ds(base + ny - LAYERS, LAYERS), :])
        zero_row = jnp.zeros((1, nz), F32)
        zero = jnp.zeros((REACH, nz), F32)
        if k_rhs is None:
            column = jnp.zeros((REACH, 1), F32)
            put(up, down, pair, x % 2, (zero, zero), (zero_row, zero_row), rows_inv, (column, column), (column, column), same)
            return
        low, high = message[pl.ds(k_rhs * ny, REACH), :], message[pl.ds((k_rhs + 1) * ny - REACH, REACH), :]
        if extra is not None:
            sign, source = extra
            low = low + sign * velocity[0, source, 0:REACH, :]
            high = high + sign * velocity[0, source, ny - REACH : ny, :]
        lines = (REACH + 1 + LAYERS) * ny + 2 * REACH + 2 * k_rhs
        ghost = (message[pl.ds(lines, 1), :], message[pl.ds(lines + 1, 1), :])
        ends = column_ends(message, ny, nz)
        head, tail = ends[0:REACH], ends[ny - REACH : ny]
        first = (head[:, 2 * k_rhs : 2 * k_rhs + 1], tail[:, 2 * k_rhs : 2 * k_rhs + 1])
        last = (head[:, 2 * k_rhs + 1 : 2 * k_rhs + 2], tail[:, 2 * k_rhs + 1 : 2 * k_rhs + 2])
        put(up, down, pair, x % 2, (low, high), ghost, rows_inv, first, last, same)

    for k in range(LAYERS):
        halo(k, below, k - 1 if k else None, k, (-0.5, 0) if k == LAYERS - 1 else None)
        halo(
            nx + LAYERS + k,
            above,
            k if k < REACH else None,
            k,
            (0.5, nx - 1) if k == 0 else None,
        )
    put_own(up, down, velocity, inv, rhs, 0, EARLY - 1, 1, below, same)
    put_own(up, down, velocity, inv, rhs, nx - 1, EARLY, 0, above, same)


def pack_z(across, index, velocity, inv, rhs, *refs):
    (below, above), received = sides_x(index, refs[:-16]), refs[-16:-12]
    received = [*sides(index, 1, received[:2]), *sides(index, 1, received[2:])]
    same = index[4] % 2 == 0
    rhs_far, inv_far, up, down, strip_rhs_far, strip_inv_far = refs[-12:-6]
    rhs_wide, inv_wide, ends, strip_rhs, strip_inv, sems = refs[-6:]
    nx, ny, nz = inv.shape
    wide = nx + 2 * LAYERS
    rows = ny + 2 * WIDE
    mine = pl.ds(WIDE, ny)
    edge = (WIDE, nz)
    groups = strip_rhs.shape[0]

    columns = [column_ends(message, ny, nz) for message in (below, above)]
    for k in range(LAYERS):
        for message, line, x, layer in (
            (below, columns[0], k, k - 1),
            (above, columns[1], nx + LAYERS + k, k if k < REACH else -1),
        ):
            base = (REACH + 1 + k) * ny
            inv_wide[x, mine, :] = message[pl.ds(base, ny), :]
            if layer < 0:
                rhs_wide[x, mine, :] = jnp.zeros((ny, nz), F32)
                ends[x, mine, :] = jnp.zeros((ny, nz), F32)
                continue
            part = message[pl.ds(layer * ny, ny), :]
            if x == LAYERS - 1:
                part = part - 0.5 * velocity[0, 0]
            if x == nx + LAYERS:
                part = part + 0.5 * velocity[0, nx - 1]
            rhs_wide[x, mine, :] = part
            ends[x, mine, :] = jnp.where(
                lanes((ny, nz)) == 0, line[:, 2 * layer : 2 * layer + 1], line[:, 2 * layer + 1 : 2 * layer + 2]
            )

    def plane(x, carry):
        inv_wide[x + LAYERS, mine, :] = inv[x]
        rhs_wide[x + LAYERS, mine, :] = rhs[x]
        ends[x + LAYERS, mine, :] = velocity[2, x]
        return carry

    lax.fori_loop(0, nx, plane, 0, unroll=4)
    rhs_wide[LAYERS, mine, :] += below[pl.ds(REACH * ny, ny), :]
    rhs_wide[LAYERS + nx - 1, mine, :] += above[pl.ds(REACH * ny, ny), :]
    for ref in (rhs_wide, inv_wide, ends):
        for x in range(wide, ref.shape[0]):
            ref[x] = jnp.zeros((rows, nz), F32)

    first = index[0] == 0
    own, far = received[:2], received[2:]

    def from_pair(refs, pair, parity):
        values = [ref[pair] for ref in refs]
        if isinstance(parity, int):
            return [(pltpu.roll(value, ROWS - EACH, 0) if parity else value)[0:SLOT] for value in values]
        return [jnp.where(parity == 0, value, pltpu.roll(value, ROWS - EACH, 0))[0:SLOT] for value in values]

    def extra(refs, pair, start, factor):
        values = [ref[pair] for ref in refs]
        size = values[0].shape[0]
        values = [pltpu.roll(value, (size - start) % size, 0)[0:SLOT] for value in values]
        return [jnp.where(sublanes((SLOT, nz)) < REACH, factor * value, 0.0) for value in values]

    def rows_of(x):
        if not isinstance(x, int):
            return from_pair(own, (x - LAYERS) // 2, (x - LAYERS) % 2)
        inside = LAYERS <= x < LAYERS + nx
        upper = x >= LAYERS + nx - 1
        if not across:
            return from_pair(far, x // 2 - (wide // 2 - 2 * EARLY if upper else 0), x % 2)
        there = jnp.where(first, 1.0, 0.0) if upper else jnp.where(first, 0.0, 1.0)
        if inside:
            values = from_pair(own, (x - LAYERS) // 2, (x - LAYERS) % 2)
            rows_at = (0, pl.ds(LAYERS * EACH // SLOT * SLOT, SLOT), slice(None))
            more = extra(far, rows_at, LAYERS * EACH % SLOT, there)
        else:
            k = x - LAYERS - nx if upper else x
            values = [there * ref[0, pl.ds(k * EACH, SLOT), :] for ref in far]
            if x == LAYERS - 1:
                more = extra(own, nx // 2, 0, -0.5)
            elif x == LAYERS + nx:
                more = extra(own, nx // 2, REACH, 0.5)
            else:
                return values
        return [one + two for one, two in zip(values, more)]

    def finish(x, ghost_low, ghost_high):
        low, high = rows_of(x)
        part = pltpu.roll(low, WIDE - REACH, 0)[0:WIDE]
        part = jnp.where(sublanes(edge) >= WIDE - REACH, part, 0.0)
        part = part - jnp.where(sublanes(edge) == WIDE - 1, 0.5 * ghost_low, 0.0)
        rhs_wide[x, 0:WIDE, :] = part
        part = pltpu.roll(low, SLOT - (REACH + 1) + WIDE - LAYERS, 0)[0:WIDE]
        inv_wide[x, 0:WIDE, :] = jnp.where(sublanes(edge) >= WIDE - LAYERS, part, 0.0)
        part = jnp.where(sublanes(edge) < REACH, high[0:WIDE], 0.0)
        part = part + jnp.where(sublanes(edge) == 0, 0.5 * ghost_high, 0.0)
        rhs_wide[x, WIDE + ny : rows, :] = part
        part = pltpu.roll(high, SLOT - (REACH + 1), 0)[0:WIDE]
        inv_wide[x, WIDE + ny : rows, :] = jnp.where(sublanes(edge) < LAYERS, part, 0.0)
        head = rhs_wide[x, WIDE : 2 * WIDE, :]
        rhs_wide[x, WIDE : 2 * WIDE, :] = head + jnp.where(sublanes(edge) == 0, low[REACH : REACH + 1], 0.0)
        tail = rhs_wide[x, ny : WIDE + ny, :]
        rhs_wide[x, ny : WIDE + ny, :] = tail + jnp.where(
            sublanes(edge) == WIDE - 1, high[REACH : REACH + 1], 0.0
        )
        for message, start, place in ((low, WIDE - REACH, 0), (high, 0, WIDE + ny)):
            line = message[EACH - 1 : EACH]
            one = jnp.zeros(edge, F32)
            two = jnp.zeros(edge, F32)
            for k in range(REACH):
                here = sublanes(edge) == start + k
                one = jnp.where(here, line[:, 2 * k : 2 * k + 1], one)
                two = jnp.where(here, line[:, 2 * k + 1 : 2 * k + 2], two)
            ends[x, place : place + WIDE, :] = jnp.where(lanes(edge) == 0, one, two)

    for k in range(LAYERS):
        for message, x, layer in ((below, k, k - 1), (above, nx + LAYERS + k, k if k < REACH else -1)):
            lines = (REACH + 1 + LAYERS) * ny + 2 * REACH + 2 * layer
            if layer < 0:
                zero = jnp.zeros((1, nz), F32)
                finish(x, zero, zero)
            else:
                finish(x, message[pl.ds(lines, 1), :], message[pl.ds(lines + 1, 1), :])

    def middle(x, carry):
        finish(x + LAYERS, velocity[1, x, 0:1, :], velocity[1, x, ny - 1 : ny, :])
        return carry

    lax.fori_loop(1, nx - 1, middle, 0, unroll=30)
    for x in (0, nx - 1):
        finish(x + LAYERS, velocity[1, x, 0:1, :], velocity[1, x, ny - 1 : ny, :])
    copies = [
        pltpu.make_async_copy(ref.at[pl.ds(0, wide)], far, sems.at[n])
        for n, (ref, far) in enumerate(((rhs_wide, rhs_far), (inv_wide, inv_far)))
    ]
    for copy in copies:
        copy.start()

    whole = (rows, nz)
    lane = lanes(whole)
    place = lane % SPAN

    def back(value, step):
        return pltpu.roll(value, nz - step, 1)

    def gather(ref, g):
        value = None
        for n in range(nz // SPAN):
            moved = pltpu.roll(ref[g + n * groups], n * SPAN + STRIP, 1)
            value = moved if value is None else jnp.where(lane >= n * SPAN, moved, value)
        return value

    def pack(g):
        r, i, e = gather(rhs_wide, g), gather(inv_wide, g), gather(ends, g)
        apart = SPAN - 2 * STRIP
        for ref, value in ((strip_rhs, r), (strip_inv, i)):
            out = jnp.where(place < STRIP, value, 0.0)
            ref[g] = jnp.where(place >= SPAN - STRIP, pltpu.roll(value, apart, 1), out)
        ghost = jnp.where(place == STRIP, 0.5 * pltpu.roll(e, 1, 1), 0.0)
        ghost = jnp.where(place == SPAN - STRIP - 1, -0.5 * pltpu.roll(e, apart - 1, 1), ghost)
        strip_rhs[g] += ghost
        out = jnp.where(place < REACH, back(r, STRIP - REACH), 0.0)
        out = jnp.where(place == REACH, 0.5 * back(e, STRIP - 1 - REACH), out)
        here = (place > REACH) & (place <= REACH + LAYERS)
        higher = jnp.where(here, pltpu.roll(i, (nz + REACH + 1 + LAYERS - STRIP) % nz, 1), out)
        out = jnp.where(place < REACH, back(r, STRIP), 0.0)
        out = jnp.where(place == REACH, -0.5 * back(e, STRIP - REACH), out)
        return higher, jnp.where(here, back(i, STRIP - REACH - 1), out)

    halves = up.shape[0]

    def both(n, carry):
        one, two = pack(n)
        up[n] = jnp.where(same, one, two)
        down[n] = jnp.where(same, two, one)
        return carry

    lax.fori_loop(0, halves, both, 0, unroll=3)

    def more(n, carry):
        one, two = pack(n + halves)
        up[n] += pltpu.roll(jnp.where(same, one, two), SPAN // 2, 1)
        down[n] += pltpu.roll(jnp.where(same, two, one), SPAN // 2, 1)
        return carry

    lax.fori_loop(0, groups - halves, more, 0, unroll=5)
    for ref, far in ((strip_rhs, strip_rhs_far), (strip_inv, strip_inv_far)):
        copies.append(pltpu.make_async_copy(ref, far, sems.at[len(copies)]))
        copies[-1].start()
    for copy in copies:
        copy.wait()


def shifted(ref, x, t, step):
    rows = ref.shape[1]
    start = t * WIDE + step
    if start < 0:
        return pltpu.roll(ref[x, 0:WIDE, :], 1, 0)
    if start + WIDE > rows:
        return pltpu.roll(ref[x, rows - WIDE : rows, :], WIDE - 1, 0)
    return ref[x, start : start + WIDE, :]


class Stencil:
    def __init__(self, inv, root, ax, ay, az, vs, planes, edges=None, unroll=10):
        self.inv, self.root, self.ax, self.ay, self.az, self.vs = inv, root, ax, ay, az, vs
        self.planes, self.edges, self.unroll = planes, edges or (lambda ref: None), unroll
        self.count, self.rows, self.nz = inv.shape
        self.tiles = self.rows // WIDE

    def here(self, t):
        return slice(t * WIDE, (t + 1) * WIDE)

    def right(self, value):
        return pltpu.roll(value, self.nz - 1, 1)

    def left(self, value):
        return pltpu.roll(value, 1, 1)

    def prepare(self, rhs, parts=None):
        inv, root = self.inv, self.root
        self.edges(inv)

        def scales(x, carry):
            writes = []
            for t in range(self.tiles):
                here = self.here(t)
                c = inv[x, here, :]
                total = (inv[x + 1, here, :] + inv[x - 1, here, :]) + (self.right(c) + self.left(c))
                total = total + (shifted(inv, x, t, 1) + shifted(inv, x, t, -1))
                value = jnp.where(c > 0.0, lax.rsqrt(SHIFT + 0.5 * (6.0 * c + total)), 0.0)
                writes.append((here, value, rhs[x, here, :] * value))
            for here, one, two in writes:
                root[x, here, :] = one
                self.vs[0][x, here, :] = two
            return carry

        for start, stop in parts or [(1, self.count - 1)]:
            lax.fori_loop(start, stop, scales, 0, unroll=self.unroll)
        zero = jnp.zeros((self.rows, self.nz), F32)
        for ref in (root, self.vs[0]):
            ref[0] = zero
            ref[self.count - 1] = zero
            self.edges(ref)

        def couplings(x, carry):
            writes = []
            for t in range(self.tiles):
                here = self.here(t)
                c, d = inv[x, here, :], root[x, here, :]
                half = 0.5 * d
                writes.append(
                    (
                        here,
                        (c + inv[x + 1, here, :]) * (half * root[x + 1, here, :]),
                        (c + shifted(inv, x, t, 1)) * (half * shifted(root, x, t, 1)),
                        (c + self.right(c)) * (half * self.right(d)),
                    )
                )
            for here, x_face, y_face, z_face in writes:
                self.ax[x, here, :] = x_face
                self.ay[x, here, :] = y_face
                self.az[x, here, :] = z_face
            return carry

        lax.fori_loop(1, self.count - 1, couplings, 0, unroll=self.unroll)
        self.ax[0] = zero
        self.edges(self.ax)

    def couple(self, k, x, t):
        here = self.here(t)
        v, ax, ay = self.vs[k], self.ax, self.ay
        c, f = v[x, here, :], self.az[x, here, :]
        total = ax[x, here, :] * v[x + 1, here, :] + ax[x - 1, here, :] * v[x - 1, here, :]
        total = total + (f * self.right(c) + self.left(f * c))
        total = total + ay[x, here, :] * shifted(v, x, t, 1)
        return c, total + shifted(ay, x, t, -1) * shifted(v, x, t, -1)

    def extend(self, k):
        scale = 1.0 - NEWTON[k]

        def step(x, carry):
            writes = []
            for t in range(self.tiles):
                c, total = self.couple(k, x, t)
                writes.append((t, scale * c - total if scale else -total))
            for t, value in writes:
                self.vs[k + 1][x, self.here(t), :] = value
            return carry

        start, stop = self.planes(k)
        lax.fori_loop(start, stop, step, 0, unroll=self.unroll)
        self.edges(self.vs[k + 1])

    def products(self, start, stop, mask):
        def measure(x, sums):
            sums = list(sums)
            for t in range(1, self.tiles - 1):
                keep = mask(x)
                v = [self.vs[k][x, self.here(t), :] for k in range(ITERS)]
                own, total = self.couple(ITERS - 1, x, t)
                kept = [jnp.where(keep, one, 0.0) for one in v]
                for n, (a, b) in enumerate(PAIRS):
                    sums[n] = sums[n] + v[a] * kept[b]
                sums[-1] = sums[-1] + kept[-1] * (own - total)
            return tuple(sums)

        zero = jnp.zeros((WIDE, self.nz), F32)
        return lax.fori_loop(start, stop, measure, (zero,) * (len(PAIRS) + 1), unroll=4)


def basis_main(rhs_far, inv_far, *refs):
    outs, sums = refs[: ITERS + 1], refs[ITERS + 1]
    rhs, inv, root, ax, ay, az = refs[ITERS + 2 : ITERS + 8]
    vs, sems = refs[ITERS + 8 : -1], refs[-1]
    wide, rows, nz = ax.shape
    nx = wide - 2 * LAYERS
    batch = 4
    bounds = [n * wide // batch for n in range(batch + 1)]
    loads = []
    for n in range(batch):
        part = pl.ds(bounds[n], bounds[n + 1] - bounds[n])
        for far, ref in ((inv_far, inv), (rhs_far, rhs)):
            loads.append(pltpu.make_async_copy(far.at[part], ref.at[part], sems.at[ITERS + 1 + len(loads)]))
            loads[-1].start()

    def ready():
        for n in range(batch):
            for load in loads[2 * n : 2 * n + 2]:
                load.wait()
            yield max(bounds[n] - 1, 1), bounds[n + 1] - 1

    stencil = Stencil(inv, root, ax, ay, az, vs, lambda k: (2 + k, wide - 2 - k))
    copies = []

    def send(n, ref):
        copy = pltpu.make_async_copy(ref.at[pl.ds(LAYERS - 1, nx + 2)], outs[n], sems.at[n])
        copy.start()
        copies.append(copy)

    stencil.prepare(rhs, ready())
    send(ITERS, root)
    send(0, vs[0])
    for k in range(ITERS - 1):
        stencil.extend(k)
        send(k + 1, vs[k + 1])
    lane = lanes((WIDE, nz))
    inner = (lane > REACH) & (lane < nz - 1 - REACH)
    for n, one in enumerate(stencil.products(LAYERS, LAYERS + nx, lambda x: inner)):
        sums[n] = one
    for copy in copies:
        copy.wait()


def basis_strips(nx, index, rhs_far, inv_far, one, two, sums, *refs):
    before, after = sides(index, 2, (one, two))
    outs, dots = refs[:ITERS], refs[ITERS]
    rhs, inv, root, ax, ay, az = refs[ITERS + 1 : ITERS + 7]
    vs, outs_near = refs[ITERS + 7 : 2 * ITERS + 7], refs[2 * ITERS + 7 : 3 * ITERS + 7]
    strip_rhs, strip_inv, sems = refs[-3:]
    groups, rows, nz = strip_inv.shape
    loads = [
        pltpu.make_async_copy(far, ref, sems.at[ITERS + n])
        for n, (far, ref) in enumerate(((rhs_far, strip_rhs), (inv_far, strip_inv)))
    ]
    for load in loads:
        load.start()
    for load in loads:
        load.wait()
    halves = one.shape[0]
    whole = (rows, nz)
    place = lanes(whole) % SPAN

    def edges(ref):
        ref[0] = pltpu.roll(ref[groups], SPAN, 1)
        ref[groups + 1] = pltpu.roll(ref[1], nz - SPAN, 1)

    def receive(g, low, high):
        start = SPAN - STRIP - LAYERS
        moved = pltpu.roll(low, start + 1, 1)
        r = strip_rhs[g] + jnp.where((place > start) & (place <= SPAN - STRIP), moved, 0.0)
        moved = pltpu.roll(low, start - REACH - 1, 1)
        i = strip_inv[g] + jnp.where((place >= start) & (place < SPAN - STRIP), moved, 0.0)
        moved = pltpu.roll(high, STRIP, 1)
        r = r + jnp.where((place >= STRIP) & (place < STRIP + REACH), moved, 0.0)
        moved = pltpu.roll(high, STRIP - REACH - 1, 1)
        r = r + jnp.where(place == STRIP - 1, moved, 0.0)
        i = i + jnp.where((place >= STRIP) & (place < STRIP + LAYERS), moved, 0.0)
        rhs[g + 1] = r
        inv[g + 1] = i

    def first(n, carry):
        receive(n, before[n], after[n])
        return carry

    def second(n, carry):
        half = nz - SPAN // 2
        receive(n + halves, pltpu.roll(before[n], half, 1), pltpu.roll(after[n], half, 1))
        return carry

    lax.fori_loop(0, halves, first, 0, unroll=3)
    lax.fori_loop(0, groups - halves, second, 0, unroll=3)
    stencil = Stencil(inv, root, ax, ay, az, vs, lambda k: (1, groups + 1), edges, groups)
    stencil.prepare(rhs)
    copies = []

    def result(k):
        ref = outs_near[k]

        def plane(g, carry):
            ref[g] = vs[k][g] * root[g]
            return carry

        lax.fori_loop(1, groups + 1, plane, 0, unroll=groups)
        copies.append(pltpu.make_async_copy(ref.at[pl.ds(1, groups)], outs[k], sems.at[k]))
        copies[-1].start()

    result(0)
    for k in range(ITERS - 1):
        stencil.extend(k)
        result(k + 1)
    lane = lanes((WIDE, nz))
    part = lane // SPAN
    spot = lane % SPAN
    ends = ((spot >= STRIP - LAYERS) & (spot < STRIP)) | (
        (spot >= SPAN - STRIP) & (spot < SPAN - STRIP + LAYERS)
    )

    def mask(x):
        plane = x - 1 + part * groups
        return ends & (plane >= LAYERS) & (plane < LAYERS + nx)

    totals = []
    for n, one in enumerate(stencil.products(1, groups + 1, mask)):
        line = jnp.sum(one + sums[n], axis=0, keepdims=True)
        totals.append(line + pltpu.roll(line, nz // 2, 1))
    row = sublanes((WIDE, nz))
    message = jnp.zeros((WIDE, nz), F32)
    for n, line in enumerate(totals):
        half = lane < nz // 2 if n < WIDE else lane >= nz // 2
        message = jnp.where((row == n % WIDE) & half, line, message)

    def send(n, carry):
        dots[n] = message
        return carry

    lax.fori_loop(0, dots.shape[0], send, 0, unroll=8)

    for copy in copies:
        copy.wait()


def coefficients(dots):
    half = lanes(dots.shape) < dots.shape[1] // 2
    one = jnp.sum(jnp.where(half, dots, 0.0), axis=1, keepdims=True)
    two = jnp.sum(jnp.where(half, 0.0, dots), axis=1, keepdims=True)

    def entry(n):
        return one[n : n + 1] if n < WIDE else two[n - WIDE : n - WIDE + 1]

    gram = {}
    for n, (a, b) in enumerate(PAIRS):
        gram[a, b] = gram[b, a] = entry(n)
    last = ITERS - 1
    image = {}
    for b in range(last):
        for a in range(ITERS):
            image[a, b] = gram[a, b + 1]
            if NEWTON[b]:
                image[a, b] = image[a, b] + NEWTON[b] * gram[a, b]
    for a in range(last):
        image[a, last] = image[last, a]
    image[last, last] = entry(len(PAIRS))

    def product(table, one, two):
        total = None
        for a, left in enumerate(one):
            for b, right in enumerate(two):
                term = left * right * table[a, b]
                total = term if total is None else total + term
        return total

    unit = jnp.ones((1, 1), F32)
    pressure = []
    precond = [unit]
    direction = [unit]
    rz = gram[0, 0]
    for iteration in range(ITERS):
        alpha = rz / product(image, direction, direction)
        pressure = [
            (pressure[n] if n < len(pressure) else 0.0) + alpha * one for n, one in enumerate(direction)
        ]
        if iteration == last:
            break
        moved = []
        for n in range(len(direction) + 1):
            value = None
            if n < len(direction) and NEWTON[n]:
                value = NEWTON[n] * direction[n]
            if n > 0:
                value = direction[n - 1] if value is None else value + direction[n - 1]
            moved.append(value)
        fresh_precond = []
        for n, one in enumerate(moved):
            old = precond[n] if n < len(precond) else None
            if one is None:
                fresh_precond.append(old)
            else:
                fresh_precond.append(-alpha * one if old is None else old - alpha * one)
        precond = fresh_precond
        fresh = product(gram, precond, precond)
        beta = fresh / rz
        direction = [
            one + beta * direction[n] if n < len(direction) else one for n, one in enumerate(precond)
        ]
        rz = fresh
    return pressure


def finish(dots, columns, *refs):
    inputs = 2 * ITERS + 3
    pressure_far, corrected_far, keep, keep_more, send, p, gaps, mixed, cut, pressure, corrected = refs[inputs : inputs + 11]
    held, sems = refs[inputs + 11 : -1], refs[-1]
    strips, spans, roots = held[:ITERS], held[ITERS : 2 * ITERS], held[2 * ITERS]
    velocity, inv = held[2 * ITERS + 1 :]
    nx, ny, nz = inv.shape
    batch = 4
    each = nx // batch
    used = 0

    def start(far, ref):
        nonlocal used
        copy = pltpu.make_async_copy(far, ref, sems.at[used])
        used += 1
        copy.start()
        return copy

    strip_loads = [start(far, ref) for far, ref in zip(refs[:ITERS], strips)]
    span_loads, other_loads, bounds = [], [], []
    for n in range(batch):
        low, high = (n * each + 2 if n else 0), (n + 1) * each + 2
        bounds.append((low, high))
        part = pl.ds(low, high - low)
        pairs = zip(refs[ITERS : 2 * ITERS + 1], held[ITERS : 2 * ITERS + 1])
        span_loads.append([start(far.at[part], ref.at[part]) for far, ref in pairs])
        part = pl.ds(n * each, each)
        other_loads.append(
            [start(refs[2 * ITERS + 1].at[d, part], velocity.at[d, part]) for d in range(3)]
            + [start(refs[2 * ITERS + 2].at[part], inv.at[part])]
        )
    shape = (ny, nz)
    groups = mixed.shape[0]
    total = dots[0]
    for n in range(1, dots.shape[0]):
        total = total + dots[n]
    weights = coefficients(total)

    def strip(g, carry):
        value = weights[0] * strips[0][g]
        for k in range(1, ITERS):
            value = value + weights[k] * strips[k][g]
        mixed[g] = value
        return carry

    for load in strip_loads:
        load.wait()
    lax.fori_loop(0, groups, strip, 0, unroll=4)
    mine = slice(WIDE, WIDE + ny)
    lane = lanes(spans[0].shape[1:])

    def combine(x, carry):
        value = weights[0] * spans[0][x]
        for k in range(1, ITERS):
            value = value + weights[k] * spans[k][x]
        value = value * roots[x]
        plane = x + LAYERS - 1
        ends = mixed[plane % groups]
        start = plane // groups * SPAN
        last = pltpu.roll(ends, lax.rem(2 * nz - STRIP - start, nz), 1)
        first = pltpu.roll(ends, lax.rem(nz + STRIP - SPAN - start + nz, nz), 1)
        value = jnp.where(lane < LAYERS, first, jnp.where(lane >= nz - LAYERS, last, value))
        p[x] = value
        after = pltpu.roll(jnp.where(lane == 0, last, value), nz - 1, 1)
        before = pltpu.roll(jnp.where(lane == nz - 1, first, value), 1, 1)
        gaps[x] = (after - before)[mine]
        return carry

    half = columns.shape[0] // 2

    def pair(n, carry):
        for which in range(2):
            x = 2 * n + which
            centre = p[x + 1, mine, :]
            pressure[x] = centre
            half_inv = 0.5 * inv[x]
            slopes = (
                p[x + 2, mine, :] - p[x, mine, :],
                p[x + 1, WIDE + 1 : WIDE + 1 + ny, :] - p[x + 1, WIDE - 1 : WIDE - 1 + ny, :],
                gaps[x + 1],
            )
            fields = [velocity[d, x] - half_inv * slopes[d] for d in range(3)] + [centre]
            for d in range(3):
                corrected[d, x] = fields[d]
            for f, field in enumerate(fields):
                high = field.astype(BF16)
                low = (field - high.astype(F32)).astype(BF16)
                cut[f, which * ny : (which + 1) * ny, 0:nz] = high
                cut[f, which * ny : (which + 1) * ny, nz : 2 * nz] = low
        for f in range(4):
            out = lax.dot_general(
                columns[...], cut[f], (((1,), (1,)), ((), ())), preferred_element_type=F32
            )
            out = out[:half] + out[half:]
            block = f * (nx // 2) + n
            quarter = half // 4
            keep[block] = out[0:quarter]
            keep_more[block] = out[quarter : 2 * quarter]
            send[0, block] = out[2 * quarter : 3 * quarter]
            send[1, block] = out[3 * quarter :]
        return carry

    stores = []
    for n in range(batch):
        for load in span_loads[n]:
            load.wait()
        lax.fori_loop(*bounds[n], combine, 0, unroll=4)
        for load in other_loads[n]:
            load.wait()
        lax.fori_loop(n * each // 2, (n + 1) * each // 2, pair, 0, unroll=4)
        part = pl.ds(n * each, each)
        stores.append(start(pressure.at[part], pressure_far.at[part]))
        for d in range(3):
            stores.append(start(corrected.at[d, part], corrected_far.at[d, part]))
    for store in stores:
        store.wait()


def tables(count_x, factor_y, factor_x, y_high, y_low, x_high, x_low, spread_high, spread_low):
    ny, rank = factor_y.shape
    nx = factor_x.shape[0]
    planes = y_high.shape[0] // ny
    nz = x_high.shape[1] // rank * planes
    count = y_high.shape[1] // nz
    ranks = rank // count
    wide = jnp.concatenate([factor_y[...], jnp.zeros((ny, nz - rank), F32)], axis=1)
    lane = lanes((ny, nz))
    for h in range(count):
        value = pltpu.roll(wide, (nz - h * ranks) % nz, 1)
        value = jnp.where(lane < ranks, value, 0.0)
        step = ranks
        while step < nz:
            value = value + pltpu.roll(value, step, 1)
            step *= 2
        for n in range(planes):
            high, low = split(jnp.where(lane // ranks == n, value, 0.0))
            y_high[n * ny : (n + 1) * ny, h * nz : (h + 1) * nz] = high
            y_low[n * ny : (n + 1) * ny, h * nz : (h + 1) * nz] = low
    width = x_high.shape[1]
    shape = (rank, width)
    own = rank // count_x
    lane = lanes(shape)
    copy = lane // (ranks * own) * own + lane % own == sublanes(shape)
    copy = jnp.where(copy, 1.0, 0.0).astype(BF16)
    for ref, value in zip((spread_high, spread_low), split(factor_x[...])):
        ref[...] = jnp.dot(value, copy, preferred_element_type=F32)
    shape = (ranks, width)
    here = lanes(shape) // own % ranks == sublanes(shape)

    def row(i, carry):
        at = pl.ds(pl.multiple_of(i * ranks, ranks), ranks)
        x_high[at, :] = jnp.where(here, spread_high[pl.ds(i, 1), :], 0.0).astype(BF16)
        x_low[at, :] = jnp.where(here, spread_low[pl.ds(i, 1), :], 0.0).astype(BF16)
        return carry

    lax.fori_loop(0, nx, row, 0, unroll=4)


def split(value):
    high = value.astype(BF16)
    return high, (value - high.astype(F32)).astype(BF16)


def split_table(value):
    high = lax.reduce_precision(value, exponent_bits=8, mantissa_bits=7)
    return high.astype(BF16), (value - high).astype(BF16)


def three(a, b, dims=(((1,), (0,)), ((), ()))):
    dot = functools.partial(lax.dot_general, dimension_numbers=dims, preferred_element_type=F32)
    (ah, al), (bh, bl) = a, b
    return dot(ah, bh) + (dot(al, bh) + dot(ah, bl))


def rank_y(x, table):
    blocks, ranks, nz = x.shape
    group = table[0].shape[0] // nz
    parts = [
        jnp.concatenate([x[n * group + q] for q in range(group)], axis=1) for n in range(blocks // group)
    ]
    out = three(split(jnp.concatenate(parts, axis=0)), table)
    return [out[:, n * nz : (n + 1) * nz] for n in range(out.shape[1] // nz)]


def tail_one(kept, more, came, high, low, p_send, p_keep, q_send, q_keep, q_more):
    half = kept.shape[0] // 2
    p_send[...] = more[0:half] + came[1, 0:half]
    p_keep[...] = kept[0:half] + came[0, 0:half]
    x = jnp.concatenate([kept[half:] + came[0, half:], more[half:] + came[1, half:]], axis=0)
    q_keep[...], q_more[...], q_send[0], q_send[1] = rank_y(x, (high[...], low[...]))


def tail_two(p_kept, p_came, q_kept, q_more, q_came, high, low, p_send, p_keep, p_more, q_send, q_keep):
    q_send[...] = q_more[...] + q_came[1]
    q_keep[...] = q_kept[...] + q_came[0]
    parts = rank_y(p_kept[...] + p_came[...], (high[...], low[...]))
    p_keep[...], p_more[...], p_send[0], p_send[1] = parts


def tail_three(p_kept, p_more, p_came, q_kept, q_came, p_send, p_keep, q_send, q_keep):
    half = q_keep.shape[0]
    p_send[...] = p_more[...] + p_came[1]
    p_keep[...] = p_kept[...] + p_came[0]
    q_send[...] = q_kept[half:] + q_came[half:]
    q_keep[...] = q_kept[0:half] + q_came[0:half]


def rank_x(ranks, p_kept, p_came, q_kept, q_came, wide_high, wide_low, *outs):
    u = jnp.concatenate([p_kept[...] + p_came[...], q_kept[...] + q_came[...]], axis=0)
    rows, nz = u.shape
    group = wide_high.shape[0] // nz
    parts = []
    for f in range(rows // ranks // group):
        parts.append(
            jnp.concatenate(
                [u[(f * group + q) * ranks : (f * group + q + 1) * ranks] for q in range(group)], axis=1
            )
        )
    x = jnp.concatenate(parts, axis=0)
    out = three(split(x), (wide_high[...], wide_low[...]))
    width = out.shape[1] // len(outs)
    for n, ref in enumerate(outs):
        ref[...] = out[:, n * width : (n + 1) * width]


def last_core(kept, came, core):
    fields, ranks_y, ranks_z, ranks_x = core.shape
    z = kept[...] + came[...]
    for f in range(fields):
        for b in range(ranks_y):
            core[f, b] = z[f * ranks_z : (f + 1) * ranks_z, b * ranks_x : (b + 1) * ranks_x]


def relative(factor, axis):
    count = lax.axis_size(axis)
    order = [0]
    step = 1
    while step < count:
        order = order + [n + step for n in order]
        step *= 2
    bits = count.bit_length() - 1
    order = [sum(((n >> b) & 1) << (bits - 1 - b) for b in range(bits)) for n in range(count)]
    blocks = factor.reshape(factor.shape[0], count, factor.shape[1] // count)
    here = lax.axis_index(axis)
    picked = [
        lax.dynamic_index_in_dim(blocks, jnp.bitwise_xor(here, n), axis=1, keepdims=False) for n in order
    ]
    return jnp.stack(picked, axis=1)


def swap(value, axis, mask):
    count = lax.axis_size(axis)
    return lax.ppermute(value, axis, [(i, i ^ mask) for i in range(count)])


def per_device(velocity, inv_density, factor_x, factor_y, factor_z):
    nx, ny, nz = inv_density.shape
    wide, rows = nx + 2 * LAYERS, ny + 2 * WIDE
    count_x, count_y, count_z = (lax.axis_size(axis) for axis in AXES)
    devices = count_x * count_y * count_z
    cells = (nx, ny, nz)
    rank = factor_x.shape[1]
    index_x = lax.axis_index("gx").reshape(1)
    index = jnp.stack([jnp.int32(f(axis)) for axis in AXES for f in (lax.axis_index, lax.axis_size)])

    shape = ((REACH + 1 + LAYERS) * ny + 4 * REACH, nz)
    number = 1 if count_x == 2 else 2
    sent = call(
        pack_x,
        [shape] * number,
        [index_x, velocity, inv_density],
        scratch=[(number, 3, LAYERS, ny, nz), (number, LAYERS, ny, nz)],
        smem=1,
        far_in=(1, 2),
        sems=4 * number,
    )
    near = [swap(sent[0], "gx", 1)] if count_x == 2 else list(exchange(*sent, "gx"))
    across = count_x == 2
    shape = (nx // 2 + 1, ROWS, nz)
    corner = (1, -(-(LAYERS * EACH + REACH) // SLOT) * SLOT, nz)
    rhs, up, down, *corners = call(
        pack_y_own,
        [cells, shape, shape] + ([corner, corner] if across else []),
        [index, velocity, inv_density, sent[0]],
        smem=1,
        cost=(nx * ny * nz * 10, 6 * cost_of(cells)),
        far_in=(3,),
    )
    received = list(ring(up, down, "gy", closed=False))
    if across:
        received += ring(*corners, "gy", beside="gx", closed=False)
    else:
        shape = (2 * EARLY, ROWS, nz)
        up, down = call(pack_y_halo, [shape, shape], [index, velocity, inv_density, rhs, *near], smem=1)
        received += ring(up, down, "gy")
    parts = nz // SPAN
    groups = -(-wide // parts)
    message = (-(-groups // 2), rows, nz)
    whole = (groups * parts, rows, nz)
    strip = (groups, rows, nz)
    rhs_wide, inv_wide, up, down, strip_rhs, strip_inv = call(
        functools.partial(pack_z, across),
        [(wide, rows, nz)] * 2 + [message, message, strip, strip],
        [index, velocity, inv_density, rhs, *near, *received],
        scratch=[whole] * 3 + [strip] * 2,
        smem=1,
        limit=18,
        far_out=(0, 1, 4, 5),
        sems=4,
    )
    came = ring(up, down, "gz")
    span = (nx + 2, rows, nz)
    whole = (wide, rows, nz)
    *spans, sums = call(
        basis_main,
        [span] * (ITERS + 1) + [(len(PAIRS) + 1, WIDE, nz)],
        [rhs_wide, inv_wide],
        scratch=[whole] * (6 + ITERS),
        limit=22,
        cost=(wide * rows * nz * 100, 7 * cost_of(whole)),
        far_in=(0, 1),
        far_out=range(ITERS + 1),
        sems=ITERS + 9,
    )
    padded = (groups + 2, rows, nz)
    *strips, dots = call(
        functools.partial(basis_strips, nx),
        [strip] * ITERS + [(devices, WIDE, nz)],
        [index, strip_rhs, strip_inv, *came, sums],
        scratch=[padded] * (6 + 2 * ITERS) + [strip] * 2,
        smem=1,
        far_in=(1, 2),
        far_out=range(ITERS),
        sems=ITERS + 2,
    )
    dots = lax.all_to_all(dots, AXES, 0, 0, tiled=True)

    ranks_y, ranks_z = rank // count_y, rank // count_z
    planes = nz // ranks_y
    table_y, table_x = (planes * ny, count_y * nz), (nx * ranks_y, rank * ranks_y)
    y_high, y_low, x_high, x_low = pl.pallas_call(
        functools.partial(tables, count_x),
        out_shape=[jax.ShapeDtypeStruct(one, BF16) for one in (table_y, table_y, table_x, table_x)],
        in_specs=[VMEM] * 2,
        out_specs=[VMEM] * 4,
        scratch_shapes=[pltpu.VMEM((nx, rank * ranks_y), F32)] * 2,
        compiler_params=pltpu.CompilerParams(vmem_limit_bytes=16 * 2**20),
        cost_estimate=pl.CostEstimate(
            flops=4 * nx * ranks_y * rank * ranks_y, bytes_accessed=6 * 2**20, transcendentals=0
        ),
    )(relative(factor_y, "gy").reshape(ny, rank), relative(factor_x, "gx").reshape(nx, rank))
    columns = relative(factor_z, "gz")
    columns = jnp.transpose(columns.reshape(nz, -1))
    high, low = split_table(columns)
    columns = jnp.concatenate(
        [jnp.concatenate([high, high], axis=1), jnp.concatenate([low, low], axis=1)], axis=0
    )
    piece = (4 * nx // 2, ranks_z, nz)
    far = [*strips, *spans, velocity, inv_density]
    pressure, corrected, keep, keep_more, send = call(
        finish,
        [cells, (3,) + cells, piece, piece, (2,) + piece],
        [dots, columns, *far],
        scratch=[span, (nx + 2, ny, nz), strip, pltpu.VMEM((4, 2 * ny, 2 * nz), BF16), cells, (3,) + cells]
        + [one.shape for one in far],
        limit=32,
        far_in=range(2, 2 + len(far)),
        far_out=(0, 1),
        sems=ITERS + 4 * (ITERS + 5) + 16,
    )

    came = swap(send, "gz", 1)
    table = [y_high, y_low]
    part = (piece[0] // 2, ranks_z, nz)
    half = (2 * nx // planes * ranks_z, nz)
    full = (2 * half[0], nz)
    p_send, p_keep, q_send, q_keep, q_more = call(
        tail_one, [part, part, (2,) + full, full, full], [keep, keep_more, came, *table], limit=16
    )
    p_came, q_came = swap(p_send, "gz", 2), swap(q_send, "gy", 1)
    p_send, p_keep, p_more, q_send, q_keep = call(
        tail_two,
        [(2,) + half, half, half, full, full],
        [p_keep, p_came, q_keep, q_more, q_came, *table],
        limit=16,
    )
    p_came, q_came = swap(p_send, "gy", 1), swap(q_send, "gy", 2)
    p_send, p_keep, q_send, q_keep = call(
        tail_three, [half] * 4, [p_keep, p_more, p_came, q_keep, q_came]
    )
    p_came, q_came = swap(p_send, "gy", 2), swap(q_send, "gz", 2)
    half = (4 * ranks_z, rank * ranks_y // 2)
    keep, send = call(
        functools.partial(rank_x, ranks_z),
        [half] * 2,
        [p_keep, p_came, q_keep, q_came, x_high, x_low],
        limit=16,
    )
    mask = 1
    while True:
        came = swap(send, "gx", mask)
        mask *= 2
        if mask >= count_x:
            break
        total = keep + came
        width = total.shape[1] // 2
        keep, send = total[:, :width], total[:, width:]
    core, = call(last_core, [(4, ranks_y, ranks_z, rank // count_x)], [keep, came], limit=16, pinned=(0,))
    return pressure, corrected, jnp.transpose(core, (3, 0, 1, 2))


def solution(mesh):
    placed = (
        P(None, "gx", "gy", "gz"),
        P("gx", "gy", "gz"),
        P("gx", None),
        P("gy", None),
        P("gz", None),
    )
    return jax.shard_map(
        per_device,
        mesh=mesh,
        in_specs=placed,
        out_specs=(P("gx", "gy", "gz"), P(None, "gx", "gy", "gz"), P("gx", None, "gy", "gz")),
        check_vma=False,
    )
```

```python
import functools
import math

import jax
import jax.numpy as jnp
from jax import lax
from jax.experimental import pallas as pl
from jax.experimental.pallas import tpu as pltpu
from jax.sharding import PartitionSpec as P

ITERS = 4
SHIFT = 0.1
AXES = ("gx", "gy", "gz")

REACH = ITERS
LAYERS = ITERS + 1
WIDE = 8
SLOT = 16
STRIP = 2 * LAYERS
SPAN = 32
ROWS = 24
NEWTON = (0.5, 0.5, 0.5)
PAIRS = [(a, b) for a in range(ITERS) for b in range(a, ITERS)]
VMEM = pl.BlockSpec(memory_space=pltpu.VMEM)
SMEM = pl.BlockSpec(memory_space=pltpu.SMEM)
HBM = pl.BlockSpec(memory_space=pltpu.HBM)
F32 = jnp.float32
BF16 = jnp.bfloat16


def call(body, outs, operands, scratch=(), smem=0, limit=12, cost=None, far_in=(), far_out=(), pinned=(), sems=0):
    scratch = [pltpu.VMEM(shape, F32) if isinstance(shape, tuple) else shape for shape in scratch]
    return pl.pallas_call(
        body,
        out_shape=[
            pltpu.HBM(shape, F32)
            if n in far_out or n in pinned
            else jax.ShapeDtypeStruct(shape, F32)
            for n, shape in enumerate(outs)
        ],
        in_specs=[SMEM if n < smem else HBM if n in far_in else VMEM for n in range(len(operands))],
        out_specs=[HBM if n in far_out else VMEM for n in range(len(outs))],
        scratch_shapes=scratch + ([pltpu.SemaphoreType.DMA((sems,))] if sems else []),
        compiler_params=pltpu.CompilerParams(vmem_limit_bytes=limit * 2**20),
        cost_estimate=cost
        and pl.CostEstimate(flops=cost[0], bytes_accessed=cost[1], transcendentals=0),
    )(
        *(
            pltpu.with_memory_space_constraint(one, pltpu.HBM)
            if n in far_in
            else one
            for n, one in enumerate(operands)
        )
    )


def cost_of(shape):
    return 4 * math.prod(shape)


def lanes(shape):
    return lax.broadcasted_iota(jnp.int32, shape, len(shape) - 1)


def sublanes(shape):
    return lax.broadcasted_iota(jnp.int32, shape, len(shape) - 2)


def exchange(up, down, axis):
    count = lax.axis_size(axis)
    ends = count - 1
    below = lax.ppermute(up, axis, [(i, i + 1) for i in range(ends)])
    above = lax.ppermute(down, axis, [(i + 1, i) for i in range(ends)])
    return below, above


def source(velocity, x, nx):
    ny, nz = velocity.shape[2:]
    shape = (ny, nz)
    before = jnp.where(x == 0, 0.0, velocity[0, jnp.maximum(x - 1, 0)])
    after = jnp.where(x == nx - 1, 0.0, velocity[0, jnp.minimum(x + 1, nx - 1)])
    along_y = velocity[1, x]
    along_z = velocity[2, x]
    total = after - before
    total = total + jnp.where(sublanes(shape) == ny - 1, 0.0, pltpu.roll(along_y, ny - 1, 0))
    total = total - jnp.where(sublanes(shape) == 0, 0.0, pltpu.roll(along_y, 1, 0))
    total = total + jnp.where(lanes(shape) == nz - 1, 0.0, pltpu.roll(along_z, nz - 1, 1))
    total = total - jnp.where(lanes(shape) == 0, 0.0, pltpu.roll(along_z, 1, 1))
    return -0.5 * total


def ring(one, two, axis, closed=True, beside=None):
    count = lax.axis_size(axis)
    near = [(i, i ^ 1) for i in range(count)]
    far = [(i, (i + 1 if i % 2 else i - 1) % count) for i in range(count)]
    if not closed:
        far = [(i, j) for i, j in far if abs(i - j) == 1]
    if beside:
        near, far = (
            [(x * count + i, (1 - x) * count + j) for x in range(2) for i, j in pairs] for pairs in (near, far)
        )
        axis = (beside, axis)
    return lax.ppermute(one, axis, near), lax.ppermute(two, axis, far)


def pack_x(index, velocity_far, inv_far, *refs):
    velocity, inv, sems = refs[-3:]
    messages = refs[:-3]
    layers, ny, nz = inv.shape[1:]
    far = inv_far.shape[0] - layers
    shape = (ny, nz)
    only = len(messages) == 1
    first = index[0] == 0

    def copies(n):
        start = jnp.where(first, far, 0) if only else (far, 0)[n]
        part = pl.ds(start, layers)
        yield pltpu.make_async_copy(inv_far.at[part], inv.at[n], sems.at[4 * n])
        for d in range(3):
            yield pltpu.make_async_copy(velocity_far.at[d, part], velocity.at[n, d], sems.at[4 * n + d + 1])

    for n in range(len(messages)):
        for copy in copies(n):
            copy.start()

    def fill(n, start, own, sign):
        message, near = messages[n], velocity.at[n]
        for k in range(REACH):
            message[k * ny : (k + 1) * ny, :] = source(near, start + k, layers)
        base = REACH * ny
        message[base : base + ny, :] = sign * near[0, own]
        base += ny
        for k in range(LAYERS):
            message[base : base + ny, :] = inv[n, k]
            base += ny
        ends = jnp.zeros(shape, F32)
        for k in range(REACH):
            plane_z = near[2, start + k]
            ends = jnp.where(lanes(shape) == 2 * k, plane_z[:, 0:1], ends)
            ends = jnp.where(lanes(shape) == 2 * k + 1, plane_z[:, nz - 1 : nz], ends)
        ends = jnp.transpose(ends)[0 : 2 * REACH]
        message[base : base + 2 * REACH, :] = jnp.concatenate(
            [ends, jnp.zeros((2 * REACH, nz - ny), F32)], axis=1
        )
        base += 2 * REACH
        for k in range(REACH):
            message[base + 2 * k : base + 2 * k + 1, :] = near[1, start + k, 0:1, :]
            message[base + 2 * k + 1 : base + 2 * k + 2, :] = near[1, start + k, ny - 1 : ny, :]

    for n in range(len(messages)):
        for copy in copies(n):
            copy.wait()
    upper = (1, layers - 1, 0.5)
    lower = (0, 0, -0.5)
    if only:
        fill(0, *(jnp.where(first, one, two) for one, two in zip(upper, lower)))
    else:
        fill(0, *upper)
        fill(1, *lower)


def column_ends(message, ny, nz):
    rows = message[pl.ds((REACH + 1 + LAYERS) * ny, 2 * REACH), :]
    return jnp.transpose(jnp.concatenate([rows, jnp.zeros((nz - 2 * REACH, nz), F32)], axis=0))[0:ny]


class Scaled:
    def __init__(self, ref, factor):
        self.ref, self.factor = ref, factor

    def __getitem__(self, where):
        return self.ref[where] * self.factor


class Picked:
    def __init__(self, first, one, two, there):
        self.first, self.one, self.two, self.factor = first, one, two, jnp.where(there, 1.0, 0.0)

    def __getitem__(self, where):
        return jnp.where(self.first, self.one[where], self.two[where]) * self.factor


def sides(index, axis, messages):
    here, count = index[2 * axis], index[2 * axis + 1]
    same, (one, two) = here % 2 == 0, messages
    return Picked(same, two, one, here > 0), Picked(same, one, two, here < count - 1)


def sides_x(index, messages):
    if len(messages) == 2:
        return messages
    first = jnp.where(index[0] == 0, 1.0, 0.0)
    return Scaled(messages[0], 1.0 - first), Scaled(messages[0], first)


EARLY = (LAYERS + 1) // 2
EACH = REACH + 1 + LAYERS + 1


def put(up, down, pair, parity, rows_rhs, ghost, rows_inv, first, last, same=None):
    offset = parity * EACH
    row = (1, up.shape[2])

    def store(start, count, lower, upper):
        if same is not None:
            lower, upper = jnp.where(same, lower, upper), jnp.where(same, upper, lower)
        up[pair, pl.ds(offset + start, count), :] = upper
        down[pair, pl.ds(offset + start, count), :] = lower

    store(0, REACH, *rows_rhs)
    store(REACH, 1, -0.5 * ghost[0], 0.5 * ghost[1])
    store(REACH + 1, LAYERS, *rows_inv)
    both = []
    for part in range(2):
        ends = jnp.zeros(row, F32)
        for k in range(REACH):
            ends = jnp.where(lanes(row) == 2 * k, first[part][k : k + 1], ends)
            ends = jnp.where(lanes(row) == 2 * k + 1, last[part][k : k + 1], ends)
        both.append(ends)
    store(EACH - 1, 1, *both)


def put_own(up, down, velocity, inv, rhs, x, pair, parity, extra, same=None):
    ny, nz = inv.shape[1:]
    low, high = rhs[x, 0:REACH, :], rhs[x, ny - REACH : ny, :]
    if extra is not None:
        low = low + extra[pl.ds(REACH * ny, REACH), :]
        high = high + extra[pl.ds((REACH + 1) * ny - REACH, REACH), :]
    ghost = (velocity[1, x, 0:1, :], velocity[1, x, ny - 1 : ny, :])
    rows_inv = (inv[x, 0:LAYERS, :], inv[x, ny - LAYERS : ny, :])
    head, tail = velocity[2, x, 0:REACH, :], velocity[2, x, ny - REACH : ny, :]
    first = (head[:, 0:1], tail[:, 0:1])
    last = (head[:, nz - 1 : nz], tail[:, nz - 1 : nz])
    put(up, down, pair, parity, (low, high), ghost, rows_inv, first, last, same)


def put_rows(up, down, pair, start, lower, upper, same):
    up[pair, pl.ds(start, REACH), :] = jnp.where(same, upper, lower)
    down[pair, pl.ds(start, REACH), :] = jnp.where(same, lower, upper)


def pack_y_own(index, velocity, inv, sent, rhs, up, down, *across):
    del sent
    nx, ny, nz = rhs.shape
    same = index[2] % 2 == 0

    def plane(x, carry):
        rhs[x] = source(velocity, x, nx)
        return carry

    lax.fori_loop(0, nx, plane, 0, unroll=4)

    def planes(n, carry):
        for parity in range(2):
            put_own(up, down, velocity, inv, rhs, 2 * n + parity, n, parity, None, same)
        return carry

    def edge_rows(x):
        return velocity[0, x, 0:REACH, :], velocity[0, x, ny - REACH : ny, :]

    if across:
        first = index[0] == 0
        for k in range(LAYERS):
            x = jnp.where(first, nx - LAYERS + k, k)
            put_own(*across, velocity, inv, rhs, x, 0, k, None, same)
        rows = edge_rows(jnp.where(first, nx - 1, 0))
        sign = jnp.where(first, 0.5, -0.5)
        put_rows(*across, 0, LAYERS * EACH, sign * rows[0], sign * rows[1], same)
    lax.fori_loop(0, nx // 2, planes, 0, unroll=4)
    put_rows(up, down, nx // 2, 0, *edge_rows(0), same)
    put_rows(up, down, nx // 2, REACH, *edge_rows(nx - 1), same)


def pack_y_halo(index, velocity, inv, rhs, *refs):
    (below, above), (up, down) = sides_x(index, refs[:-2]), refs[-2:]
    same = index[2] % 2 == 0
    nx, ny, nz = inv.shape
    skip = (nx + 2 * LAYERS) // 2 - 2 * EARLY

    def halo(x, message, k_rhs, k_inv, extra):
        pair = x // 2 if x // 2 < EARLY else x // 2 - skip
        base = (REACH + 1 + k_inv) * ny
        rows_inv = (message[pl.ds(base, LAYERS), :], message[pl.ds(base + ny - LAYERS, LAYERS), :])
        zero_row = jnp.zeros((1, nz), F32)
        zero = jnp.zeros((REACH, nz), F32)
        if k_rhs is None:
            column = jnp.zeros((REACH, 1), F32)
            put(up, down, pair, x % 2, (zero, zero), (zero_row, zero_row), rows_inv, (column, column), (column, column), same)
            return
        low, high = message[pl.ds(k_rhs * ny, REACH), :], message[pl.ds((k_rhs + 1) * ny - REACH, REACH), :]
        if extra is not None:
            sign, source = extra
            low = low + sign * velocity[0, source, 0:REACH, :]
            high = high + sign * velocity[0, source, ny - REACH : ny, :]
        lines = (REACH + 1 + LAYERS) * ny + 2 * REACH + 2 * k_rhs
        ghost = (message[pl.ds(lines, 1), :], message[pl.ds(lines + 1, 1), :])
        ends = column_ends(message, ny, nz)
        head, tail = ends[0:REACH], ends[ny - REACH : ny]
        first = (head[:, 2 * k_rhs : 2 * k_rhs + 1], tail[:, 2 * k_rhs : 2 * k_rhs + 1])
        last = (head[:, 2 * k_rhs + 1 : 2 * k_rhs + 2], tail[:, 2 * k_rhs + 1 : 2 * k_rhs + 2])
        put(up, down, pair, x % 2, (low, high), ghost, rows_inv, first, last, same)

    for k in range(LAYERS):
        halo(k, below, k - 1 if k else None, k, (-0.5, 0) if k == LAYERS - 1 else None)
        halo(
            nx + LAYERS + k,
            above,
            k if k < REACH else None,
            k,
            (0.5, nx - 1) if k == 0 else None,
        )
    put_own(up, down, velocity, inv, rhs, 0, EARLY - 1, 1, below, same)
    put_own(up, down, velocity, inv, rhs, nx - 1, EARLY, 0, above, same)


def pack_z(across, index, velocity, inv, rhs, *refs):
    (below, above), received = sides_x(index, refs[:-16]), refs[-16:-12]
    received = [*sides(index, 1, received[:2]), *sides(index, 1, received[2:])]
    same = index[4] % 2 == 0
    rhs_far, inv_far, up, down, strip_rhs_far, strip_inv_far = refs[-12:-6]
    rhs_wide, inv_wide, ends, strip_rhs, strip_inv, sems = refs[-6:]
    nx, ny, nz = inv.shape
    wide = nx + 2 * LAYERS
    rows = ny + 2 * WIDE
    mine = pl.ds(WIDE, ny)
    edge = (WIDE, nz)
    groups = strip_rhs.shape[0]

    columns = [column_ends(message, ny, nz) for message in (below, above)]
    for k in range(LAYERS):
        for message, line, x, layer in (
            (below, columns[0], k, k - 1),
            (above, columns[1], nx + LAYERS + k, k if k < REACH else -1),
        ):
            base = (REACH + 1 + k) * ny
            inv_wide[x, mine, :] = message[pl.ds(base, ny), :]
            if layer < 0:
                rhs_wide[x, mine, :] = jnp.zeros((ny, nz), F32)
                ends[x, mine, :] = jnp.zeros((ny, nz), F32)
                continue
            part = message[pl.ds(layer * ny, ny), :]
            if x == LAYERS - 1:
                part = part - 0.5 * velocity[0, 0]
            if x == nx + LAYERS:
                part = part + 0.5 * velocity[0, nx - 1]
            rhs_wide[x, mine, :] = part
            ends[x, mine, :] = jnp.where(
                lanes((ny, nz)) == 0, line[:, 2 * layer : 2 * layer + 1], line[:, 2 * layer + 1 : 2 * layer + 2]
            )

    def plane(x, carry):
        inv_wide[x + LAYERS, mine, :] = inv[x]
        rhs_wide[x + LAYERS, mine, :] = rhs[x]
        ends[x + LAYERS, mine, :] = velocity[2, x]
        return carry

    lax.fori_loop(0, nx, plane, 0, unroll=4)
    rhs_wide[LAYERS, mine, :] += below[pl.ds(REACH * ny, ny), :]
    rhs_wide[LAYERS + nx - 1, mine, :] += above[pl.ds(REACH * ny, ny), :]
    for ref in (rhs_wide, inv_wide, ends):
        for x in range(wide, ref.shape[0]):
            ref[x] = jnp.zeros((rows, nz), F32)

    first = index[0] == 0
    own, far = received[:2], received[2:]

    def from_pair(refs, pair, parity):
        values = [ref[pair] for ref in refs]
        if isinstance(parity, int):
            return [(pltpu.roll(value, ROWS - EACH, 0) if parity else value)[0:SLOT] for value in values]
        return [jnp.where(parity == 0, value, pltpu.roll(value, ROWS - EACH, 0))[0:SLOT] for value in values]

    def extra(refs, pair, start, factor):
        values = [ref[pair] for ref in refs]
        size = values[0].shape[0]
        values = [pltpu.roll(value, (size - start) % size, 0)[0:SLOT] for value in values]
        return [jnp.where(sublanes((SLOT, nz)) < REACH, factor * value, 0.0) for value in values]

    def rows_of(x):
        if not isinstance(x, int):
            return from_pair(own, (x - LAYERS) // 2, (x - LAYERS) % 2)
        inside = LAYERS <= x < LAYERS + nx
        upper = x >= LAYERS + nx - 1
        if not across:
            return from_pair(far, x // 2 - (wide // 2 - 2 * EARLY if upper else 0), x % 2)
        there = jnp.where(first, 1.0, 0.0) if upper else jnp.where(first, 0.0, 1.0)
        if inside:
            values = from_pair(own, (x - LAYERS) // 2, (x - LAYERS) % 2)
            rows_at = (0, pl.ds(LAYERS * EACH // SLOT * SLOT, SLOT), slice(None))
            more = extra(far, rows_at, LAYERS * EACH % SLOT, there)
        else:
            k = x - LAYERS - nx if upper else x
            values = [there * ref[0, pl.ds(k * EACH, SLOT), :] for ref in far]
            if x == LAYERS - 1:
                more = extra(own, nx // 2, 0, -0.5)
            elif x == LAYERS + nx:
                more = extra(own, nx // 2, REACH, 0.5)
            else:
                return values
        return [one + two for one, two in zip(values, more)]

    def finish(x, ghost_low, ghost_high):
        low, high = rows_of(x)
        part = pltpu.roll(low, WIDE - REACH, 0)[0:WIDE]
        part = jnp.where(sublanes(edge) >= WIDE - REACH, part, 0.0)
        part = part - jnp.where(sublanes(edge) == WIDE - 1, 0.5 * ghost_low, 0.0)
        rhs_wide[x, 0:WIDE, :] = part
        part = pltpu.roll(low, SLOT - (REACH + 1) + WIDE - LAYERS, 0)[0:WIDE]
        inv_wide[x, 0:WIDE, :] = jnp.where(sublanes(edge) >= WIDE - LAYERS, part, 0.0)
        part = jnp.where(sublanes(edge) < REACH, high[0:WIDE], 0.0)
        part = part + jnp.where(sublanes(edge) == 0, 0.5 * ghost_high, 0.0)
        rhs_wide[x, WIDE + ny : rows, :] = part
        part = pltpu.roll(high, SLOT - (REACH + 1), 0)[0:WIDE]
        inv_wide[x, WIDE + ny : rows, :] = jnp.where(sublanes(edge) < LAYERS, part, 0.0)
        head = rhs_wide[x, WIDE : 2 * WIDE, :]
        rhs_wide[x, WIDE : 2 * WIDE, :] = head + jnp.where(sublanes(edge) == 0, low[REACH : REACH + 1], 0.0)
        tail = rhs_wide[x, ny : WIDE + ny, :]
        rhs_wide[x, ny : WIDE + ny, :] = tail + jnp.where(
            sublanes(edge) == WIDE - 1, high[REACH : REACH + 1], 0.0
        )
        for message, start, place in ((low, WIDE - REACH, 0), (high, 0, WIDE + ny)):
            line = message[EACH - 1 : EACH]
            one = jnp.zeros(edge, F32)
            two = jnp.zeros(edge, F32)
            for k in range(REACH):
                here = sublanes(edge) == start + k
                one = jnp.where(here, line[:, 2 * k : 2 * k + 1], one)
                two = jnp.where(here, line[:, 2 * k + 1 : 2 * k + 2], two)
            ends[x, place : place + WIDE, :] = jnp.where(lanes(edge) == 0, one, two)

    for k in range(LAYERS):
        for message, x, layer in ((below, k, k - 1), (above, nx + LAYERS + k, k if k < REACH else -1)):
            lines = (REACH + 1 + LAYERS) * ny + 2 * REACH + 2 * layer
            if layer < 0:
                zero = jnp.zeros((1, nz), F32)
                finish(x, zero, zero)
            else:
                finish(x, message[pl.ds(lines, 1), :], message[pl.ds(lines + 1, 1), :])

    def middle(x, carry):
        finish(x + LAYERS, velocity[1, x, 0:1, :], velocity[1, x, ny - 1 : ny, :])
        return carry

    lax.fori_loop(1, nx - 1, middle, 0, unroll=30)
    for x in (0, nx - 1):
        finish(x + LAYERS, velocity[1, x, 0:1, :], velocity[1, x, ny - 1 : ny, :])
    copies = [
        pltpu.make_async_copy(ref.at[pl.ds(0, wide)], far, sems.at[n])
        for n, (ref, far) in enumerate(((rhs_wide, rhs_far), (inv_wide, inv_far)))
    ]
    for copy in copies:
        copy.start()

    whole = (rows, nz)
    lane = lanes(whole)
    place = lane % SPAN

    def back(value, step):
        return pltpu.roll(value, nz - step, 1)

    def gather(ref, g):
        value = None
        for n in range(nz // SPAN):
            moved = pltpu.roll(ref[g + n * groups], n * SPAN + STRIP, 1)
            value = moved if value is None else jnp.where(lane >= n * SPAN, moved, value)
        return value

    def pack(g):
        r, i, e = gather(rhs_wide, g), gather(inv_wide, g), gather(ends, g)
        apart = SPAN - 2 * STRIP
        for ref, value in ((strip_rhs, r), (strip_inv, i)):
            out = jnp.where(place < STRIP, value, 0.0)
            ref[g] = jnp.where(place >= SPAN - STRIP, pltpu.roll(value, apart, 1), out)
        ghost = jnp.where(place == STRIP, 0.5 * pltpu.roll(e, 1, 1), 0.0)
        ghost = jnp.where(place == SPAN - STRIP - 1, -0.5 * pltpu.roll(e, apart - 1, 1), ghost)
        strip_rhs[g] += ghost
        out = jnp.where(place < REACH, back(r, STRIP - REACH), 0.0)
        out = jnp.where(place == REACH, 0.5 * back(e, STRIP - 1 - REACH), out)
        here = (place > REACH) & (place <= REACH + LAYERS)
        higher = jnp.where(here, pltpu.roll(i, (nz + REACH + 1 + LAYERS - STRIP) % nz, 1), out)
        out = jnp.where(place < REACH, back(r, STRIP), 0.0)
        out = jnp.where(place == REACH, -0.5 * back(e, STRIP - REACH), out)
        return higher, jnp.where(here, back(i, STRIP - REACH - 1), out)

    halves = up.shape[0]

    def both(n, carry):
        one, two = pack(n)
        up[n] = jnp.where(same, one, two)
        down[n] = jnp.where(same, two, one)
        return carry

    lax.fori_loop(0, halves, both, 0, unroll=3)

    def more(n, carry):
        one, two = pack(n + halves)
        up[n] += pltpu.roll(jnp.where(same, one, two), SPAN // 2, 1)
        down[n] += pltpu.roll(jnp.where(same, two, one), SPAN // 2, 1)
        return carry

    lax.fori_loop(0, groups - halves, more, 0, unroll=5)
    for ref, far in ((strip_rhs, strip_rhs_far), (strip_inv, strip_inv_far)):
        copies.append(pltpu.make_async_copy(ref, far, sems.at[len(copies)]))
        copies[-1].start()
    for copy in copies:
        copy.wait()


def shifted(ref, x, t, step):
    rows = ref.shape[1]
    start = t * WIDE + step
    if start < 0:
        return pltpu.roll(ref[x, 0:WIDE, :], 1, 0)
    if start + WIDE > rows:
        return pltpu.roll(ref[x, rows - WIDE : rows, :], WIDE - 1, 0)
    return ref[x, start : start + WIDE, :]


class Stencil:
    def __init__(self, inv, root, ax, ay, az, vs, planes, edges=None, unroll=10):
        self.inv, self.root, self.ax, self.ay, self.az, self.vs = inv, root, ax, ay, az, vs
        self.planes, self.edges, self.unroll = planes, edges or (lambda ref: None), unroll
        self.count, self.rows, self.nz = inv.shape
        self.tiles = self.rows // WIDE

    def here(self, t):
        return slice(t * WIDE, (t + 1) * WIDE)

    def right(self, value):
        return pltpu.roll(value, self.nz - 1, 1)

    def left(self, value):
        return pltpu.roll(value, 1, 1)

    def prepare(self, rhs, parts=None):
        inv, root = self.inv, self.root
        self.edges(inv)

        def scales(x, carry):
            writes = []
            for t in range(self.tiles):
                here = self.here(t)
                c = inv[x, here, :]
                total = (inv[x + 1, here, :] + inv[x - 1, here, :]) + (self.right(c) + self.left(c))
                total = total + (shifted(inv, x, t, 1) + shifted(inv, x, t, -1))
                value = jnp.where(c > 0.0, lax.rsqrt(SHIFT + 0.5 * (6.0 * c + total)), 0.0)
                writes.append((here, value, rhs[x, here, :] * value))
            for here, one, two in writes:
                root[x, here, :] = one
                self.vs[0][x, here, :] = two
            return carry

        for start, stop in parts or [(1, self.count - 1)]:
            lax.fori_loop(start, stop, scales, 0, unroll=self.unroll)
        zero = jnp.zeros((self.rows, self.nz), F32)
        for ref in (root, self.vs[0]):
            ref[0] = zero
            ref[self.count - 1] = zero
            self.edges(ref)

        def couplings(x, carry):
            writes = []
            for t in range(self.tiles):
                here = self.here(t)
                c, d = inv[x, here, :], root[x, here, :]
                half = 0.5 * d
                writes.append(
                    (
                        here,
                        (c + inv[x + 1, here, :]) * (half * root[x + 1, here, :]),
                        (c + shifted(inv, x, t, 1)) * (half * shifted(root, x, t, 1)),
                        (c + self.right(c)) * (half * self.right(d)),
                    )
                )
            for here, x_face, y_face, z_face in writes:
                self.ax[x, here, :] = x_face
                self.ay[x, here, :] = y_face
                self.az[x, here, :] = z_face
            return carry

        lax.fori_loop(1, self.count - 1, couplings, 0, unroll=self.unroll)
        self.ax[0] = zero
        self.edges(self.ax)

    def couple(self, k, x, t):
        here = self.here(t)
        v, ax, ay = self.vs[k], self.ax, self.ay
        c, f = v[x, here, :], self.az[x, here, :]
        total = ax[x, here, :] * v[x + 1, here, :] + ax[x - 1, here, :] * v[x - 1, here, :]
        total = total + (f * self.right(c) + self.left(f * c))
        total = total + ay[x, here, :] * shifted(v, x, t, 1)
        return c, total + shifted(ay, x, t, -1) * shifted(v, x, t, -1)

    def extend(self, k):
        scale = 1.0 - NEWTON[k]

        def step(x, carry):
            writes = []
            for t in range(self.tiles):
                c, total = self.couple(k, x, t)
                writes.append((t, scale * c - total if scale else -total))
            for t, value in writes:
                self.vs[k + 1][x, self.here(t), :] = value
            return carry

        start, stop = self.planes(k)
        lax.fori_loop(start, stop, step, 0, unroll=self.unroll)
        self.edges(self.vs[k + 1])

    def products(self, start, stop, mask):
        def measure(x, sums):
            sums = list(sums)
            for t in range(1, self.tiles - 1):
                keep = mask(x)
                v = [self.vs[k][x, self.here(t), :] for k in range(ITERS)]
                own, total = self.couple(ITERS - 1, x, t)
                kept = [jnp.where(keep, one, 0.0) for one in v]
                for n, (a, b) in enumerate(PAIRS):
                    sums[n] = sums[n] + v[a] * kept[b]
                sums[-1] = sums[-1] + kept[-1] * (own - total)
            return tuple(sums)

        zero = jnp.zeros((WIDE, self.nz), F32)
        return lax.fori_loop(start, stop, measure, (zero,) * (len(PAIRS) + 1), unroll=11 if self.unroll > 10 else 4)


def basis_main(rhs_far, inv_far, *refs):
    outs, sums = refs[: ITERS + 1], refs[ITERS + 1]
    rhs, inv, root, ax, ay, az = refs[ITERS + 2 : ITERS + 8]
    vs, sems = refs[ITERS + 8 : -1], refs[-1]
    wide, rows, nz = ax.shape
    nx = wide - 2 * LAYERS
    batch = 4
    bounds = [n * wide // batch for n in range(batch + 1)]
    loads = []
    for n in range(batch):
        part = pl.ds(bounds[n], bounds[n + 1] - bounds[n])
        for far, ref in ((inv_far, inv), (rhs_far, rhs)):
            loads.append(pltpu.make_async_copy(far.at[part], ref.at[part], sems.at[ITERS + 1 + len(loads)]))
            loads[-1].start()

    def ready():
        for n in range(batch):
            for load in loads[2 * n : 2 * n + 2]:
                load.wait()
            yield max(bounds[n] - 1, 1), bounds[n + 1] - 1

    stencil = Stencil(inv, root, ax, ay, az, vs, lambda k: (2 + k, wide - 2 - k))
    copies = []

    def send(n, ref):
        copy = pltpu.make_async_copy(ref.at[pl.ds(LAYERS - 1, nx + 2)], outs[n], sems.at[n])
        copy.start()
        copies.append(copy)

    stencil.prepare(rhs, ready())
    send(ITERS, root)
    send(0, vs[0])
    for k in range(ITERS - 1):
        stencil.extend(k)
        send(k + 1, vs[k + 1])
    lane = lanes((WIDE, nz))
    inner = (lane > REACH) & (lane < nz - 1 - REACH)
    for n, one in enumerate(stencil.products(LAYERS, LAYERS + nx, lambda x: inner)):
        sums[n] = one
    for copy in copies:
        copy.wait()


def basis_strips(nx, index, rhs_far, inv_far, one, two, sums, *refs):
    before, after = sides(index, 2, (one, two))
    outs, dots = refs[:ITERS], refs[ITERS]
    rhs, inv, root, ax, ay, az = refs[ITERS + 1 : ITERS + 7]
    vs, outs_near = refs[ITERS + 7 : 2 * ITERS + 7], refs[2 * ITERS + 7 : 3 * ITERS + 7]
    strip_rhs, strip_inv, sems = refs[-3:]
    groups, rows, nz = strip_inv.shape
    loads = [
        pltpu.make_async_copy(far, ref, sems.at[ITERS + n])
        for n, (far, ref) in enumerate(((rhs_far, strip_rhs), (inv_far, strip_inv)))
    ]
    for load in loads:
        load.start()
    for load in loads:
        load.wait()
    halves = one.shape[0]
    whole = (rows, nz)
    place = lanes(whole) % SPAN

    def edges(ref):
        ref[0] = pltpu.roll(ref[groups], SPAN, 1)
        ref[groups + 1] = pltpu.roll(ref[1], nz - SPAN, 1)

    def receive(g, low, high):
        start = SPAN - STRIP - LAYERS
        moved = pltpu.roll(low, start + 1, 1)
        r = strip_rhs[g] + jnp.where((place > start) & (place <= SPAN - STRIP), moved, 0.0)
        moved = pltpu.roll(low, start - REACH - 1, 1)
        i = strip_inv[g] + jnp.where((place >= start) & (place < SPAN - STRIP), moved, 0.0)
        moved = pltpu.roll(high, STRIP, 1)
        r = r + jnp.where((place >= STRIP) & (place < STRIP + REACH), moved, 0.0)
        moved = pltpu.roll(high, STRIP - REACH - 1, 1)
        r = r + jnp.where(place == STRIP - 1, moved, 0.0)
        i = i + jnp.where((place >= STRIP) & (place < STRIP + LAYERS), moved, 0.0)
        rhs[g + 1] = r
        inv[g + 1] = i

    def first(n, carry):
        receive(n, before[n], after[n])
        return carry

    def second(n, carry):
        half = nz - SPAN // 2
        receive(n + halves, pltpu.roll(before[n], half, 1), pltpu.roll(after[n], half, 1))
        return carry

    lax.fori_loop(0, halves, first, 0, unroll=6)
    lax.fori_loop(0, groups - halves, second, 0, unroll=5)
    stencil = Stencil(inv, root, ax, ay, az, vs, lambda k: (1, groups + 1), edges, groups)
    stencil.prepare(rhs)
    copies = []

    def result(k):
        ref = outs_near[k]

        def plane(g, carry):
            ref[g] = vs[k][g] * root[g]
            return carry

        lax.fori_loop(1, groups + 1, plane, 0, unroll=groups)
        copies.append(pltpu.make_async_copy(ref.at[pl.ds(1, groups)], outs[k], sems.at[k]))
        copies[-1].start()

    result(0)
    for k in range(ITERS - 1):
        stencil.extend(k)
        result(k + 1)
    lane = lanes((WIDE, nz))
    part = lane // SPAN
    spot = lane % SPAN
    ends = ((spot >= STRIP - LAYERS) & (spot < STRIP)) | (
        (spot >= SPAN - STRIP) & (spot < SPAN - STRIP + LAYERS)
    )

    def mask(x):
        plane = x - 1 + part * groups
        return ends & (plane >= LAYERS) & (plane < LAYERS + nx)

    totals = []
    for n, one in enumerate(stencil.products(1, groups + 1, mask)):
        line = jnp.sum(one + sums[n], axis=0, keepdims=True)
        totals.append(line + pltpu.roll(line, nz // 2, 1))
    row = sublanes((WIDE, nz))
    message = jnp.zeros((WIDE, nz), F32)
    for n, line in enumerate(totals):
        half = lane < nz // 2 if n < WIDE else lane >= nz // 2
        message = jnp.where((row == n % WIDE) & half, line, message)

    def send(n, carry):
        dots[n] = message
        return carry

    lax.fori_loop(0, dots.shape[0], send, 0, unroll=8)

    for copy in copies:
        copy.wait()


def coefficients(dots):
    half = lanes(dots.shape) < dots.shape[1] // 2
    one = jnp.sum(jnp.where(half, dots, 0.0), axis=1, keepdims=True)
    two = jnp.sum(jnp.where(half, 0.0, dots), axis=1, keepdims=True)

    def entry(n):
        return one[n : n + 1] if n < WIDE else two[n - WIDE : n - WIDE + 1]

    gram = {}
    for n, (a, b) in enumerate(PAIRS):
        gram[a, b] = gram[b, a] = entry(n)
    last = ITERS - 1
    image = {}
    for b in range(last):
        for a in range(ITERS):
            image[a, b] = gram[a, b + 1]
            if NEWTON[b]:
                image[a, b] = image[a, b] + NEWTON[b] * gram[a, b]
    for a in range(last):
        image[a, last] = image[last, a]
    image[last, last] = entry(len(PAIRS))

    def product(table, one, two):
        total = None
        for a, left in enumerate(one):
            for b, right in enumerate(two):
                term = left * right * table[a, b]
                total = term if total is None else total + term
        return total

    unit = jnp.ones((1, 1), F32)
    pressure = []
    precond = [unit]
    direction = [unit]
    rz = gram[0, 0]
    for iteration in range(ITERS):
        alpha = rz / product(image, direction, direction)
        pressure = [
            (pressure[n] if n < len(pressure) else 0.0) + alpha * one for n, one in enumerate(direction)
        ]
        if iteration == last:
            break
        moved = []
        for n in range(len(direction) + 1):
            value = None
            if n < len(direction) and NEWTON[n]:
                value = NEWTON[n] * direction[n]
            if n > 0:
                value = direction[n - 1] if value is None else value + direction[n - 1]
            moved.append(value)
        fresh_precond = []
        for n, one in enumerate(moved):
            old = precond[n] if n < len(precond) else None
            if one is None:
                fresh_precond.append(old)
            else:
                fresh_precond.append(-alpha * one if old is None else old - alpha * one)
        precond = fresh_precond
        fresh = product(gram, precond, precond)
        beta = fresh / rz
        direction = [
            one + beta * direction[n] if n < len(direction) else one for n, one in enumerate(precond)
        ]
        rz = fresh
    return pressure


def finish(dots, columns, *refs):
    inputs = 2 * ITERS + 3
    pressure_far, corrected_far, keep, keep_more, send, p, gaps, mixed, cut, pressure, corrected = refs[inputs : inputs + 11]
    held, sems = refs[inputs + 11 : -1], refs[-1]
    strips, spans, roots = held[:ITERS], held[ITERS : 2 * ITERS], held[2 * ITERS]
    velocity, inv = held[2 * ITERS + 1 :]
    nx, ny, nz = inv.shape
    batch = 4
    each = nx // batch
    used = 0

    def start(far, ref):
        nonlocal used
        copy = pltpu.make_async_copy(far, ref, sems.at[used])
        used += 1
        copy.start()
        return copy

    strip_loads = [start(far, ref) for far, ref in zip(refs[:ITERS], strips)]
    span_loads, other_loads, bounds = [], [], []
    for n in range(batch):
        low, high = (n * each + 2 if n else 0), (n + 1) * each + 2
        bounds.append((low, high))
        part = pl.ds(low, high - low)
        pairs = zip(refs[ITERS : 2 * ITERS + 1], held[ITERS : 2 * ITERS + 1])
        span_loads.append([start(far.at[part], ref.at[part]) for far, ref in pairs])
        part = pl.ds(n * each, each)
        other_loads.append(
            [start(refs[2 * ITERS + 1].at[d, part], velocity.at[d, part]) for d in range(3)]
            + [start(refs[2 * ITERS + 2].at[part], inv.at[part])]
        )
    shape = (ny, nz)
    groups = mixed.shape[0]
    total = dots[0]
    for n in range(1, dots.shape[0]):
        total = total + dots[n]
    weights = coefficients(total)

    def strip(g, carry):
        value = weights[0] * strips[0][g]
        for k in range(1, ITERS):
            value = value + weights[k] * strips[k][g]
        mixed[g] = value
        return carry

    for load in strip_loads:
        load.wait()
    lax.fori_loop(0, groups, strip, 0, unroll=4)
    mine = slice(WIDE, WIDE + ny)
    lane = lanes(spans[0].shape[1:])

    def combine(x, carry):
        value = weights[0] * spans[0][x]
        for k in range(1, ITERS):
            value = value + weights[k] * spans[k][x]
        value = value * roots[x]
        plane = x + LAYERS - 1
        ends = mixed[plane % groups]
        start = plane // groups * SPAN
        last = pltpu.roll(ends, lax.rem(2 * nz - STRIP - start, nz), 1)
        first = pltpu.roll(ends, lax.rem(nz + STRIP - SPAN - start + nz, nz), 1)
        value = jnp.where(lane < LAYERS, first, jnp.where(lane >= nz - LAYERS, last, value))
        p[x] = value
        after = pltpu.roll(jnp.where(lane == 0, last, value), nz - 1, 1)
        before = pltpu.roll(jnp.where(lane == nz - 1, first, value), 1, 1)
        gaps[x] = (after - before)[mine]
        return carry

    half = columns.shape[0] // 2

    def pair(n, carry):
        for which in range(2):
            x = 2 * n + which
            centre = p[x + 1, mine, :]
            pressure[x] = centre
            half_inv = 0.5 * inv[x]
            slopes = (
                p[x + 2, mine, :] - p[x, mine, :],
                p[x + 1, WIDE + 1 : WIDE + 1 + ny, :] - p[x + 1, WIDE - 1 : WIDE - 1 + ny, :],
                gaps[x + 1],
            )
            fields = [velocity[d, x] - half_inv * slopes[d] for d in range(3)] + [centre]
            for d in range(3):
                corrected[d, x] = fields[d]
            for f, field in enumerate(fields):
                high = field.astype(BF16)
                low = (field - high.astype(F32)).astype(BF16)
                cut[f, which * ny : (which + 1) * ny, 0:nz] = high
                cut[f, which * ny : (which + 1) * ny, nz : 2 * nz] = low
        for f in range(4):
            out = lax.dot_general(
                columns[...], cut[f], (((1,), (1,)), ((), ())), preferred_element_type=F32
            )
            out = out[:half] + out[half:]
            block = f * (nx // 2) + n
            quarter = half // 4
            keep[block] = out[0:quarter]
            keep_more[block] = out[quarter : 2 * quarter]
            send[0, block] = out[2 * quarter : 3 * quarter]
            send[1, block] = out[3 * quarter :]
        return carry

    stores = []
    for n in range(batch):
        for load in span_loads[n]:
            load.wait()
        lax.fori_loop(*bounds[n], combine, 0, unroll=4)
        for load in other_loads[n]:
            load.wait()
        lax.fori_loop(n * each // 2, (n + 1) * each // 2, pair, 0, unroll=4)
        part = pl.ds(n * each, each)
        stores.append(start(pressure.at[part], pressure_far.at[part]))
        for d in range(3):
            stores.append(start(corrected.at[d, part], corrected_far.at[d, part]))
    for store in stores:
        store.wait()


def tables(count_x, factor_y, factor_x, y_high, y_low, x_high, x_low, spread_high, spread_low):
    ny, rank = factor_y.shape
    nx = factor_x.shape[0]
    planes = y_high.shape[0] // ny
    nz = x_high.shape[1] // rank * planes
    count = y_high.shape[1] // nz
    ranks = rank // count
    wide = jnp.concatenate([factor_y[...], jnp.zeros((ny, nz - rank), F32)], axis=1)
    lane = lanes((ny, nz))
    for h in range(count):
        value = pltpu.roll(wide, (nz - h * ranks) % nz, 1)
        value = jnp.where(lane < ranks, value, 0.0)
        step = ranks
        while step < nz:
            value = value + pltpu.roll(value, step, 1)
            step *= 2
        for n in range(planes):
            high, low = split(jnp.where(lane // ranks == n, value, 0.0))
            y_high[n * ny : (n + 1) * ny, h * nz : (h + 1) * nz] = high
            y_low[n * ny : (n + 1) * ny, h * nz : (h + 1) * nz] = low
    width = x_high.shape[1]
    shape = (rank, width)
    own = rank // count_x
    lane = lanes(shape)
    copy = lane // (ranks * own) * own + lane % own == sublanes(shape)
    copy = jnp.where(copy, 1.0, 0.0).astype(BF16)
    for ref, value in zip((spread_high, spread_low), split(factor_x[...])):
        ref[...] = jnp.dot(value, copy, preferred_element_type=F32)
    shape = (ranks, width)
    here = lanes(shape) // own % ranks == sublanes(shape)

    def row(i, carry):
        at = pl.ds(pl.multiple_of(i * ranks, ranks), ranks)
        x_high[at, :] = jnp.where(here, spread_high[pl.ds(i, 1), :], 0.0).astype(BF16)
        x_low[at, :] = jnp.where(here, spread_low[pl.ds(i, 1), :], 0.0).astype(BF16)
        return carry

    lax.fori_loop(0, nx, row, 0, unroll=4)


def split(value):
    high = value.astype(BF16)
    return high, (value - high.astype(F32)).astype(BF16)


def split_table(value):
    high = lax.reduce_precision(value, exponent_bits=8, mantissa_bits=7)
    return high.astype(BF16), (value - high).astype(BF16)


def three(a, b, dims=(((1,), (0,)), ((), ()))):
    dot = functools.partial(lax.dot_general, dimension_numbers=dims, preferred_element_type=F32)
    (ah, al), (bh, bl) = a, b
    return dot(ah, bh) + (dot(al, bh) + dot(ah, bl))


def rank_y(x, table):
    blocks, ranks, nz = x.shape
    group = table[0].shape[0] // nz
    parts = [
        jnp.concatenate([x[n * group + q] for q in range(group)], axis=1) for n in range(blocks // group)
    ]
    out = three(split(jnp.concatenate(parts, axis=0)), table)
    return [out[:, n * nz : (n + 1) * nz] for n in range(out.shape[1] // nz)]


def tail_one(kept, more, came, high, low, p_send, p_keep, q_send, q_keep, q_more):
    half = kept.shape[0] // 2
    p_send[...] = more[0:half] + came[1, 0:half]
    p_keep[...] = kept[0:half] + came[0, 0:half]
    x = jnp.concatenate([kept[half:] + came[0, half:], more[half:] + came[1, half:]], axis=0)
    q_keep[...], q_more[...], q_send[0], q_send[1] = rank_y(x, (high[...], low[...]))


def tail_two(p_kept, p_came, q_kept, q_more, q_came, high, low, p_send, p_keep, p_more, q_send, q_keep):
    q_send[...] = q_more[...] + q_came[1]
    q_keep[...] = q_kept[...] + q_came[0]
    parts = rank_y(p_kept[...] + p_came[...], (high[...], low[...]))
    p_keep[...], p_more[...], p_send[0], p_send[1] = parts


def tail_three(p_kept, p_more, p_came, q_kept, q_came, p_send, p_keep, q_send, q_keep):
    half = q_keep.shape[0]
    p_send[...] = p_more[...] + p_came[1]
    p_keep[...] = p_kept[...] + p_came[0]
    q_send[...] = q_kept[half:] + q_came[half:]
    q_keep[...] = q_kept[0:half] + q_came[0:half]


def rank_x(ranks, p_kept, p_came, q_kept, q_came, wide_high, wide_low, *outs):
    u = jnp.concatenate([p_kept[...] + p_came[...], q_kept[...] + q_came[...]], axis=0)
    rows, nz = u.shape
    group = wide_high.shape[0] // nz
    parts = []
    for f in range(rows // ranks // group):
        parts.append(
            jnp.concatenate(
                [u[(f * group + q) * ranks : (f * group + q + 1) * ranks] for q in range(group)], axis=1
            )
        )
    x = jnp.concatenate(parts, axis=0)
    out = three(split(x), (wide_high[...], wide_low[...]))
    width = out.shape[1] // len(outs)
    for n, ref in enumerate(outs):
        ref[...] = out[:, n * width : (n + 1) * width]


def last_core(kept, came, core):
    fields, ranks_y, ranks_z, ranks_x = core.shape
    z = kept[...] + came[...]
    for f in range(fields):
        for b in range(ranks_y):
            core[f, b] = z[f * ranks_z : (f + 1) * ranks_z, b * ranks_x : (b + 1) * ranks_x]


def relative(factor, axis):
    count = lax.axis_size(axis)
    order = [0]
    step = 1
    while step < count:
        order = order + [n + step for n in order]
        step *= 2
    bits = count.bit_length() - 1
    order = [sum(((n >> b) & 1) << (bits - 1 - b) for b in range(bits)) for n in range(count)]
    blocks = factor.reshape(factor.shape[0], count, factor.shape[1] // count)
    here = lax.axis_index(axis)
    picked = [
        lax.dynamic_index_in_dim(blocks, jnp.bitwise_xor(here, n), axis=1, keepdims=False) for n in order
    ]
    return jnp.stack(picked, axis=1)


def swap(value, axis, mask):
    count = lax.axis_size(axis)
    return lax.ppermute(value, axis, [(i, i ^ mask) for i in range(count)])


def per_device(velocity, inv_density, factor_x, factor_y, factor_z):
    nx, ny, nz = inv_density.shape
    wide, rows = nx + 2 * LAYERS, ny + 2 * WIDE
    count_x, count_y, count_z = (lax.axis_size(axis) for axis in AXES)
    devices = count_x * count_y * count_z
    cells = (nx, ny, nz)
    rank = factor_x.shape[1]
    index_x = lax.axis_index("gx").reshape(1)
    index = jnp.stack([jnp.int32(f(axis)) for axis in AXES for f in (lax.axis_index, lax.axis_size)])

    shape = ((REACH + 1 + LAYERS) * ny + 4 * REACH, nz)
    number = 1 if count_x == 2 else 2
    sent = call(
        pack_x,
        [shape] * number,
        [index_x, velocity, inv_density],
        scratch=[(number, 3, LAYERS, ny, nz), (number, LAYERS, ny, nz)],
        smem=1,
        far_in=(1, 2),
        sems=4 * number,
    )
    near = [swap(sent[0], "gx", 1)] if count_x == 2 else list(exchange(*sent, "gx"))
    across = count_x == 2
    shape = (nx // 2 + 1, ROWS, nz)
    corner = (1, -(-(LAYERS * EACH + REACH) // SLOT) * SLOT, nz)
    rhs, up, down, *corners = call(
        pack_y_own,
        [cells, shape, shape] + ([corner, corner] if across else []),
        [index, velocity, inv_density, sent[0]],
        smem=1,
        cost=(nx * ny * nz * 10, 6 * cost_of(cells)),
        far_in=(3,),
    )
    received = list(ring(up, down, "gy", closed=False))
    if across:
        received += ring(*corners, "gy", beside="gx", closed=False)
    else:
        shape = (2 * EARLY, ROWS, nz)
        up, down = call(pack_y_halo, [shape, shape], [index, velocity, inv_density, rhs, *near], smem=1)
        received += ring(up, down, "gy")
    parts = nz // SPAN
    groups = -(-wide // parts)
    message = (-(-groups // 2), rows, nz)
    whole = (groups * parts, rows, nz)
    strip = (groups, rows, nz)
    rhs_wide, inv_wide, up, down, strip_rhs, strip_inv = call(
        functools.partial(pack_z, across),
        [(wide, rows, nz)] * 2 + [message, message, strip, strip],
        [index, velocity, inv_density, rhs, *near, *received],
        scratch=[whole] * 3 + [strip] * 2,
        smem=1,
        limit=18,
        far_out=(0, 1, 4, 5),
        sems=4,
    )
    came = ring(up, down, "gz")
    span = (nx + 2, rows, nz)
    whole = (wide, rows, nz)
    *spans, sums = call(
        basis_main,
        [span] * (ITERS + 1) + [(len(PAIRS) + 1, WIDE, nz)],
        [rhs_wide, inv_wide],
        scratch=[whole] * (6 + ITERS),
        limit=22,
        cost=(wide * rows * nz * 100, 7 * cost_of(whole)),
        far_in=(0, 1),
        far_out=range(ITERS + 1),
        sems=ITERS + 9,
    )
    padded = (groups + 2, rows, nz)
    *strips, dots = call(
        functools.partial(basis_strips, nx),
        [strip] * ITERS + [(devices, WIDE, nz)],
        [index, strip_rhs, strip_inv, *came, sums],
        scratch=[padded] * (6 + 2 * ITERS) + [strip] * 2,
        smem=1,
        far_in=(1, 2),
        far_out=range(ITERS),
        sems=ITERS + 2,
    )
    dots = lax.all_to_all(dots, AXES, 0, 0, tiled=True)

    ranks_y, ranks_z = rank // count_y, rank // count_z
    planes = nz // ranks_y
    table_y, table_x = (planes * ny, count_y * nz), (nx * ranks_y, rank * ranks_y)
    y_high, y_low, x_high, x_low = pl.pallas_call(
        functools.partial(tables, count_x),
        out_shape=[jax.ShapeDtypeStruct(one, BF16) for one in (table_y, table_y, table_x, table_x)],
        in_specs=[VMEM] * 2,
        out_specs=[VMEM] * 4,
        scratch_shapes=[pltpu.VMEM((nx, rank * ranks_y), F32)] * 2,
        compiler_params=pltpu.CompilerParams(vmem_limit_bytes=16 * 2**20),
        cost_estimate=pl.CostEstimate(
            flops=4 * nx * ranks_y * rank * ranks_y, bytes_accessed=6 * 2**20, transcendentals=0
        ),
    )(relative(factor_y, "gy").reshape(ny, rank), relative(factor_x, "gx").reshape(nx, rank))
    columns = relative(factor_z, "gz")
    columns = jnp.transpose(columns.reshape(nz, -1))
    high, low = split_table(columns)
    columns = jnp.concatenate(
        [jnp.concatenate([high, high], axis=1), jnp.concatenate([low, low], axis=1)], axis=0
    )
    piece = (4 * nx // 2, ranks_z, nz)
    far = [*strips, *spans, velocity, inv_density]
    pressure, corrected, keep, keep_more, send = call(
        finish,
        [cells, (3,) + cells, piece, piece, (2,) + piece],
        [dots, columns, *far],
        scratch=[span, (nx + 2, ny, nz), strip, pltpu.VMEM((4, 2 * ny, 2 * nz), BF16), cells, (3,) + cells]
        + [one.shape for one in far],
        limit=32,
        far_in=range(2, 2 + len(far)),
        far_out=(0, 1),
        sems=ITERS + 4 * (ITERS + 5) + 16,
    )

    came = swap(send, "gz", 1)
    table = [y_high, y_low]
    part = (piece[0] // 2, ranks_z, nz)
    half = (2 * nx // planes * ranks_z, nz)
    full = (2 * half[0], nz)
    p_send, p_keep, q_send, q_keep, q_more = call(
        tail_one, [part, part, (2,) + full, full, full], [keep, keep_more, came, *table], limit=16
    )
    p_came, q_came = swap(p_send, "gz", 2), swap(q_send, "gy", 1)
    p_send, p_keep, p_more, q_send, q_keep = call(
        tail_two,
        [(2,) + half, half, half, full, full],
        [p_keep, p_came, q_keep, q_more, q_came, *table],
        limit=16,
    )
    p_came, q_came = swap(p_send, "gy", 1), swap(q_send, "gy", 2)
    p_send, p_keep, q_send, q_keep = call(
        tail_three, [half] * 4, [p_keep, p_more, p_came, q_keep, q_came]
    )
    p_came, q_came = swap(p_send, "gy", 2), swap(q_send, "gz", 2)
    half = (4 * ranks_z, rank * ranks_y // 2)
    keep, send = call(
        functools.partial(rank_x, ranks_z),
        [half] * 2,
        [p_keep, p_came, q_keep, q_came, x_high, x_low],
        limit=16,
    )
    mask = 1
    while True:
        came = swap(send, "gx", mask)
        mask *= 2
        if mask >= count_x:
            break
        total = keep + came
        width = total.shape[1] // 2
        keep, send = total[:, :width], total[:, width:]
    core, = call(last_core, [(4, ranks_y, ranks_z, rank // count_x)], [keep, came], limit=16, pinned=(0,))
    return pressure, corrected, jnp.transpose(core, (3, 0, 1, 2))


def solution(mesh):
    placed = (
        P(None, "gx", "gy", "gz"),
        P("gx", "gy", "gz"),
        P("gx", None),
        P("gy", None),
        P("gz", None),
    )
    return jax.shard_map(
        per_device,
        mesh=mesh,
        in_specs=placed,
        out_specs=(P("gx", "gy", "gz"), P(None, "gx", "gy", "gz"), P("gx", None, "gy", "gz")),
        check_vma=False,
    )
```
